32 devices in a mesh: seq: 4 (over z), row: 8 (over y, x, core).
Axes of the slice: x: 2, y: 2, z: 4, core: 2. Of those that a mesh axis runs over, the one named last changes fastest.
Arguments:
- tokens: bfloat16 [16, 2048, 1024], P('row', 'seq'), may hold values from -6 to 6
- segment_ids: int32 [16, 2048], P('row', 'seq'), may hold values from 0 to 3, as said below
- memory: bfloat16 [16, 512, 1024], P('row', 'seq'), may hold values from -6 to 6
- cotangent: bfloat16 [16, 2048, 1024], P('row', 'seq'), may hold values from -6 to 6
- gain_attend: float32 [1024], replicated, may hold values from 0.1 to 1.9
- gain_cross: float32 [1024], replicated, may hold values from 0.1 to 1.9
- gain_feed: float32 [1024], replicated, may hold values from 0.1 to 1.9
- bias_table: float32 [32, 16], replicated, may hold values from -4 to 4
- self_query: bfloat16 [1024, 1024], replicated, may hold values from -0.1875 to 0.1875
- self_keyvalue: bfloat16 [1024, 1024], replicated, may hold values from -0.1875 to 0.1875
- self_output: bfloat16 [1024, 1024], replicated, may hold values from -2 to 2
- cross_query: bfloat16 [1024, 1024], replicated, may hold values from -0.1875 to 0.1875
- cross_keyvalue: bfloat16 [1024, 1024], replicated, may hold values from -0.1875 to 0.1875
- cross_output: bfloat16 [1024, 1024], replicated, may hold values from -2 to 2
- feed_gate: bfloat16 [1024, 2816], replicated, may hold values from -0.1875 to 0.1875
- feed_up: bfloat16 [1024, 2816], replicated, may hold values from -0.1875 to 0.1875
- feed_down: bfloat16 [2816, 1024], replicated, may hold values from -0.109375 to 0.109375
Outputs:
- layer_output: bfloat16 [16, 2048, 1024], P('row', 'seq')
- tokens_grad: bfloat16 [16, 2048, 1024], P('row', 'seq')
- memory_grad: bfloat16 [16, 512, 1024], P('row', 'seq')
- self_query_grad: float32 [1024, 1024], P(('seq', 'row'))
- self_keyvalue_grad: float32 [1024, 1024], P(('seq', 'row'))
- self_output_grad: float32 [1024, 1024], P(('seq', 'row'))
- cross_query_grad: float32 [1024, 1024], P(('seq', 'row'))
- cross_keyvalue_grad: float32 [1024, 1024], P(('seq', 'row'))
- cross_output_grad: float32 [1024, 1024], P(('seq', 'row'))
- feed_gate_grad: float32 [1024, 2816], P(('seq', 'row'))
- feed_up_grad: float32 [1024, 2816], P(('seq', 'row'))
- feed_down_grad: float32 [2816, 1024], P(('seq', 'row'))
- gain_attend_grad: float32 [1024], replicated
- gain_cross_grad: float32 [1024], replicated
- gain_feed_grad: float32 [1024], replicated
- bias_table_grad: float32 [32, 16], replicated
The draws below stay inside these ranges and needn't reach their ends.
Inputs may be any that keep to these rules, and one draw needn't show every extreme that they name: `segment_ids`: along each row the document numbers start at 0 and never fall; documents never cross rows.
All inputs are finite; a program needn't handle non-finite values.
Results may differ from the reference program's by a relative error of at most 0.03.
Values may be sent and summed in bfloat16 or wider, within the bound.
A program may use at most 576 MiB of HBM per device.

```python
import math
import jax
import jax.numpy as jnp
import numpy as np
from jax import lax

D = 1024
HEADS = 16
KV_HEADS = 8
HEAD = 64
FF = 2816
BUCKETS = 32
MAX_DIST = 128
LENGTH = 2048
MEMORY = 512
ROWS_DEV = 2
SHARD = 512
ROWS = 16


def draw_segment_ids(key, part):
    key = jax.random.fold_in(key, 11)
    cut_key, near_key, row_key = jax.random.split(key, 3)
    cuts = jax.random.randint(cut_key, (ROWS, 3), 1, LENGTH)
    near_cuts = jax.random.randint(near_key, (ROWS, 3), 1, SHARD)
    chosen = jax.random.randint(row_key, (ROWS // ROWS_DEV,), 0, ROWS_DEV)
    row_numbers = jnp.arange(ROWS)
    spanning = row_numbers % ROWS_DEV == jnp.repeat(chosen, ROWS_DEV)
    cuts = jnp.where(spanning[:, None], near_cuts, cuts)
    places = jnp.arange(LENGTH)
    return jnp.sum((places[None, :, None] >= cuts[:, None, :]).astype(jnp.int32), axis=2)


def block_levels(stream_key, extent, cuts, low, largest):
    def one(axis_at, blocks):
        draws = jax.random.uniform(jax.random.fold_in(jax.random.fold_in(stream_key, 6), axis_at), (blocks,), jnp.float32, low / len(cuts), largest / len(cuts))
        return jnp.repeat(jnp.exp(draws), extent[axis_at] // blocks).reshape((-1,) + (1,) * (len(extent) - axis_at - 1))

    level = one(*cuts[0])
    for cut in cuts[1:]:
        level = level * one(*cut)
    return level


def gaussian(key, extent, width, bound, cuts=(), kind=jnp.bfloat16):
    drawn = width * jax.random.normal(key, extent, jnp.float32)
    if cuts:
        drawn = drawn * block_levels(key, extent, cuts, -0.22, 0.18)
    return jnp.clip(drawn, -bound, bound).astype(kind)


def setup_inputs(seed: int = 0) -> dict:
    splits = jax.random.split(jax.random.key(seed), 18)
    return {
        "tokens": gaussian(splits[0], (ROWS, LENGTH, D), 1.0, 6.0, ((0, 8), (1, 4))),
        "segment_ids": draw_segment_ids(jax.random.fold_in(splits[17], 71), 0),
        "memory": gaussian(splits[2], (ROWS, MEMORY, D), 1.0, 6.0, ((0, 8), (1, 4))),
        "cotangent": gaussian(splits[3], (ROWS, LENGTH, D), 1.0, 6.0, ((0, 8), (1, 4))),
        "gain_attend": jnp.clip(1.0 + 0.18 * jax.random.normal(splits[4], (D,), jnp.float32), 0.1, 1.9),
        "gain_cross": jnp.clip(1.0 + 0.18 * jax.random.normal(splits[5], (D,), jnp.float32), 0.1, 1.9),
        "gain_feed": jnp.clip(1.0 + 0.18 * jax.random.normal(splits[6], (D,), jnp.float32), 0.1, 1.9),
        "bias_table": gaussian(splits[7], (BUCKETS, HEADS), 1.0, 4.0, (), jnp.float32),
        "self_query": gaussian(splits[8], (D, HEADS * HEAD), D ** -0.5, 0.1875),
        "self_keyvalue": gaussian(splits[9], (D, 2 * KV_HEADS * HEAD), D ** -0.5, 0.1875),
        "self_output": gaussian(splits[10], (HEADS * HEAD, D), 8 ** -0.5, 2.0),
        "cross_query": gaussian(splits[11], (D, HEADS * HEAD), D ** -0.5, 0.1875),
        "cross_keyvalue": gaussian(splits[12], (D, 2 * KV_HEADS * HEAD), D ** -0.5, 0.1875),
        "cross_output": gaussian(splits[13], (HEADS * HEAD, D), 8 ** -0.5, 2.0),
        "feed_gate": gaussian(splits[14], (D, FF), D ** -0.5, 0.1875),
        "feed_up": gaussian(splits[15], (D, FF), D ** -0.5, 0.1875),
        "feed_down": gaussian(splits[16], (FF, D), FF ** -0.5, 0.109375),
    }


@jax.custom_vjp
def low(v):
    return lax.optimization_barrier(v.astype(jnp.bfloat16)).astype(jnp.float32)

@jax.custom_vjp
def low_back(v):
    return v

def low_keep(v):
    return (low(v), None)

def low_pass(kept, grad):
    return (grad,)

def back_keep(v):
    return (v, None)

def back_low(kept, grad):
    return (low(grad),)
low.defvjp(low_keep, low_pass)
low_back.defvjp(back_keep, back_low)

def both_round(value):
    return low_back(low(value))

def matmul(left, right):
    return jnp.dot(left, right, precision=lax.Precision.HIGHEST)

def norm_rows(values, gain):
    return values * lax.rsqrt(lax.optimization_barrier(jnp.mean(values * values, axis=-1, keepdims=True)) + 1e-06) * gain

def gated_mix(gate_pre, up_pre):
    return jax.nn.gelu(gate_pre, approximate=True) * up_pre

def bucket_level(distance):
    exact_part = BUCKETS // 2
    if distance < exact_part:
        return distance
    which_bucket = exact_part + math.floor(math.log(distance / exact_part) / math.log(MAX_DIST / exact_part) * (BUCKETS - exact_part))
    return min(BUCKETS - 1, which_bucket)

def bucket_limits():
    bounds = []
    distance = 0
    for which_bucket in range(1, BUCKETS):
        while bucket_level(distance) < which_bucket:
            distance = distance + 1
        bounds.append(distance)
    return np.array(bounds, dtype=np.int32)

def attend_self(queries, key_heads, value_heads, segments, bias_table):
    length = queries.shape[0]
    block_len = min(512, length)
    places = jnp.arange(length).astype(jnp.int32)
    limits = jnp.asarray(bucket_limits()).astype(jnp.int32)

    def block(offset):
        q_part = lax.dynamic_slice_in_dim(queries, offset, block_len, 0)
        seg_part = lax.dynamic_slice_in_dim(segments, offset, block_len, 0)
        place_part = offset + jnp.arange(block_len).astype(jnp.int32)
        raw_scores = jnp.einsum('qkgd,tkd->kgqt', q_part, key_heads, precision=lax.Precision.HIGHEST) * 0.125
        distance = place_part[:, None] - places[None, :]
        levels = lax.optimization_barrier(jnp.sum((jnp.maximum(distance, 0)[None] >= limits[:, None, None]).astype(jnp.int32), axis=0))
        bias_rows = jnp.transpose(bias_table[levels], (2, 0, 1)).reshape(KV_HEADS, HEADS // KV_HEADS, block_len, length)
        scores = low_back(raw_scores + bias_rows)
        allowed = (seg_part[:, None] == segments[None, :]) & (distance >= 0)
        scores = jnp.where(allowed[None, None], scores, -1e+30)
        weights = low(jax.nn.softmax(scores, axis=-1))
        return jnp.einsum('kgqt,tkd->qkgd', weights, value_heads, precision=lax.Precision.HIGHEST)
    offsets = jnp.arange(0, length, block_len).astype(jnp.int32)
    pieces = lax.map(jax.checkpoint(block), offsets)
    return pieces.reshape(queries.shape)

def attend_cross(queries, key_heads, value_heads):
    length = queries.shape[0]
    block_len = min(512, length)

    def block(offset):
        q_part = lax.dynamic_slice_in_dim(queries, offset, block_len, 0)
        scores = low_back(jnp.einsum('qkgd,tkd->kgqt', q_part, key_heads, precision=lax.Precision.HIGHEST) * 0.125)
        weights = low(jax.nn.softmax(scores, axis=-1))
        return jnp.einsum('kgqt,tkd->qkgd', weights, value_heads, precision=lax.Precision.HIGHEST)
    offsets = jnp.arange(0, length, block_len).astype(jnp.int32)
    pieces = lax.map(jax.checkpoint(block), offsets)
    return pieces.reshape(queries.shape)

def layer_row(inputs, segments, memory_row, params):
    gain_attend, gain_cross, gain_feed, bias_table, self_query, self_keyvalue, self_output, cross_query, cross_keyvalue, cross_output, feed_gate, feed_up, feed_down = params
    length = inputs.shape[0]
    mem_length = memory_row.shape[0]
    kv_width = KV_HEADS * HEAD
    group_size = HEADS // KV_HEADS
    normed_one = low(norm_rows(inputs, gain_attend))
    queries = both_round(matmul(normed_one, self_query)).reshape(length, KV_HEADS, group_size, HEAD)
    self_pairs = both_round(matmul(normed_one, self_keyvalue))
    key_heads = self_pairs[:, :kv_width].reshape(length, KV_HEADS, HEAD)
    value_heads = self_pairs[:, kv_width:].reshape(length, KV_HEADS, HEAD)
    attended = both_round(attend_self(queries, key_heads, value_heads, segments, bias_table))
    after_self = inputs + low_back(matmul(attended.reshape(length, HEADS * HEAD), self_output))
    normed_two = low(norm_rows(after_self, gain_cross))
    cross_heads = both_round(matmul(normed_two, cross_query)).reshape(length, KV_HEADS, group_size, HEAD)
    memory_pairs = both_round(matmul(memory_row, cross_keyvalue))
    memory_keys = memory_pairs[:, :kv_width].reshape(mem_length, KV_HEADS, HEAD)
    memory_values = memory_pairs[:, kv_width:].reshape(mem_length, KV_HEADS, HEAD)
    crossed = both_round(attend_cross(cross_heads, memory_keys, memory_values))
    after_cross = after_self + low_back(matmul(crossed.reshape(length, HEADS * HEAD), cross_output))
    normed_three = low(norm_rows(after_cross, gain_feed))
    gate_pre = low_back(matmul(normed_three, feed_gate))
    up_pre = low_back(matmul(normed_three, feed_up))
    hidden = low(gated_mix(gate_pre, up_pre))
    return after_cross + low_back(matmul(hidden, feed_down))

def reference(tokens, segment_ids, memory, cotangent, gain_attend, gain_cross, gain_feed, bias_table, self_query, self_keyvalue, self_output, cross_query, cross_keyvalue, cross_output, feed_gate, feed_up, feed_down):

    def forward(tokens_wide, memory_wide, gain_one, gain_two, gain_three, table_wide, query_one, pairs_one, output_one, query_two, pairs_two, output_two, gate_wide, up_wide, down_wide):
        params = (gain_one, gain_two, gain_three, table_wide, query_one, pairs_one, output_one, query_two, pairs_two, output_two, gate_wide, up_wide, down_wide)

        def one_row(packed):
            row_tokens, row_segments, row_memory = packed
            return layer_row(row_tokens, row_segments, row_memory, params)
        return lax.map(jax.checkpoint(one_row), (tokens_wide, segment_ids, memory_wide))
    layer_output, pullback = jax.vjp(forward, tokens.astype(jnp.float32), memory.astype(jnp.float32), gain_attend.astype(jnp.float32), gain_cross.astype(jnp.float32), gain_feed.astype(jnp.float32), bias_table.astype(jnp.float32), self_query.astype(jnp.float32), self_keyvalue.astype(jnp.float32), self_output.astype(jnp.float32), cross_query.astype(jnp.float32), cross_keyvalue.astype(jnp.float32), cross_output.astype(jnp.float32), feed_gate.astype(jnp.float32), feed_up.astype(jnp.float32), feed_down.astype(jnp.float32))
    grads = pullback(cotangent.astype(jnp.float32))
    return (layer_output.astype(jnp.bfloat16), grads[0].astype(jnp.bfloat16), grads[1].astype(jnp.bfloat16), grads[6], grads[7], grads[8], grads[9], grads[10], grads[11], grads[12], grads[13], grads[14], grads[2], grads[3], grads[4], grads[5])
```

```python
import functools
import math

import jax
import jax.numpy as jnp
import numpy as np
from jax import lax
from jax.experimental import pallas as pl
from jax.experimental.pallas import tpu as pltpu
from jax.sharding import PartitionSpec as P

HEADS = 16
BUCKETS = 32
MAX_DIST = 128
HIGHEST = lax.Precision.HIGHEST
F32, BF16 = jnp.float32, jnp.bfloat16
MASK = -float(2.0**100)
NEAR = 128
VMEM = 56 * 1024 * 1024
GELU_A = math.sqrt(2.0 / math.pi)
GELU_B = GELU_A * 0.044715


def bucket_level(distance):
    exact_part = BUCKETS // 2
    if distance < exact_part:
        return distance
    which_bucket = exact_part + math.floor(
        math.log(distance / exact_part) / math.log(MAX_DIST / exact_part) * (BUCKETS - exact_part)
    )
    return min(BUCKETS - 1, which_bucket)


def call(kernel, inputs, in_specs, out_shape, out_specs, name, flops, grid=(), scratch=(), prefetch=0,
         hold=(), after=(), alias=None):
    hold, after = list(hold), list(after)
    count_in, count_out = len(inputs), len(out_shape)
    anywhere = pl.BlockSpec(memory_space=pl.ANY)

    def body(*refs):
        kept = count_in + len(hold) + len(after)
        kernel(*refs[:count_in], *refs[kept:kept + count_out], *refs[kept + count_out + len(hold):])

    aliases = {count_in + i: count_out + i for i in range(len(hold))}
    aliases.update(alias or {})
    outs = pl.pallas_call(
        body,
        grid_spec=pltpu.PrefetchScalarGridSpec(
            num_scalar_prefetch=prefetch,
            grid=grid,
            in_specs=list(in_specs) + [anywhere] * (len(hold) + len(after)),
            out_specs=list(out_specs) + [anywhere] * len(hold),
            scratch_shapes=list(scratch),
        ),
        out_shape=list(out_shape) + [jax.ShapeDtypeStruct(x.shape, x.dtype) for x in hold],
        input_output_aliases=aliases,
        compiler_params=pltpu.CompilerParams(vmem_limit_bytes=VMEM),
        cost_estimate=pl.CostEstimate(flops=int(flops), bytes_accessed=10**7, transcendentals=0),
        name=name,
    )(*inputs, *hold, *after)
    return list(outs[:count_out]), list(outs[count_out:])


def nt(a, b):
    return lax.dot_general(a, b, (((1,), (1,)), ((), ())), preferred_element_type=F32)


def nn(a, b):
    return jnp.dot(a, b, preferred_element_type=F32)


def tn(a, b):
    return lax.dot_general(a, b, (((0,), (0,)), ((), ())), preferred_element_type=F32)


def halves(block):
    low = lax.broadcasted_iota(jnp.int32, block.shape, 1) < 64
    zero = jnp.zeros_like(block)
    return jnp.where(low, block, zero), jnp.where(low, zero, block)


def lanes(a, b):
    return jnp.concatenate([a, b], axis=1)


def rows(a, b):
    return jnp.concatenate([a, b], axis=0)


def chunk_of(member, part, chunks):
    return jnp.where(part == 0, member, chunks - 1 - member)


def slot_of(member, chunk, chunks):
    high = (chunk >= chunks // 2).astype(jnp.int32)
    other = jnp.where(chunk >= chunks // 2, chunks - 1 - chunk, chunk)
    return 2 * jnp.bitwise_xor(other, member) + high


def first_block(meta, member, chunk, chunks):
    mine = meta[1 + slot_of(member, chunk, chunks)]

    def skip(block, start):
        last = meta[1 + chunks + slot_of(member, block, chunks)]
        return start + jnp.where((block < chunk) & (last < mine), 1, 0)

    return lax.fori_loop(0, chunks, skip, jnp.int32(0))


def self_forward_kernel(chunks, sub, meta, q_ref, k_ref, v_ref, qf_ref, kf_ref, near_ref, corner_ref,
                        o_ref, lse_ref, acc_ref, m_ref):
    size = q_ref.shape[0]
    member = meta[0]
    chunk = chunk_of(member, pl.program_id(1), chunks)
    q_both = [lanes(part, qf_ref[...]) for part in halves(q_ref[...])]

    def values(at, length):
        low, high = halves(v_ref[pl.ds(at, length), :])
        one_low, one_high = halves(jnp.ones((length, 128), BF16))
        return rows(lanes(low, one_low), lanes(high, one_high))

    own = pl.multiple_of(slot_of(member, chunk, chunks) * size, size)
    for strip in range(size // sub):
        span = (strip + 1) * sub
        here = slice(strip * sub, span)
        keys = lanes(k_ref[pl.ds(own, span), :], kf_ref[pl.ds(own, span), :])
        weights = []
        for head in range(2):
            s = nt(q_both[head][here], keys)
            last = s[:, span - sub:] + near_ref[head]
            if strip:
                edge = s[:, span - sub - NEAR:span - sub]
                edge = rows(edge[:NEAR] + corner_ref[head], edge[NEAR:])
                s = jnp.concatenate([s[:, :span - sub - NEAR], edge, last], axis=1)
            else:
                s = last
            top = jnp.max(s, axis=1, keepdims=True)
            m_ref[head, here, :] = jnp.broadcast_to(top, (sub, 128))
            weights.append(jnp.exp(s - top).astype(BF16))
        acc_ref[here, :] = nn(lanes(*weights), values(own, span))

    def far(block, carry):
        at = pl.multiple_of(slot_of(member, block, chunks) * size, size)
        keys = lanes(k_ref[pl.ds(at, size), :], kf_ref[pl.ds(at, size), :])
        flag = jnp.where(block == chunk - 1, 1.0, 0.0).astype(F32)
        weights, scales = [], []
        for head in range(2):
            s = nt(q_both[head], keys)
            edge = s[:NEAR, size - NEAR:] + corner_ref[head] * flag
            s = rows(lanes(s[:NEAR, :size - NEAR], edge), s[NEAR:])
            old = m_ref[head]
            top = jnp.maximum(old, jnp.max(s, axis=1, keepdims=True))
            scales.append(jnp.exp(old - top))
            m_ref[head] = top
            weights.append(jnp.exp(s - top[:, :1]).astype(BF16))
        low = lax.broadcasted_iota(jnp.int32, (size, 128), 1) < 64
        scale = jnp.where(low, scales[0], scales[1])
        acc_ref[...] = acc_ref[...] * lanes(scale, scale) + nn(lanes(*weights), values(at, size))
        return carry

    lax.fori_loop(first_block(meta, member, chunk, chunks), chunk, far, 0)
    low = lax.broadcasted_iota(jnp.int32, (size, 128), 1) < 64
    total = acc_ref[:, 128:]
    o_ref[...] = (acc_ref[:, :128] / total).astype(BF16)
    lse_ref[...] = jnp.where(low, m_ref[0], m_ref[1]) + jnp.log(total)


def pieces(column, shape):
    lane = lax.broadcasted_iota(jnp.int32, shape, 1)
    high = column.astype(BF16).astype(F32)
    rest = column - high
    middle = rest.astype(BF16).astype(F32)
    low = rest - middle
    full = jnp.where(lane == 4, high, jnp.where(lane == 5, middle, jnp.where(lane == 6, low, 0.0)))
    return full.astype(BF16)


def back_operands(q_ref, do_ref, o_ref, lse_ref, qf):
    shape = q_ref.shape
    q_both = halves(q_ref[...])
    do_both = halves(do_ref[...])
    product = do_ref[...].astype(F32) * o_ref[...].astype(F32)
    low = lax.broadcasted_iota(jnp.int32, shape, 1) < 64
    deltas = [jnp.sum(jnp.where(low, product, 0.0), axis=1, keepdims=True),
              jnp.sum(jnp.where(low, 0.0, product), axis=1, keepdims=True)]
    logs = [lse_ref[:, 0:1], lse_ref[:, 64:65]]
    extra = [pieces(log, shape) for log in logs]
    if qf is not None:
        extra = [part + qf for part in extra]
    q_wide = [lanes(part, more) for part, more in zip(q_both, extra)]
    do_wide = [lanes(part, pieces(delta, shape)) for part, delta in zip(do_both, deltas)]
    return q_both, do_both, q_wide, do_wide


def diagonal_sums(block):
    count, wide = block.shape[0], 2 * block.shape[1]
    block = lanes(block, jnp.zeros_like(block))
    while count > 8:
        count = count // 2
        block = block[:count] + pltpu.roll(block[count:], wide - count, 1)
    return block


def self_backward_kernel(chunks, sub, meta, q_ref, do_ref, o_ref, lse_ref, k_ref, v_ref, qf_ref, kf_ref,
                         near_ref, corner_ref, dq_ref, dkv_ref, near_out, corner_out,
                         dq_acc, dk_acc, dv_acc, near_acc, corner_acc):
    size = q_ref.shape[0]
    member = meta[0]
    chunk = chunk_of(member, pl.program_id(2), chunks)
    first = (pl.program_id(1) == 0) & (pl.program_id(2) == 0)
    last = (pl.program_id(1) == 1) & (pl.program_id(2) == 1)

    @pl.when(first)
    def _():
        dk_acc[...] = jnp.zeros_like(dk_acc)
        dv_acc[...] = jnp.zeros_like(dv_acc)

    @pl.when(pl.program_id(2) == 0)
    def _():
        near_acc[...] = jnp.zeros_like(near_acc)
        corner_acc[...] = jnp.zeros_like(corner_acc)

    q_both, do_both, q_wide, do_wide = back_operands(q_ref, do_ref, o_ref, lse_ref, qf_ref[...])
    own = pl.multiple_of(slot_of(member, chunk, chunks) * size, size)
    dq_acc[...] = jnp.zeros_like(dq_acc)

    def add(at, length, here, weights, grads, keys):
        dv_acc[pl.ds(at, length), :] += nn(lanes(*weights), rows(do_both[0][here], do_both[1][here]))
        dk_acc[pl.ds(at, length), :] += nn(lanes(*grads), rows(q_both[0][here], q_both[1][here]))
        dq_acc[here, :] += tn(rows(*grads), rows(*halves(keys)))

    for strip in range(size // sub):
        at = pl.multiple_of(own + strip * sub, sub)
        here = slice(strip * sub, size)
        k, v, kf = (ref[pl.ds(at, sub), :] for ref in (k_ref, v_ref, kf_ref))
        keys, vals = lanes(k, kf), lanes(v, kf)
        weights, grads = [], []
        for head in range(2):
            s = nt(keys, q_wide[head][here])
            dp = nt(vals, do_wide[head][here])
            block = s[:, :sub] + near_ref[head]
            more = (strip + 1) * sub < size
            if more:
                edge = s[sub - NEAR:, sub:sub + NEAR] + corner_ref[head]
                rest = s[:, sub:]
                rest = rows(rest[:sub - NEAR], lanes(edge, rest[sub - NEAR:, NEAR:]))
                s = lanes(block, rest)
            else:
                s = block
            p = jnp.exp(s)
            ds = p * dp
            near_acc[head] += ds[:, :sub]
            if more:
                corner_acc[head] += ds[sub - NEAR:, sub:sub + NEAR]
            weights.append(p.astype(BF16))
            grads.append(ds.astype(BF16))
        add(at, sub, here, weights, grads, k)

    def far(block, carry):
        at = pl.multiple_of(slot_of(member, block, chunks) * size, size)
        k, v, kf = (ref[pl.ds(at, size), :] for ref in (k_ref, v_ref, kf_ref))
        keys, vals = lanes(k, kf), lanes(v, kf)
        flag = jnp.where(block == chunk - 1, 1.0, 0.0).astype(F32)
        weights, grads = [], []
        for head in range(2):
            s = nt(keys, q_wide[head])
            dp = nt(vals, do_wide[head])
            edge = s[size - NEAR:, :NEAR] + corner_ref[head] * flag
            s = rows(s[:size - NEAR], lanes(edge, s[size - NEAR:, NEAR:]))
            p = jnp.exp(s)
            ds = p * dp
            corner_acc[head] += ds[size - NEAR:, :NEAR] * flag
            weights.append(p.astype(BF16))
            grads.append(ds.astype(BF16))
        add(at, size, slice(None), weights, grads, k)
        return carry

    lax.fori_loop(first_block(meta, member, chunk, chunks), chunk, far, 0)
    dq_ref[...] = (dq_acc[...] * 0.125).astype(BF16)

    @pl.when(last)
    def _():
        dkv_ref[0] = dk_acc[...].astype(BF16)
        dkv_ref[1] = dv_acc[...].astype(BF16)

    @pl.when(pl.program_id(2) == 1)
    def _():
        for head in range(2):
            near_out[head] = diagonal_sums(near_acc[head])
            corner_out[head] = diagonal_sums(corner_acc[head])


def self_forward(meta, q, kv, qf, kf, near, corner, chunks, hold=(), after=()):
    size = q.shape[0] // 2
    sub = min(256, size)
    length = kv.shape[0]
    own = pl.BlockSpec((size, 128), lambda b, c, m: (c, b))
    return call(
        functools.partial(self_forward_kernel, chunks, sub),
        (meta, q, kv, kv, qf, kf, near, corner),
        [
            own,
            pl.BlockSpec((length, 128), lambda b, c, m: (0, b // 2)),
            pl.BlockSpec((length, 128), lambda b, c, m: (0, 4 + b // 2)),
            pl.BlockSpec((size, 128), lambda b, c, m: (c, 0)),
            pl.BlockSpec((length, 128), lambda b, c, m: (0, 0)),
            pl.BlockSpec((2, sub, sub), lambda b, c, m: (b, 0, 0)),
            pl.BlockSpec((2, NEAR, NEAR), lambda b, c, m: (b, 0, 0)),
        ],
        [jax.ShapeDtypeStruct(q.shape, BF16), jax.ShapeDtypeStruct(q.shape, F32)],
        [own, own],
        "self_forward", 4e10, grid=(8, 2), prefetch=1, hold=hold, after=after,
        scratch=[pltpu.VMEM((size, 256), F32), pltpu.VMEM((2, size, 128), F32)],
    )


def self_backward(meta, q, do, o, lse, kv, qf, kf, near, corner, chunks, part, parts, before, hold=(), after=()):
    pairs = 4 // parts
    shift = pairs * part
    size = q.shape[0] // 2
    sub = min(256, size)
    length = kv.shape[0]
    own = pl.BlockSpec((size, 128), lambda g, b, c, m: (c, 2 * (g + shift) + b))
    inputs = [meta, q, do, o, lse, kv, kv, qf, kf, near, corner]
    in_specs = [
        own, own, own, own,
        pl.BlockSpec((length, 128), lambda g, b, c, m: (0, g + shift)),
        pl.BlockSpec((length, 128), lambda g, b, c, m: (0, 4 + g + shift)),
        pl.BlockSpec((size, 128), lambda g, b, c, m: (c, 0)),
        pl.BlockSpec((length, 128), lambda g, b, c, m: (0, 0)),
        pl.BlockSpec((2, sub, sub), lambda g, b, c, m: (2 * (g + shift) + b, 0, 0)),
        pl.BlockSpec((2, NEAR, NEAR), lambda g, b, c, m: (2 * (g + shift) + b, 0, 0)),
    ]
    kernel = functools.partial(self_backward_kernel, chunks, sub)
    alias = None
    if before is not None:
        count = len(inputs)
        alias = {count + i: i for i in range(len(before))}
        inputs += before
        in_specs += [pl.BlockSpec(memory_space=pl.ANY)] * len(before)
        inner = kernel

        def kernel(*refs):
            inner(*refs[:count], *refs[count + len(before):])

    return call(
        kernel, tuple(inputs), in_specs,
        [
            jax.ShapeDtypeStruct(q.shape, BF16),
            jax.ShapeDtypeStruct((2, length, 512), BF16),
            jax.ShapeDtypeStruct((16, 8, 2 * sub), F32),
            jax.ShapeDtypeStruct((16, 8, 2 * NEAR), F32),
        ],
        [
            own,
            pl.BlockSpec((2, length, 128), lambda g, b, c, m: (0, 0, g + shift)),
            pl.BlockSpec((2, 8, 2 * sub), lambda g, b, c, m: (2 * (g + shift) + b, 0, 0)),
            pl.BlockSpec((2, 8, 2 * NEAR), lambda g, b, c, m: (2 * (g + shift) + b, 0, 0)),
        ],
        "self_backward", 6e10 / parts, grid=(pairs, 2, 2), prefetch=1, hold=hold, after=after, alias=alias,
        scratch=[
            pltpu.VMEM((size, 128), F32),
            pltpu.VMEM((length, 128), F32),
            pltpu.VMEM((length, 128), F32),
            pltpu.VMEM((2, sub, sub), F32),
            pltpu.VMEM((2, NEAR, NEAR), F32),
        ],
    )


def cross_forward_kernel(q_ref, k_ref, v_ref, o_ref, lse_ref):
    length = k_ref.shape[0]
    keys = k_ref[...]
    low, high = halves(v_ref[...])
    one_low, one_high = halves(jnp.ones((length, 128), BF16))
    values = rows(lanes(low, one_low), lanes(high, one_high))
    weights, tops = [], []
    for part in halves(q_ref[...]):
        s = nt(part, keys)
        top = jnp.max(s, axis=1, keepdims=True)
        tops.append(top)
        weights.append(jnp.exp(s - top).astype(BF16))
    acc = nn(lanes(*weights), values)
    is_low = lax.broadcasted_iota(jnp.int32, q_ref.shape, 1) < 64
    total = acc[:, 128:]
    o_ref[...] = (acc[:, :128] / total).astype(BF16)
    lse_ref[...] = jnp.where(is_low, tops[0], tops[1]) + jnp.log(total)


def cross_backward_kernel(q_ref, do_ref, o_ref, lse_ref, k_ref, v_ref, dq_ref, dkv_ref, dk_acc, dv_acc):
    first = (pl.program_id(1) == 0) & (pl.program_id(2) == 0)
    last = (pl.program_id(1) == 1) & (pl.program_id(2) == 1)

    @pl.when(first)
    def _():
        dk_acc[...] = jnp.zeros_like(dk_acc)
        dv_acc[...] = jnp.zeros_like(dv_acc)

    q_both, do_both, q_wide, do_wide = back_operands(q_ref, do_ref, o_ref, lse_ref, None)
    k = k_ref[...]
    lane = lax.broadcasted_iota(jnp.int32, k.shape, 1)
    minus = jnp.where((lane >= 4) & (lane < 7), -1.0, 0.0).astype(BF16)
    keys, vals = lanes(k, minus), lanes(v_ref[...], minus)
    weights, grads = [], []
    for head in range(2):
        p = jnp.exp(nt(keys, q_wide[head]))
        ds = p * nt(vals, do_wide[head])
        weights.append(p.astype(BF16))
        grads.append(ds.astype(BF16))
    dv_acc[...] += nn(lanes(*weights), rows(*do_both))
    dk_acc[...] += nn(lanes(*grads), rows(*q_both))
    dq_ref[...] = (tn(rows(*grads), rows(*halves(k))) * 0.125).astype(BF16)

    @pl.when(last)
    def _():
        dkv_ref[0] = dk_acc[...].astype(BF16)
        dkv_ref[1] = dv_acc[...].astype(BF16)


def cross_forward(q, kv, hold=(), after=()):
    size, length = q.shape[0] // 2, kv.shape[0]
    own = pl.BlockSpec((size, 128), lambda b, c: (c, b))
    return call(
        cross_forward_kernel, (q, kv, kv),
        [
            own,
            pl.BlockSpec((length, 128), lambda b, c: (0, b // 2)),
            pl.BlockSpec((length, 128), lambda b, c: (0, 4 + b // 2)),
        ],
        [jax.ShapeDtypeStruct(q.shape, BF16), jax.ShapeDtypeStruct(q.shape, F32)],
        [own, own],
        "cross_forward", 15e9, grid=(8, 2), hold=hold, after=after,
    )


def cross_backward(q, do, o, lse, kv, hold=(), after=()):
    size, length = q.shape[0] // 2, kv.shape[0]
    own = pl.BlockSpec((size, 128), lambda g, b, c: (c, 2 * g + b))
    return call(
        cross_backward_kernel, (q, do, o, lse, kv, kv),
        [
            own, own, own, own,
            pl.BlockSpec((length, 128), lambda g, b, c: (0, g)),
            pl.BlockSpec((length, 128), lambda g, b, c: (0, 4 + g)),
        ],
        [jax.ShapeDtypeStruct(q.shape, BF16), jax.ShapeDtypeStruct((2, length, 512), BF16)],
        [own, pl.BlockSpec((2, length, 128), lambda g, b, c: (0, 0, g))],
        "cross_backward", 30e9, grid=(4, 2, 2), hold=hold, after=after,
        scratch=[pltpu.VMEM((length, 128), F32), pltpu.VMEM((length, 128), F32)],
    )


def bias_kernel(sub, near_ref, corner_ref, near_out, back_out, corner_out, corner_back):
    for head in range(2):
        wide = jnp.broadcast_to(near_ref[head, :1], (sub, 2 * sub))
        block = pltpu.roll(wide, 0, 1, stride=1, stride_axis=0)[:, :sub]
        back_out[head] = block
        near_out[head] = block.T
        wide = jnp.broadcast_to(corner_ref[head, :1], (NEAR, 2 * NEAR))
        block = pltpu.roll(wide, 0, 1, stride=1, stride_axis=0)[:, :NEAR]
        corner_back[head] = block
        corner_out[head] = block.T


def bias_tiles(near, corner, sub):
    def spec(a, b):
        return pl.BlockSpec((2, a, b), lambda h: (h, 0, 0))

    def shape(a):
        return jax.ShapeDtypeStruct((16, a, a), F32)

    return pl.pallas_call(
        functools.partial(bias_kernel, sub),
        grid=(8,),
        in_specs=[spec(8, 2 * sub), spec(8, 2 * NEAR)],
        out_specs=[spec(sub, sub), spec(sub, sub), spec(NEAR, NEAR), spec(NEAR, NEAR)],
        out_shape=[shape(sub), shape(sub), shape(NEAR), shape(NEAR)],
        compiler_params=pltpu.CompilerParams(vmem_limit_bytes=VMEM),
        name="bias_tiles",
    )(near, corner)


def inverse_rms(h):
    return lax.rsqrt(jnp.mean(h * h, axis=1, keepdims=True) + 1e-06)


def norm(values, gain):
    return (values * inverse_rms(values) * gain).astype(BF16)


def norm_back(h, dn, gain):
    scale = inverse_rms(h)
    unit = h * scale
    spread = dn * unit
    share = jnp.mean(spread * gain, axis=1, keepdims=True)
    gain_part = jnp.sum(spread.reshape(-1, 8, spread.shape[1]), axis=0)
    return scale * (dn * gain - unit * share), gain_part


def entry_kernel(x_ref, gain_ref, weight_ref, n_ref, kv_ref):
    n_ref[...] = norm(x_ref[...].astype(F32), gain_ref[...])
    kv_ref[...] = nn(n_ref[...], weight_ref[...]).astype(BF16)


def middle_kernel(x_ref, o_ref, out_ref, gain_ref, query_ref, h_ref, n_ref, c_ref):
    h = x_ref[...].astype(F32) + nn(o_ref[...], out_ref[...])
    h_ref[...] = h
    n_ref[...] = norm(h, gain_ref[...])
    c_ref[...] = nn(n_ref[...], query_ref[...]).astype(BF16) * BF16(0.125)


def back_middle_kernel(dc_ref, query_ref, h_ref, gain_ref, dh_ref, out_ref, dh1_ref, r_ref, do_ref, dgain_ref):
    @pl.when(pl.program_id(0) == 0)
    def _():
        dgain_ref[...] = jnp.zeros_like(dgain_ref)

    back, part = norm_back(h_ref[...], nt(dc_ref[...], query_ref[...]), gain_ref[...])
    dgain_ref[...] += part
    dh1 = dh_ref[...] + back
    dh1_ref[...] = dh1
    r_ref[...] = dh1.astype(BF16)
    do_ref[...] = nt(r_ref[...], out_ref[...]).astype(BF16)


def exit_kernel(dq_ref, query_ref, dkv_ref, keyvalue_ref, x_ref, gain_ref, dh_ref, dx_ref, dgain_ref):
    @pl.when(pl.program_id(0) == 0)
    def _():
        dgain_ref[...] = jnp.zeros_like(dgain_ref)

    dn = nt(dq_ref[...], query_ref[...]) + nt(dkv_ref[...], keyvalue_ref[...])
    back, part = norm_back(x_ref[...].astype(F32), dn, gain_ref[...])
    dgain_ref[...] += part
    dx_ref[...] = (dh_ref[...] + back).astype(BF16)


def by_rows(kernel, name, flops, arrays, outs, width, dgain=False, hold=(), after=()):
    tokens = next(x.shape[0] for x, cut in arrays if cut)
    tile = min(256, tokens)
    blocks = pl.BlockSpec((tile, width), lambda i: (i, 0))
    in_specs = [blocks if cut else pl.BlockSpec(x.shape, lambda i: (0, 0)) for x, cut in arrays]
    shapes = [jax.ShapeDtypeStruct((tokens, width), kind) for kind in outs]
    specs = [blocks] * len(outs)
    if dgain:
        shapes.append(jax.ShapeDtypeStruct((8, width), F32))
        specs.append(pl.BlockSpec((8, width), lambda i: (0, 0)))
    return call(kernel, tuple(x for x, _ in arrays), in_specs, shapes, specs, name, flops,
                grid=(tokens // tile,), hold=hold, after=after)


def feed_kernel(tile_rows, h1_ref, co_ref, cross_ref, g_ref, gain_ref, gate_ref, up_ref, down_ref,
                out_ref, n_ref, hidden_ref, dgu_ref, dh_ref, low_ref, dco_ref, dgain_ref,
                out_acc, dn_acc, h_acc):
    tokens, width = h1_ref.shape
    count = tokens // tile_rows
    tile = gate_ref.shape[1]
    step = pl.program_id(0)

    def each(body):
        def one(i, carry):
            body(pl.ds(pl.multiple_of(i * tile_rows, tile_rows), tile_rows))
            return carry

        lax.fori_loop(0, count, one, 0)

    @pl.when(step == 0)
    def _():
        def start(at):
            h = h1_ref[at, :] + nn(co_ref[at, :], cross_ref[...])
            h_acc[at, :] = h
            n_ref[at, :] = norm(h, gain_ref[...])
            out_acc[at, :] = jnp.zeros((tile_rows, width), F32)
            dn_acc[at, :] = jnp.zeros((tile_rows, width), F32)

        each(start)
        dgain_ref[...] = jnp.zeros_like(dgain_ref)

    def main(at):
        n = n_ref[at, :]
        gate = nn(n, gate_ref[...])
        up = nn(n, up_ref[...])
        dhidden = nt(g_ref[at, :], down_ref[...])
        square = gate * gate
        bend = jnp.tanh(gate * (GELU_A + GELU_B * square))
        half = 0.5 + 0.5 * bend
        gelu = gate * half
        slope = half + gate * (0.5 - 0.5 * bend * bend) * (GELU_A + 3.0 * GELU_B * square)
        hidden = (gelu * up).astype(BF16)
        dgate = (dhidden * up * slope).astype(BF16)
        dup = (dhidden * gelu).astype(BF16)
        hidden_ref[at, :] = hidden
        dgu_ref[at, :tile] = dgate
        dgu_ref[at, tile:] = dup
        out_acc[at, :] += nn(hidden, down_ref[...])
        dn_acc[at, :] += nt(dgate, gate_ref[...]) + nt(dup, up_ref[...])

    each(main)

    @pl.when(step == pl.num_programs(0) - 1)
    def _():
        def finish(at):
            h = h_acc[at, :]
            out_ref[at, :] = (h + out_acc[at, :]).astype(BF16)
            back, gain_part = norm_back(h, dn_acc[at, :], gain_ref[...])
            dh = g_ref[at, :].astype(F32) + back
            dh_ref[at, :] = dh
            low_ref[at, :] = dh.astype(BF16)
            dco_ref[at, :] = nt(low_ref[at, :], cross_ref[...]).astype(BF16)
            dgain_ref[...] += gain_part

        each(finish)


def feed_forward(h, co, cross_output, g, gain, feed_gate, feed_up, feed_down, hold=(), after=()):
    tokens, width = h.shape
    hidden = feed_gate.shape[1]
    tile = 256
    whole = pl.BlockSpec((tokens, width), lambda i: (0, 0), pipeline_mode=pl.Buffered(1))
    square = pl.BlockSpec((width, width), lambda i: (0, 0), pipeline_mode=pl.Buffered(1))
    row = pl.BlockSpec((1, width), lambda i: (0, 0))
    low, wide = jax.ShapeDtypeStruct(h.shape, BF16), jax.ShapeDtypeStruct(h.shape, F32)
    return call(
        functools.partial(feed_kernel, 256),
        (h, co, cross_output, g, gain, feed_gate, feed_up, feed_down),
        [
            whole, whole, square, whole, row,
            pl.BlockSpec((width, tile), lambda i: (0, i)),
            pl.BlockSpec((width, tile), lambda i: (0, i)),
            pl.BlockSpec((tile, width), lambda i: (i, 0)),
        ],
        [low, low, jax.ShapeDtypeStruct((tokens, hidden), BF16), jax.ShapeDtypeStruct((tokens, 2 * hidden), BF16),
         wide, low, low, jax.ShapeDtypeStruct((8, width), F32)],
        [whole, whole, pl.BlockSpec((tokens, tile), lambda i: (0, i)), pl.BlockSpec((tokens, 2 * tile), lambda i: (0, i)),
         whole, whole, whole, pl.BlockSpec((8, width), lambda i: (0, 0))],
        "feed_forward", 45e9, grid=(hidden // tile,), hold=hold, after=after,
        scratch=[pltpu.VMEM((tokens, width), F32) for _ in range(3)],
    )


class Group:
    def __init__(self):
        self.S, self.R = lax.axis_size("seq"), lax.axis_size("row")
        self.s, self.r = lax.axis_index("seq"), lax.axis_index("row")
        self.core = self.r % 2
        self.chunks = self.S
        self.members = self.S // 2
        self.member = (self.s // 4) * 2 + self.core
        self.first_half = self.s < self.S // 2
        self.even_row = self.s % 2 == 0
        self.places = [(s, r) for s in range(self.S) for r in range(self.R)]

    def index(self, s, r):
        return s * self.R + r

    def send(self, x, target):
        pairs = [(self.index(s, r), self.index(*target(s, r))) for s, r in self.places]
        return lax.ppermute(x, ("seq", "row"), pairs)

    def route(self, way):
        S = self.S

        def target(s, r):
            second = (s >= S // 2) if way == 0 else (s < S // 2)
            row = 2 * (r % 2) + (1 if second else 0)
            member = min(s, S - 1 - s)
            return (row + 4 * (member // 2), r - r % 2 + member % 2)

        return [(self.index(s, r), self.index(*target(s, r))) for s, r in self.places]

    def part(self, x, way):
        return jnp.where(self.first_half == (way == 0), x[0], x[1])

    def go(self, x, way):
        return lax.ppermute(x, ("seq", "row"), self.route(way))

    def back_part(self, low, high, way):
        return jnp.where(self.even_row == (way == 0), low, high)

    def back(self, x, way):
        return lax.ppermute(x, ("seq", "row"), [(t, f) for f, t in self.route(way)])

    def low_high(self, a, b):
        return jnp.where(self.even_row, a, b), jnp.where(self.even_row, b, a)

    def two_rows(self, a, b):
        return jnp.where(self.first_half, a, b), jnp.where(self.first_half, b, a)

    def peer(self, x, distance):
        return self.send(x, lambda s, r: (s ^ (4 * (distance >> 1)), r ^ (distance & 1)))

    def peers(self, x):
        return [x] + [self.peer(x, p) for p in range(1, self.members)]

    def core_swap(self, x):
        return self.send(x, lambda s, r: (s, r ^ 1))

    def all_sum(self, x):
        for axis, size in (("row", self.R), ("seq", self.S)):
            step = 1
            while step < size:
                x = x + lax.ppermute(x, axis, [(i, i ^ step) for i in range(size)])
                step *= 2
        return x

    def halves_of(self, left):
        half = left.shape[1] // 2
        theirs = lax.dynamic_slice_in_dim(left, (1 - self.core) * half, half, 1)
        return theirs, lax.dynamic_slice_in_dim(left, self.core * half, half, 1)

    def bit(self, name):
        return ((self.s if name[0] == "seq" else self.r) >> name[1]) & 1

    def names(self):
        top = self.S.bit_length() - 2
        row_bits = list(range(1, self.R.bit_length() - 1))
        return [("seq", k) for k in reversed(range(top))] + [("row", k) for k in reversed(row_bits)] + [("row", 0)]

    def begin(self, x):
        names = self.names()
        return x.reshape((2,) * len(names) + (x.shape[0] // 2 ** len(names), x.shape[1])), names

    def split(self, x, names, name):
        at = names.index(name)
        flat = x.reshape(math.prod(x.shape[:at]), 2, math.prod(x.shape[at + 1:-1]), x.shape[-1])
        give = lax.dynamic_index_in_dim(flat, 1 - self.bit(name), 1, keepdims=False)
        keep = lax.dynamic_index_in_dim(flat, self.bit(name), 1, keepdims=False)
        return give, keep

    def swap(self, give, name):
        size = self.S if name[0] == "seq" else self.R
        return lax.ppermute(give, name[0], [(i, i ^ (1 << name[1])) for i in range(size)])

    def merge(self, keep, got, x, names, name):
        at = names.index(name)
        total = (keep.astype(F32) + got.astype(F32)).astype(BF16)
        return total.reshape(x.shape[:at] + x.shape[at + 1:]), names[:at] + names[at + 1:]

    def last_sends(self, x):
        top = self.S.bit_length() - 2
        upper, half = self.s >> top, self.S // 2
        straight = lax.dynamic_index_in_dim(x, upper, 0, keepdims=False)
        crossed = lax.dynamic_index_in_dim(x, 1 - upper, 0, keepdims=False)
        one = self.send(straight, lambda s, r: ((r % 2) * half + s % half, (r - r % 2) + s // half))
        two = self.send(crossed, lambda s, r: ((r % 2) * half + s % half, (r - r % 2) + 1 - s // half))
        return one, two


class Scatter:
    def __init__(self, group, x, flip=False):
        self.group = group
        self.x, self.names = group.begin(x)
        row_names = [name for name in self.names if name[0] == "row" and name[1]]
        seq_names = [name for name in self.names if name[0] == "seq"]
        self.stages = (row_names if flip else row_names[::-1]) + seq_names[::-1]

    def start(self):
        if self.stages:
            self.give = self.group.split(self.x, self.names, self.stages[0])[0]
            self.got = self.group.swap(self.give, self.stages[0])
        else:
            self.got = self.group.last_sends(self.x)
            self.give = self.x

    def end(self):
        name = self.stages.pop(0)
        keep = self.group.split(self.x, self.names, name)[1]
        self.x, self.names = self.group.merge(keep, self.got, self.x, self.names, name)

    def step(self):
        if self.stages:
            self.end()
            self.start()

    def result(self):
        while self.stages:
            self.step()
        return self.got[0].astype(F32) + self.got[1].astype(F32)


def through(function, *args, run=(), hold=(), **more):
    hold = list(hold)
    outs, kept = function(*args, hold=hold + [one.x for one in run], after=[one.give for one in run], **more)
    for one, x in zip(run, kept[len(hold):]):
        one.x = x
    return outs, kept[:len(hold)]


def by_pairs(weight, axis):
    shape = weight.shape
    split = shape[:axis] + (shape[axis] // 256, 2, 2, 64) + shape[axis + 1:]
    return jnp.swapaxes(weight.reshape(split), axis + 1, axis + 2).reshape(shape)


def bias_rows(bias_table, sub):
    table = by_heads((bias_table - bias_table[BUCKETS - 1:]).T)
    levels = np.array([bucket_level(d) for d in range(2 * NEAR)])
    values = jnp.dot(table, jnp.asarray(np.eye(BUCKETS, dtype=np.float32)[levels].T), precision=HIGHEST)
    near = values[:, :sub] if sub <= 2 * NEAR else jnp.pad(values, ((0, 0), (0, sub - 2 * NEAR)))
    near = jnp.concatenate([near, jnp.full((HEADS, sub), MASK, F32)], axis=1)
    corner = jnp.concatenate([values[:, NEAR:], jnp.zeros((HEADS, 1), F32), values[:, 1:NEAR]], axis=1)
    return [jnp.broadcast_to(a[:, None], (HEADS, 8, a.shape[1])) for a in (near, corner)]


def by_heads(x):
    return jnp.swapaxes(x.reshape((4, 2, 2) + x.shape[1:]), 1, 2).reshape(x.shape)


def bias_table_sums(near, corner):
    def fold(wide, distances):
        matrix = np.zeros((8, wide, BUCKETS), np.float32)
        for row in range(8):
            for lane in range(wide):
                distance = distances((lane - row) % wide)
                if distance is not None:
                    matrix[row, lane, bucket_level(distance)] = 1.0
        return jnp.asarray(matrix.reshape(8 * wide, BUCKETS))

    sub = near.shape[2] // 2
    first = fold(2 * sub, lambda d: d if d < sub else None)
    second = fold(2 * NEAR, lambda d: NEAR + d if d < NEAR else (d - NEAR if d > NEAR else None))
    total = jnp.dot(near.reshape(HEADS, -1), first, precision=HIGHEST)
    total = total + jnp.dot(corner.reshape(HEADS, -1), second, precision=HIGHEST)
    rest = -jnp.sum(total[:, :BUCKETS - 1], axis=1, keepdims=True)
    return by_heads(jnp.concatenate([total[:, :BUCKETS - 1], rest], axis=1)).T


def on_device(tokens, segment_ids, memory, cotangent, gain_attend, gain_cross, gain_feed, bias_table,
              self_query, self_keyvalue, self_output, cross_query, cross_keyvalue, cross_output,
              feed_gate, feed_up, feed_down):
    group = Group()
    size, width = tokens.shape[1:]
    span = memory.shape[1]
    chunks = group.chunks
    sub = min(256, size)
    pad = 16

    numbers = jnp.pad(segment_ids.astype(BF16)[:, None, :], ((0, 0), (0, pad - 1), (0, width - size)))
    token_message = jnp.concatenate([tokens, numbers], axis=1)
    way_a = group.go(group.part(token_message, 0), 0)
    way_b = group.go(group.part(token_message, 1), 1)

    memory_rows = memory.reshape(-1, width)
    pairs = nn(memory_rows, cross_keyvalue).astype(BF16).reshape(2, span, width)
    own_query, own_output = by_pairs(self_query, 1), by_pairs(self_output, 0)
    other_query, other_output = by_pairs(cross_query, 1), by_pairs(cross_output, 0)
    near, near_back, corner, corner_back = bias_tiles(*bias_rows(bias_table, sub), sub)
    pairs_a, pairs_b = group.part(pairs, 0), group.part(pairs, 1)

    low, high = group.low_high(way_a, way_b)
    x = rows(low[:size], high[:size])
    memory_a = group.go(pairs_a, 0)

    (n1, kv), (pairs_b,) = by_rows(
        entry_kernel, "entry", 2e9, [(x, True), (gain_attend[None], False), (self_keyvalue, False)], [BF16, BF16], width,
        hold=[pairs_b], after=[pairs_a, own_query, own_output, other_query, other_output, near])
    memory_b = group.go(pairs_b, 1)
    kv_messages = group.peers(jnp.concatenate([kv, low[size:], high[size:]], axis=0))
    q = nn(n1, own_query).astype(BF16) * BF16(0.125)
    kv = jnp.concatenate([part[:2 * size] for part in kv_messages], axis=0)
    segments = jnp.concatenate([part[2 * size::pad, :size] for part in kv_messages], axis=0).astype(jnp.int32)
    meta = jnp.concatenate([group.member[None].astype(jnp.int32), segments[:, 0], segments[:, -1]])
    lane = jnp.arange(128)[None]
    same = (segments.reshape(-1, 1) == lane) & (lane < 4)
    key_marks = jnp.where(lane < 4, jnp.where(same, 0.0, MASK), jnp.where(lane < 7, -1.0, 0.0)).astype(BF16)
    query_marks = same[: 2 * size].astype(BF16)
    grad_a, grad_b = group.part(cotangent, 0), group.part(cotangent, 1)
    g_a = group.go(grad_a, 0)
    (o, lse), (grad_b, memory_a) = self_forward(
        meta, q, kv, query_marks, key_marks, near, corner, chunks, hold=[grad_b, memory_a], after=[grad_a, memory_b])
    g_b = group.go(grad_b, 1)
    memory_kv = rows(*group.low_high(memory_a, memory_b))
    (h1, n2, c), (memory_kv,) = by_rows(
        middle_kernel, "middle", 5e9,
        [(x, True), (o, True), (own_output, False), (gain_cross[None], False), (other_query, False)],
        [F32, BF16, BF16], width, hold=[memory_kv], after=[grad_b, g_a])
    memory_kv = jnp.concatenate(group.peers(memory_kv), axis=0)
    (co, cross_lse), _ = cross_forward(c, memory_kv, after=[grad_b])
    g = rows(*group.low_high(g_a, g_b))
    (out, n3, hidden, dgu, dh2, r2, dco, dgain_feed), _ = feed_forward(
        h1, co, other_output, g, gain_feed[None], feed_gate, feed_up, feed_down)
    out_parts = [group.back_part(out[:size], out[size:], way) for way in range(2)]
    out_a = group.back(out_parts[0], 0)

    hidden_theirs, hidden_mine = group.halves_of(hidden)
    n3_theirs, n3_mine = group.halves_of(n3)
    down_other = group.core_swap(tn(hidden_theirs, g).astype(BF16))
    dgu_other = group.core_swap(tn(n3_theirs, dgu).astype(BF16))
    down_part = (tn(hidden_mine, g) + down_other.astype(F32)).astype(BF16)
    dgu_part = (tn(n3_mine, dgu) + dgu_other.astype(F32)).astype(BF16)
    quarter = dgu_part.shape[1] // 4
    feed = [
        Scatter(group, down_part),
        Scatter(group, dgu_part[:, :quarter]),
        Scatter(group, dgu_part[:, quarter:], True),
    ]
    for one in feed:
        one.start()

    out_b = group.back(out_parts[1], 1)
    (dc, dm), (out_a,) = through(
        cross_backward, c, dco, co, cross_lse, memory_kv, run=feed, hold=[out_a])
    dm = lanes(dm[0], dm[1]).reshape(group.members, 2 * span, width)
    dm_parts = [dm[0]] + [group.peer(dm[p], p) for p in range(1, group.members)]
    (dh1, r1, do, dgain_cross), (out_a, dm_own) = through(
        by_rows, back_middle_kernel, "back_middle", 5e9,
        [(dc, True), (other_query, False), (h1, True), (gain_cross[None], False), (dh2, True), (own_output, False)],
        [F32, BF16, BF16], width, dgain=True, run=feed, hold=[out_a, dm_parts[0]])
    layer_output = jnp.stack(group.two_rows(out_a, out_b))
    dm = sum((part.astype(F32) for part in dm_parts[1:]), dm_own.astype(F32)).astype(BF16)
    dm_a = group.back(group.back_part(dm[:span], dm[span:], 0), 0)
    dm_b = group.back(group.back_part(dm[:span], dm[span:], 1), 1)
    for one in feed:
        one.step()
    cross_lefts = [group.halves_of(left) for left in (co, n2, o)]
    cross_others = [group.core_swap(tn(left[0], right).astype(BF16)) for left, right in zip(cross_lefts, (r2, dc, r1))]
    cross_parts = [
        (tn(left[1], right) + other.astype(F32)).astype(BF16)
        for left, right, other in zip(cross_lefts, (r2, dc, r1), cross_others)
    ]
    dm = rows(*group.two_rows(dm_a, dm_b))
    memory_lefts = group.halves_of(memory_rows)
    memory_other = group.core_swap(tn(memory_lefts[0], dm).astype(BF16))
    memory_grad = nt(dm, cross_keyvalue).astype(BF16).reshape(memory.shape)
    memory_part = (tn(memory_lefts[1], dm) + memory_other.astype(F32)).astype(BF16)
    cross = [
        Scatter(group, jnp.concatenate([by_pairs(cross_parts[0], 0), cross_parts[1]], axis=1)),
        Scatter(group, jnp.concatenate([by_pairs(cross_parts[2], 0), memory_part], axis=1), True),
    ]
    for one in cross:
        one.start()

    back = None
    parts = 4
    for part in range(parts):
        back, _ = through(
            self_backward, meta, q, do, o, lse, kv, query_marks, key_marks, near_back, corner_back, chunks,
            part, parts, back, run=feed + cross)
        if part == 0:
            for one in feed:
                one.step()
        if part == 1:
            for one in cross:
                one.step()
        if part == 2:
            for one in feed + cross:
                one.step()
    dq, dkv, near_sum, corner_sum = back
    dkv = lanes(dkv[0], dkv[1]).reshape(group.members, 2 * size, width)
    dkv = sum((group.peer(dkv[p], p).astype(F32) for p in range(1, group.members)), dkv[0].astype(F32)).astype(BF16)
    (tokens_grad, dgain_attend), _ = through(
        by_rows, exit_kernel, "exit", 5e9,
        [(dq, True), (own_query, False), (dkv, True), (self_keyvalue, False), (x, True), (gain_attend[None], False), (dh1, True)],
        [BF16], width, dgain=True, run=cross)
    token_a = group.back(group.back_part(tokens_grad[:size], tokens_grad[size:], 0), 0)
    left = group.halves_of(n1)
    right = lanes(dq, dkv)
    other = group.core_swap(tn(left[0], right).astype(BF16))
    own_part = (tn(left[1], right) + other.astype(F32)).astype(BF16)
    own = [Scatter(group, own_part[:, :width]), Scatter(group, own_part[:, width:], True)]
    for one in own:
        one.start()
    token_b = group.back(group.back_part(tokens_grad[:size], tokens_grad[size:], 1), 1)
    tokens_grad = jnp.stack(group.two_rows(token_a, token_b))
    grad_own = [one.result() for one in own]
    grad_cross = [one.result() for one in cross]
    grad_feed = [one.result() for one in feed]

    dbias = bias_table_sums(near_sum, corner_sum)
    small = jnp.stack([jnp.sum(dgain_attend, axis=0), jnp.sum(dgain_cross, axis=0), jnp.sum(dgain_feed, axis=0),
                       jnp.pad(dbias.reshape(-1), (0, width - dbias.size))])
    small = group.all_sum(small)

    dgu = jnp.concatenate(grad_feed[1:], axis=1).reshape(-1, feed_gate.shape[1] // 256, 2, 256)
    return (
        layer_output,
        tokens_grad,
        memory_grad,
        by_pairs(grad_own[0], 1),
        grad_own[1],
        grad_cross[1][:, :width],
        by_pairs(grad_cross[0][:, width:], 1),
        grad_cross[1][:, width:],
        grad_cross[0][:, :width],
        dgu[:, :, 0].reshape(-1, feed_gate.shape[1]),
        dgu[:, :, 1].reshape(-1, feed_gate.shape[1]),
        grad_feed[0],
        small[0],
        small[1],
        small[2],
        small[3, :dbias.size].reshape(dbias.shape),
    )


def solution(mesh):
    data, whole, grads = P("row", "seq", None), P(), P(("seq", "row"), None)
    in_specs = (data, P("row", "seq"), data, data) + (whole,) * 13
    out_specs = (data,) * 3 + (grads,) * 9 + (whole,) * 4
    return jax.shard_map(on_device, mesh=mesh, in_specs=in_specs, out_specs=out_specs, check_vma=False)
```

```python
import functools
import math

import jax
import jax.numpy as jnp
import numpy as np
from jax import lax
from jax.experimental import pallas as pl
from jax.experimental.pallas import tpu as pltpu
from jax.sharding import PartitionSpec as P

HEADS = 16
BUCKETS = 32
MAX_DIST = 128
HIGHEST = lax.Precision.HIGHEST
F32, BF16 = jnp.float32, jnp.bfloat16
MASK = -float(2.0**100)
NEAR = 128
VMEM = 56 * 1024 * 1024
CHUNK = 512
PAD = 16
FEED = 512
COST = {
    "entry": 6, "query": 6, "gather": 5, "self_forward": 23, "middle": 9, "cross_forward": 20, "feed_forward": 70,
    "weight_grads": 9, "stage": 4, "cross_backward": 31, "back_middle": 12, "self_backward": 18, "exit": 11,
}
COST_SCALE = 0.001e9
GELU_A = math.sqrt(2.0 / math.pi)
GELU_B = GELU_A * 0.044715


def bucket_level(distance):
    exact_part = BUCKETS // 2
    if distance < exact_part:
        return distance
    which_bucket = exact_part + math.floor(
        math.log(distance / exact_part) / math.log(MAX_DIST / exact_part) * (BUCKETS - exact_part)
    )
    return min(BUCKETS - 1, which_bucket)


def call(kernel, inputs, in_specs, out_shape, out_specs, name, flops, grid=(), scratch=(), prefetch=0,
         hold=(), after=(), alias=None):
    hold, after = list(hold), list(after)
    count_in, count_out = len(inputs), len(out_shape)
    anywhere = pl.BlockSpec(memory_space=pl.ANY)

    def body(*refs):
        kept = count_in + len(hold) + len(after)
        kernel(*refs[:count_in], *refs[kept:kept + count_out], *refs[kept + count_out + len(hold):])

    aliases = {count_in + i: count_out + i for i in range(len(hold))}
    aliases.update(alias or {})
    outs = pl.pallas_call(
        body,
        grid_spec=pltpu.PrefetchScalarGridSpec(
            num_scalar_prefetch=prefetch,
            grid=grid,
            in_specs=list(in_specs) + [anywhere] * (len(hold) + len(after)),
            out_specs=list(out_specs) + [anywhere] * len(hold),
            scratch_shapes=list(scratch),
        ),
        out_shape=list(out_shape) + [jax.ShapeDtypeStruct(x.shape, x.dtype) for x in hold],
        input_output_aliases=aliases,
        compiler_params=pltpu.CompilerParams(vmem_limit_bytes=VMEM),
        cost_estimate=pl.CostEstimate(flops=int(COST.get(name, 5) * COST_SCALE), bytes_accessed=10**4, transcendentals=0),
        name=name,
    )(*inputs, *hold, *after)
    return list(outs[:count_out]), list(outs[count_out:])


def nt(a, b):
    return lax.dot_general(a, b, (((1,), (1,)), ((), ())), preferred_element_type=F32)


def nn(a, b):
    return jnp.dot(a, b, preferred_element_type=F32)


def tn(a, b):
    return lax.dot_general(a, b, (((0,), (0,)), ((), ())), preferred_element_type=F32)


def halves(block):
    low = lax.broadcasted_iota(jnp.int32, block.shape, 1) < 64
    zero = jnp.zeros_like(block)
    return jnp.where(low, block, zero), jnp.where(low, zero, block)


def lanes(a, b):
    return jnp.concatenate([a, b], axis=1)


def rows(a, b):
    return jnp.concatenate([a, b], axis=0)


def chunk_of(member, part, chunks):
    high = jnp.bitwise_xor(part, member % 2)
    return jnp.where(high == 0, member // 2, chunks - 1 - member // 2)


def slot_of(member, chunk, chunks):
    high = (chunk >= chunks // 2).astype(jnp.int32)
    other = jnp.where(chunk >= chunks // 2, chunks - 1 - chunk, chunk)
    return 2 * jnp.bitwise_xor(other, member // 2) + jnp.bitwise_xor(high, member % 2)


def first_block(meta, member, chunk, chunks):
    mine = meta[1 + slot_of(member, chunk, chunks)]

    def skip(block, start):
        last = meta[1 + chunks + slot_of(member, block, chunks)]
        return start + jnp.where((block < chunk) & (last < mine), 1, 0)

    return lax.fori_loop(0, chunks, skip, jnp.int32(0))


def self_forward_kernel(chunks, sub, meta, q_ref, k_ref, v_ref, qf_ref, kf_ref, near_ref, corner_ref,
                        o_ref, lse_ref, acc_ref, m_ref):
    size = q_ref.shape[0]
    member = meta[0]
    chunk = chunk_of(member, pl.program_id(1), chunks)
    q_both = [lanes(part, qf_ref[...]) for part in halves(q_ref[...])]

    def values(at, length):
        low, high = halves(v_ref[pl.ds(at, length), :])
        one_low, one_high = halves(jnp.ones((length, 128), BF16))
        return rows(lanes(low, one_low), lanes(high, one_high))

    own = pl.multiple_of(slot_of(member, chunk, chunks) * size, size)
    for strip in range(size // sub):
        span = (strip + 1) * sub
        here = slice(strip * sub, span)
        keys = lanes(k_ref[pl.ds(own, span), :], kf_ref[pl.ds(own, span), :])
        weights = []
        for head in range(2):
            s = nt(q_both[head][here], keys)
            last = s[:, span - sub:] + near_ref[head]
            if strip:
                edge = s[:, span - sub - NEAR:span - sub]
                edge = rows(edge[:NEAR] + corner_ref[head], edge[NEAR:])
                s = jnp.concatenate([s[:, :span - sub - NEAR], edge, last], axis=1)
            else:
                s = last
            top = jnp.max(s, axis=1, keepdims=True)
            m_ref[head, here, :] = jnp.broadcast_to(top, (sub, 128))
            weights.append(jnp.exp(s - top).astype(BF16))
        acc_ref[here, :] = nn(lanes(*weights), values(own, span))

    def far(block, carry):
        at = pl.multiple_of(slot_of(member, block, chunks) * size, size)
        keys = lanes(k_ref[pl.ds(at, size), :], kf_ref[pl.ds(at, size), :])
        flag = jnp.where(block == chunk - 1, 1.0, 0.0).astype(F32)
        weights, scales = [], []
        for head in range(2):
            s = nt(q_both[head], keys)
            edge = s[:NEAR, size - NEAR:] + corner_ref[head] * flag
            s = rows(lanes(s[:NEAR, :size - NEAR], edge), s[NEAR:])
            old = m_ref[head]
            top = jnp.maximum(old, jnp.max(s, axis=1, keepdims=True))
            scales.append(jnp.exp(old - top))
            m_ref[head] = top
            weights.append(jnp.exp(s - top[:, :1]).astype(BF16))
        low = lax.broadcasted_iota(jnp.int32, (size, 128), 1) < 64
        scale = jnp.where(low, scales[0], scales[1])
        acc_ref[...] = acc_ref[...] * lanes(scale, scale) + nn(lanes(*weights), values(at, size))
        return carry

    lax.fori_loop(first_block(meta, member, chunk, chunks), chunk, far, 0)
    low = lax.broadcasted_iota(jnp.int32, (size, 128), 1) < 64
    total = acc_ref[:, 128:]
    o_ref[...] = (acc_ref[:, :128] / total).astype(BF16)
    lse_ref[...] = jnp.where(low, m_ref[0], m_ref[1]) + jnp.log(total)


def pieces(column, shape):
    lane = lax.broadcasted_iota(jnp.int32, shape, 1)
    high = column.astype(BF16).astype(F32)
    rest = column - high
    middle = rest.astype(BF16).astype(F32)
    low = rest - middle
    full = jnp.where(lane == 4, high, jnp.where(lane == 5, middle, jnp.where(lane == 6, low, 0.0)))
    return full.astype(BF16)


def back_operands(q_ref, do_ref, o_ref, lse_ref, qf):
    shape = q_ref.shape
    q_both = halves(q_ref[...])
    do_both = halves(do_ref[...])
    product = do_ref[...].astype(F32) * o_ref[...].astype(F32)
    low = lax.broadcasted_iota(jnp.int32, shape, 1) < 64
    deltas = [jnp.sum(jnp.where(low, product, 0.0), axis=1, keepdims=True),
              jnp.sum(jnp.where(low, 0.0, product), axis=1, keepdims=True)]
    logs = [lse_ref[:, 0:1], lse_ref[:, 64:65]]
    extra = [pieces(log, shape) for log in logs]
    if qf is not None:
        extra = [part + qf for part in extra]
    q_wide = [lanes(part, more) for part, more in zip(q_both, extra)]
    do_wide = [lanes(part, pieces(delta, shape)) for part, delta in zip(do_both, deltas)]
    return q_both, do_both, q_wide, do_wide


def diagonal_sums(block):
    count, wide = block.shape[0], 2 * block.shape[1]
    block = lanes(block, jnp.zeros_like(block))
    while count > 8:
        count = count // 2
        block = block[:count] + pltpu.roll(block[count:], wide - count, 1)
    return block


def self_backward_kernel(chunks, sub, meta, q_ref, do_ref, o_ref, lse_ref, k_ref, v_ref, qf_ref, kf_ref,
                         near_ref, corner_ref, dq_ref, own_ref, peer_ref, near_out, corner_out,
                         dq_acc, dk_acc, dv_acc, near_acc, corner_acc):
    size = q_ref.shape[0]
    member = meta[0]
    chunk = chunk_of(member, pl.program_id(2), chunks)
    first = (pl.program_id(1) == 0) & (pl.program_id(2) == 0)
    last = (pl.program_id(1) == 1) & (pl.program_id(2) == 1)

    @pl.when(first)
    def _():
        dk_acc[...] = jnp.zeros_like(dk_acc)
        dv_acc[...] = jnp.zeros_like(dv_acc)

    @pl.when(pl.program_id(2) == 0)
    def _():
        near_acc[...] = jnp.zeros_like(near_acc)
        corner_acc[...] = jnp.zeros_like(corner_acc)

    q_both, do_both, q_wide, do_wide = back_operands(q_ref, do_ref, o_ref, lse_ref, qf_ref[...])
    own = pl.multiple_of(slot_of(member, chunk, chunks) * size, size)
    dq_acc[...] = jnp.zeros_like(dq_acc)

    def add(at, length, here, weights, grads, keys):
        dv_acc[pl.ds(at, length), :] += nn(lanes(*weights), rows(do_both[0][here], do_both[1][here]))
        dk_acc[pl.ds(at, length), :] += nn(lanes(*grads), rows(q_both[0][here], q_both[1][here]))
        dq_acc[here, :] += tn(rows(*grads), rows(*halves(keys)))

    for strip in range(size // sub):
        at = pl.multiple_of(own + strip * sub, sub)
        here = slice(strip * sub, size)
        k, v, kf = (ref[pl.ds(at, sub), :] for ref in (k_ref, v_ref, kf_ref))
        keys, vals = lanes(k, kf), lanes(v, kf)
        weights, grads = [], []
        for head in range(2):
            s = nt(keys, q_wide[head][here])
            dp = nt(vals, do_wide[head][here])
            block = s[:, :sub] + near_ref[head]
            more = (strip + 1) * sub < size
            if more:
                edge = s[sub - NEAR:, sub:sub + NEAR] + corner_ref[head]
                rest = s[:, sub:]
                rest = rows(rest[:sub - NEAR], lanes(edge, rest[sub - NEAR:, NEAR:]))
                s = lanes(block, rest)
            else:
                s = block
            p = jnp.exp(s)
            ds = p * dp
            near_acc[head] += ds[:, :sub]
            if more:
                corner_acc[head] += ds[sub - NEAR:, sub:sub + NEAR]
            weights.append(p.astype(BF16))
            grads.append(ds.astype(BF16))
        add(at, sub, here, weights, grads, k)

    def far(block, carry):
        at = pl.multiple_of(slot_of(member, block, chunks) * size, size)
        k, v, kf = (ref[pl.ds(at, size), :] for ref in (k_ref, v_ref, kf_ref))
        keys, vals = lanes(k, kf), lanes(v, kf)
        flag = jnp.where(block == chunk - 1, 1.0, 0.0).astype(F32)
        weights, grads = [], []
        for head in range(2):
            s = nt(keys, q_wide[head])
            dp = nt(vals, do_wide[head])
            edge = s[size - NEAR:, :NEAR] + corner_ref[head] * flag
            s = rows(s[:size - NEAR], lanes(edge, s[size - NEAR:, NEAR:]))
            p = jnp.exp(s)
            ds = p * dp
            corner_acc[head] += ds[size - NEAR:, :NEAR] * flag
            weights.append(p.astype(BF16))
            grads.append(ds.astype(BF16))
        add(at, size, slice(None), weights, grads, k)
        return carry

    lax.fori_loop(first_block(meta, member, chunk, chunks), chunk, far, 0)
    dq_ref[...] = (dq_acc[...] * 0.125).astype(BF16)

    @pl.when(last)
    def _():
        for side, acc in enumerate((dk_acc, dv_acc)):
            own_ref[side] = acc[: 2 * size, :].astype(BF16)
            for other in range(peer_ref.shape[0]):
                at = 2 * size * (other + 1)
                peer_ref[other, side] = acc[at:at + 2 * size, :].astype(BF16)

    @pl.when(pl.program_id(2) == 1)
    def _():
        for head in range(2):
            near_out[head] = diagonal_sums(near_acc[head])
            corner_out[head] = diagonal_sums(corner_acc[head])


def with_before(kernel, inputs, in_specs, before):
    if before is None:
        return kernel, tuple(inputs), list(in_specs), None
    count = len(inputs)

    def body(*refs):
        kernel(*refs[:count], *refs[count + len(before):])

    specs = list(in_specs) + [pl.BlockSpec(memory_space=pl.ANY)] * len(before)
    return body, tuple(inputs) + tuple(before), specs, {count + i: i for i in range(len(before))}


def self_forward(meta, q, kv, qf, kf, near, corner, chunks, part, parts, before, hold=(), after=()):
    size = q.shape[0] // 2
    sub = min(256, size)
    length = kv.shape[0]
    blocks = 8 // parts
    shift = blocks * part
    own = pl.BlockSpec((size, 128), lambda b, c, m: (c, b + shift))
    kernel, inputs, in_specs, alias = with_before(
        functools.partial(self_forward_kernel, chunks, sub),
        (meta, q, kv, kv, qf, kf, near, corner),
        [
            own,
            pl.BlockSpec((length, 128), lambda b, c, m: (0, (b + shift) // 2)),
            pl.BlockSpec((length, 128), lambda b, c, m: (0, 4 + (b + shift) // 2)),
            pl.BlockSpec((size, 128), lambda b, c, m: (c, 0)),
            pl.BlockSpec((length, 128), lambda b, c, m: (0, 0)),
            pl.BlockSpec((2, sub, sub), lambda b, c, m: (b + shift, 0, 0)),
            pl.BlockSpec((2, NEAR, NEAR), lambda b, c, m: (b + shift, 0, 0)),
        ], before)
    return call(
        kernel, inputs, in_specs,
        [jax.ShapeDtypeStruct(q.shape, BF16), jax.ShapeDtypeStruct(q.shape, F32)],
        [own, own],
        "self_forward", 4e10 / parts, grid=(blocks, 2), prefetch=1, hold=hold, after=after, alias=alias,
        scratch=[pltpu.VMEM((size, 256), F32), pltpu.VMEM((2, size, 128), F32)],
    )


def self_backward(meta, q, do, o, lse, kv, qf, kf, near, corner, chunks, part, parts, before, hold=(), after=()):
    pairs = 4 // parts
    shift = pairs * part
    size = q.shape[0] // 2
    sub = min(256, size)
    length = kv.shape[0]
    own = pl.BlockSpec((size, 128), lambda g, b, c, m: (c, 2 * (g + shift) + b))
    inputs = [meta, q, do, o, lse, kv, kv, qf, kf, near, corner]
    in_specs = [
        own, own, own, own,
        pl.BlockSpec((length, 128), lambda g, b, c, m: (0, g + shift)),
        pl.BlockSpec((length, 128), lambda g, b, c, m: (0, 4 + g + shift)),
        pl.BlockSpec((size, 128), lambda g, b, c, m: (c, 0)),
        pl.BlockSpec((length, 128), lambda g, b, c, m: (0, 0)),
        pl.BlockSpec((2, sub, sub), lambda g, b, c, m: (2 * (g + shift) + b, 0, 0)),
        pl.BlockSpec((2, NEAR, NEAR), lambda g, b, c, m: (2 * (g + shift) + b, 0, 0)),
    ]
    kernel, inputs, in_specs, alias = with_before(
        functools.partial(self_backward_kernel, chunks, sub), inputs, in_specs, before)
    others = length // (2 * size) - 1
    return call(
        kernel, inputs, in_specs,
        [
            jax.ShapeDtypeStruct(q.shape, BF16),
            jax.ShapeDtypeStruct((2, 2 * size, 512), BF16),
            jax.ShapeDtypeStruct((others, 2, 2 * size, 512), BF16),
            jax.ShapeDtypeStruct((16, 8, 2 * sub), F32),
            jax.ShapeDtypeStruct((16, 8, 2 * NEAR), F32),
        ],
        [
            own,
            pl.BlockSpec((2, 2 * size, 128), lambda g, b, c, m: (0, 0, g + shift)),
            pl.BlockSpec((others, 2, 2 * size, 128), lambda g, b, c, m: (0, 0, 0, g + shift)),
            pl.BlockSpec((2, 8, 2 * sub), lambda g, b, c, m: (2 * (g + shift) + b, 0, 0)),
            pl.BlockSpec((2, 8, 2 * NEAR), lambda g, b, c, m: (2 * (g + shift) + b, 0, 0)),
        ],
        "self_backward", 6e10 / parts, grid=(pairs, 2, 2), prefetch=1, hold=hold, after=after, alias=alias,
        scratch=[
            pltpu.VMEM((size, 128), F32),
            pltpu.VMEM((length, 128), F32),
            pltpu.VMEM((length, 128), F32),
            pltpu.VMEM((2, sub, sub), F32),
            pltpu.VMEM((2, NEAR, NEAR), F32),
        ],
    )


def stacked(refs):
    return refs[0][...] if len(refs) == 1 else jnp.concatenate([ref[...] for ref in refs], axis=0)


def cross_forward_kernel(count, q_ref, *refs):
    keys, v = stacked(refs[:count]), stacked(refs[count:2 * count])
    o_ref, lse_ref = refs[2 * count:]
    length = keys.shape[0]
    low, high = halves(v)
    one_low, one_high = halves(jnp.ones((length, 128), BF16))
    values = rows(lanes(low, one_low), lanes(high, one_high))
    weights, tops = [], []
    for part in halves(q_ref[...]):
        s = nt(part, keys)
        top = jnp.max(s, axis=1, keepdims=True)
        tops.append(top)
        weights.append(jnp.exp(s - top).astype(BF16))
    acc = nn(lanes(*weights), values)
    is_low = lax.broadcasted_iota(jnp.int32, q_ref.shape, 1) < 64
    total = acc[:, 128:]
    o_ref[...] = (acc[:, :128] / total).astype(BF16)
    lse_ref[...] = jnp.where(is_low, tops[0], tops[1]) + jnp.log(total)


def cross_backward_kernel(count, q_ref, do_ref, o_ref, lse_ref, *refs):
    k, v = stacked(refs[:count]), stacked(refs[count:2 * count])
    dq_ref, dkv_refs, (dk_acc, dv_acc) = refs[2 * count], refs[2 * count + 1:3 * count + 1], refs[3 * count + 1:]
    first = (pl.program_id(1) == 0) & (pl.program_id(2) == 0)
    last = (pl.program_id(1) == 1) & (pl.program_id(2) == 1)

    @pl.when(first)
    def _():
        dk_acc[...] = jnp.zeros_like(dk_acc)
        dv_acc[...] = jnp.zeros_like(dv_acc)

    q_both, do_both, q_wide, do_wide = back_operands(q_ref, do_ref, o_ref, lse_ref, None)
    lane = lax.broadcasted_iota(jnp.int32, k.shape, 1)
    minus = jnp.where((lane >= 4) & (lane < 7), -1.0, 0.0).astype(BF16)
    keys, vals = lanes(k, minus), lanes(v, minus)
    weights, grads = [], []
    for head in range(2):
        p = jnp.exp(nt(keys, q_wide[head]))
        ds = p * nt(vals, do_wide[head])
        weights.append(p.astype(BF16))
        grads.append(ds.astype(BF16))
    dv_acc[...] += nn(lanes(*weights), rows(*do_both))
    dk_acc[...] += nn(lanes(*grads), rows(*q_both))
    dq_ref[...] = (tn(rows(*grads), rows(*halves(k))) * 0.125).astype(BF16)

    @pl.when(last)
    def _():
        part = dk_acc.shape[0] // count
        for number, ref in enumerate(dkv_refs):
            at = slice(number * part, (number + 1) * part)
            ref[0] = dk_acc[at, :].astype(BF16)
            ref[1] = dv_acc[at, :].astype(BF16)


def cross_forward(q, memories, hold=(), after=()):
    size, part, count = q.shape[0] // 2, memories[0].shape[0], len(memories)
    own = pl.BlockSpec((size, 128), lambda b, c: (c, b))
    return call(
        functools.partial(cross_forward_kernel, count), (q, *memories, *memories),
        [own] + [pl.BlockSpec((part, 128), lambda b, c: (0, b // 2))] * count
        + [pl.BlockSpec((part, 128), lambda b, c: (0, 4 + b // 2))] * count,
        [jax.ShapeDtypeStruct(q.shape, BF16), jax.ShapeDtypeStruct(q.shape, F32)],
        [own, own],
        "cross_forward", 15e9, grid=(8, 2), hold=hold, after=after,
    )


def cross_backward(q, do, o, lse, memories, hold=(), after=()):
    size, part, count = q.shape[0] // 2, memories[0].shape[0], len(memories)
    own = pl.BlockSpec((size, 128), lambda g, b, c: (c, 2 * g + b))
    return call(
        functools.partial(cross_backward_kernel, count), (q, do, o, lse, *memories, *memories),
        [own, own, own, own] + [pl.BlockSpec((part, 128), lambda g, b, c: (0, g))] * count
        + [pl.BlockSpec((part, 128), lambda g, b, c: (0, 4 + g))] * count,
        [jax.ShapeDtypeStruct(q.shape, BF16)] + [jax.ShapeDtypeStruct((2, part, 512), BF16)] * count,
        [own] + [pl.BlockSpec((2, part, 128), lambda g, b, c: (0, 0, g))] * count,
        "cross_backward", 30e9, grid=(4, 2, 2), hold=hold, after=after,
        scratch=[pltpu.VMEM((part * count, 128), F32), pltpu.VMEM((part * count, 128), F32)],
    )


def add_kernel(*refs):
    terms, outs = refs[:-2], refs[-2:]
    for number, out in enumerate(outs):
        at = slice(number * out.shape[0], (number + 1) * out.shape[0])
        sides = [sum((ref[side, at, :].astype(F32) for ref in terms[1:]), terms[0][side, at, :].astype(F32)) for side in range(2)]
        out[...] = lanes(*sides).astype(BF16)


def add_memory(terms, hold=(), after=()):
    shape = jax.ShapeDtypeStruct((terms[0].shape[1] // 2, 2 * terms[0].shape[2]), BF16)
    (low, high), kept = call(
        add_kernel, tuple(terms), [pl.BlockSpec(x.shape, lambda: (0, 0, 0)) for x in terms],
        [shape] * 2, [pl.BlockSpec(shape.shape, lambda: (0, 0))] * 2, "add_memory", 1e9, hold=hold, after=after)
    return low, high, kept


def bias_kernel(sub, near_ref, corner_ref, near_out, back_out, corner_out, corner_back):
    for head in range(2):
        wide = jnp.broadcast_to(near_ref[head, :1], (sub, 2 * sub))
        block = pltpu.roll(wide, 0, 1, stride=1, stride_axis=0)[:, :sub]
        back_out[head] = block
        near_out[head] = block.T
        wide = jnp.broadcast_to(corner_ref[head, :1], (NEAR, 2 * NEAR))
        block = pltpu.roll(wide, 0, 1, stride=1, stride_axis=0)[:, :NEAR]
        corner_back[head] = block
        corner_out[head] = block.T


def bias_tiles(near, corner, sub):
    def spec(a, b):
        return pl.BlockSpec((2, a, b), lambda h: (h, 0, 0))

    def shape(a):
        return jax.ShapeDtypeStruct((16, a, a), F32)

    return pl.pallas_call(
        functools.partial(bias_kernel, sub),
        grid=(8,),
        in_specs=[spec(8, 2 * sub), spec(8, 2 * NEAR)],
        out_specs=[spec(sub, sub), spec(sub, sub), spec(NEAR, NEAR), spec(NEAR, NEAR)],
        out_shape=[shape(sub), shape(sub), shape(NEAR), shape(NEAR)],
        compiler_params=pltpu.CompilerParams(vmem_limit_bytes=VMEM),
        name="bias_tiles",
    )(near, corner)


def inverse_rms(h):
    return lax.rsqrt(jnp.mean(h * h, axis=1, keepdims=True) + 1e-06)


def norm(values, gain):
    return (values * inverse_rms(values) * gain).astype(BF16)


def norm_back(h, dn, gain):
    scale = inverse_rms(h)
    unit = h * scale
    spread = dn * unit
    share = jnp.mean(spread * gain, axis=1, keepdims=True)
    gain_part = jnp.sum(spread.reshape(-1, 8, spread.shape[1]), axis=0)
    return scale * (dn * gain - unit * share), gain_part


def entry_kernel(a_ref, b_ref, gain_ref, weight_ref, x_ref, n_ref, message_ref):
    tokens = x_ref.shape[0]
    size = tokens // 2
    tile = min(256, size)
    for side, ref in enumerate((a_ref, b_ref)):
        for i in range(size // tile):
            at = slice(side * size + i * tile, side * size + (i + 1) * tile)
            x = ref[i * tile:(i + 1) * tile, :]
            x_ref[at, :] = x
            n_ref[at, :] = norm(x.astype(F32), gain_ref[...])
            message_ref[at, :] = nn(n_ref[at, :], weight_ref[...]).astype(BF16)
        message_ref[tokens + side * PAD:tokens + (side + 1) * PAD, :] = ref[size:, :]


def entry(way_a, way_b, gain, weight, hold=(), after=()):
    tokens, width = 2 * (way_a.shape[0] - PAD), way_a.shape[1]
    inputs = (way_a, way_b, gain, weight)
    shapes = [jax.ShapeDtypeStruct((count, width), BF16) for count in (tokens, tokens, tokens + 2 * PAD)]
    return call(entry_kernel, inputs, [pl.BlockSpec(y.shape, lambda: (0, 0)) for y in inputs], shapes,
                [pl.BlockSpec(s.shape, lambda: (0, 0)) for s in shapes], "entry", 2e9, hold=hold, after=after)


def unpack_kernel(a_ref, b_ref, memory_ref, g_ref):
    span, size = memory_ref.shape[0] // 2, g_ref.shape[0] // 2
    for side, ref in enumerate((a_ref, b_ref)):
        g_ref[side * size:(side + 1) * size, :] = ref[:size, :]
        memory_ref[side * span:(side + 1) * span, :] = ref[size:, :]


def unpack(second_a, second_b, size, after):
    count, width = second_a.shape
    whole = pl.BlockSpec((count, width), lambda: (0, 0))
    shapes = [jax.ShapeDtypeStruct((2 * (count - size), width), BF16), jax.ShapeDtypeStruct((2 * size, width), BF16)]
    outs, _ = call(unpack_kernel, (second_a, second_b), [whole, whole], shapes,
                   [pl.BlockSpec(s.shape, lambda: (0, 0)) for s in shapes], "unpack", 1e9, after=after)
    return outs


def query_kernel(n_ref, weight_ref, q_ref):
    q_ref[...] = nn(n_ref[...], weight_ref[...]).astype(BF16) * BF16(0.125)


def gather_kernel(member_ref, *refs):
    messages = refs[:len(refs) - 4]
    kv_ref, key_ref, query_ref, meta_ref = refs[len(refs) - 4:]
    step = pl.program_id(0)
    tokens = messages[0].shape[0] - 2 * PAD
    size = tokens // 2
    for p, message in enumerate(messages):
        @pl.when(step == p)
        def _(p=p, message=message):
            kv_ref[...] = message[:tokens, :]
            shape = (size, 128)
            lane = lax.broadcasted_iota(jnp.int32, shape, 1)
            place = lax.broadcasted_iota(jnp.int32, (8, 128), 1)
            chunks = 2 * len(messages)
            meta = meta_ref[...]
            if p == 0:
                meta = jnp.where(place == 0, member_ref[0], 0)
            for side in range(2):
                at = tokens + side * PAD
                numbers = message[at:at + PAD, :size].astype(F32)[:1]
                column = jnp.broadcast_to(numbers, (128, size)).T.astype(jnp.int32)
                same = (column == lane) & (lane < 4)
                marks = jnp.where(lane < 4, jnp.where(same, 0.0, MASK), jnp.where(lane < 7, -1.0, 0.0))
                key_ref[side * size:(side + 1) * size, :] = marks.astype(BF16)
                if p == 0:
                    query_ref[side * size:(side + 1) * size, :] = jnp.where(same, 1.0, 0.0).astype(BF16)
                slot = 2 * p + side
                meta = jnp.where(place == 1 + slot, column[:1, :], meta)
                meta = jnp.where(place == 1 + chunks + slot, column[size - 1:, :], meta)
            meta_ref[...] = meta


def gather(member, messages, hold=(), after=()):
    tokens, width = messages[0].shape[0] - 2 * PAD, messages[0].shape[1]
    count = len(messages)
    shapes = [
        jax.ShapeDtypeStruct((count * tokens, width), BF16),
        jax.ShapeDtypeStruct((count * tokens, 128), BF16),
        jax.ShapeDtypeStruct((tokens, 128), BF16),
        jax.ShapeDtypeStruct((8, 128), jnp.int32),
    ]
    outs, kept = call(
        gather_kernel, (member,) + tuple(messages),
        [pl.BlockSpec(m.shape, lambda i, s: (0, 0)) for m in messages], shapes,
        [
            pl.BlockSpec((tokens, width), lambda i, s: (i, 0)),
            pl.BlockSpec((tokens, 128), lambda i, s: (i, 0)),
            pl.BlockSpec((tokens, 128), lambda i, s: (0, 0)),
            pl.BlockSpec((8, 128), lambda i, s: (0, 0)),
        ],
        "gather", 1e9, grid=(count,), prefetch=1, hold=hold, after=after)
    return (outs[0], outs[1], outs[2], outs[3][0]), kept


def middle_kernel(x_ref, o_ref, out_ref, gain_ref, query_ref, h_ref, n_ref, c_ref):
    h = x_ref[...].astype(F32) + nn(o_ref[...], out_ref[...])
    h_ref[...] = h
    n_ref[...] = norm(h, gain_ref[...])
    c_ref[...] = nn(n_ref[...], query_ref[...]).astype(BF16) * BF16(0.125)


def back_middle_kernel(dc_ref, query_ref, h_ref, gain_ref, dh_ref, out_ref, dh1_ref, r_ref, do_ref, dgain_ref):
    @pl.when(pl.program_id(0) == 0)
    def _():
        dgain_ref[...] = jnp.zeros_like(dgain_ref)

    back, part = norm_back(h_ref[...], nt(dc_ref[...], query_ref[...]), gain_ref[...])
    dgain_ref[...] += part
    dh1 = dh_ref[...] + back
    dh1_ref[...] = dh1
    r_ref[...] = dh1.astype(BF16)
    do_ref[...] = nt(r_ref[...], out_ref[...]).astype(BF16)


def exit_kernel(dq_ref, query_ref, own_ref, *refs):
    peers = refs[:len(refs) - 7]
    keyvalue_ref, x_ref, gain_ref, dh_ref, dx_ref, dkv_ref, dgain_ref = refs[len(refs) - 7:]

    @pl.when(pl.program_id(0) == 0)
    def _():
        dgain_ref[...] = jnp.zeros_like(dgain_ref)

    sides = [sum((ref[side].astype(F32) for ref in peers), own_ref[side].astype(F32)) for side in range(2)]
    dkv_ref[...] = lanes(sides[0], sides[1]).astype(BF16)
    dn = nt(dq_ref[...], query_ref[...]) + nt(dkv_ref[...], keyvalue_ref[...])
    back, part = norm_back(x_ref[...].astype(F32), dn, gain_ref[...])
    dgain_ref[...] += part
    dx_ref[...] = (dh_ref[...] + back).astype(BF16)


def by_rows(kernel, name, flops, arrays, outs, width, dgain=False, hold=(), after=()):
    tokens = next(x.shape[0] for x, cut in arrays if cut)
    tile = min(256, tokens)
    blocks = pl.BlockSpec((tile, width), lambda i: (i, 0))

    def spec(x, cut):
        if x.ndim == 3:
            return pl.BlockSpec((x.shape[0], tile, x.shape[2]), lambda i: (0, i, 0))
        return blocks if cut else pl.BlockSpec(x.shape, lambda i: (0, 0))

    in_specs = [spec(x, cut) for x, cut in arrays]
    shapes = [jax.ShapeDtypeStruct((tokens, width), kind) for kind in outs]
    specs = [blocks] * len(outs)
    if dgain:
        shapes.append(jax.ShapeDtypeStruct((8, width), F32))
        specs.append(pl.BlockSpec((8, width), lambda i: (0, 0)))
    return call(kernel, tuple(x for x, _ in arrays), in_specs, shapes, specs, name, flops,
                grid=(tokens // tile,), hold=hold, after=after)


def feed_kernel(tile_rows, rest, h1_ref, co_ref, cross_ref, g_ref, gain_ref, gate_ref, up_ref, down_ref,
                out_ref, n_ref, hidden_ref, dgu_ref, dh_ref, low_ref, dco_ref, dgain_ref,
                out_acc, dn_acc, h_acc):
    tokens, width = h1_ref.shape
    count = tokens // tile_rows
    tile = gate_ref.shape[1]
    step = pl.program_id(0)

    def each(body):
        def one(i, carry):
            body(pl.ds(pl.multiple_of(i * tile_rows, tile_rows), tile_rows))
            return carry

        lax.fori_loop(0, count, one, 0)

    @pl.when(step == 0)
    def _():
        def start(at):
            h = h1_ref[at, :] + nn(co_ref[at, :], cross_ref[...])
            h_acc[at, :] = h
            n_ref[at, :] = norm(h, gain_ref[...])
            out_acc[at, :] = jnp.zeros((tile_rows, width), F32)
            dn_acc[at, :] = jnp.zeros((tile_rows, width), F32)

        each(start)
        dgain_ref[...] = jnp.zeros_like(dgain_ref)

    def main(at, tile):
        n = n_ref[at, :]
        gate = nn(n, gate_ref[:, :tile])
        up = nn(n, up_ref[:, :tile])
        dhidden = nt(g_ref[at, :], down_ref[:tile, :])
        square = gate * gate
        bend = jnp.tanh(gate * (GELU_A + GELU_B * square))
        half = 0.5 + 0.5 * bend
        gelu = gate * half
        slope = half + gate * (0.5 - 0.5 * bend * bend) * (GELU_A + 3.0 * GELU_B * square)
        hidden = (gelu * up).astype(BF16)
        dgate = (dhidden * up * slope).astype(BF16)
        dup = (dhidden * gelu).astype(BF16)
        hidden_ref[at, :tile] = hidden
        dgu_ref[at, :tile] = dgate
        dgu_ref[at, tile:2 * tile] = dup
        out_acc[at, :] += nn(hidden, down_ref[:tile, :])
        dn_acc[at, :] += nt(dgate, gate_ref[:, :tile]) + nt(dup, up_ref[:, :tile])

    steps = pl.num_programs(0)
    if rest == tile:
        each(functools.partial(main, tile=tile))
    else:
        pl.when(step < steps - 1)(lambda: each(functools.partial(main, tile=tile)))
        pl.when(step == steps - 1)(lambda: each(functools.partial(main, tile=rest)))

    @pl.when(step == pl.num_programs(0) - 1)
    def _():
        def finish(at):
            h = h_acc[at, :]
            out_ref[at, :] = (h + out_acc[at, :]).astype(BF16)
            back, gain_part = norm_back(h, dn_acc[at, :], gain_ref[...])
            dh = g_ref[at, :].astype(F32) + back
            dh_ref[at, :] = dh
            low_ref[at, :] = dh.astype(BF16)
            dco_ref[at, :] = nt(low_ref[at, :], cross_ref[...]).astype(BF16)
            dgain_ref[...] += gain_part

        each(finish)


def feed_forward(h, co, cross_output, g, gain, feed_gate, feed_up, feed_down, hold=(), after=()):
    tokens, width = h.shape
    hidden = feed_gate.shape[1]
    tile = FEED
    rest = hidden - (hidden - 1) // tile * tile
    whole = pl.BlockSpec((tokens, width), lambda i: (0, 0), pipeline_mode=pl.Buffered(1))
    square = pl.BlockSpec((width, width), lambda i: (0, 0), pipeline_mode=pl.Buffered(1))
    row = pl.BlockSpec((1, width), lambda i: (0, 0))
    low, wide = jax.ShapeDtypeStruct(h.shape, BF16), jax.ShapeDtypeStruct(h.shape, F32)
    return call(
        functools.partial(feed_kernel, min(1024, tokens), rest),
        (h, co, cross_output, g, gain, feed_gate, feed_up, feed_down),
        [
            whole, whole, square, whole, row,
            pl.BlockSpec((width, tile), lambda i: (0, i)),
            pl.BlockSpec((width, tile), lambda i: (0, i)),
            pl.BlockSpec((tile, width), lambda i: (i, 0)),
        ],
        [low, low, jax.ShapeDtypeStruct((tokens, hidden), BF16), jax.ShapeDtypeStruct((tokens, 2 * hidden), BF16),
         wide, low, low, jax.ShapeDtypeStruct((8, width), F32)],
        [whole, whole, pl.BlockSpec((tokens, tile), lambda i: (0, i)), pl.BlockSpec((tokens, 2 * tile), lambda i: (0, i)),
         whole, whole, whole, pl.BlockSpec((8, width), lambda i: (0, 0))],
        "feed_forward", 45e9, grid=(pl.cdiv(hidden, tile),), hold=hold, after=after,
        scratch=[pltpu.VMEM((tokens, width), F32) for _ in range(3)],
    )


class Group:
    def __init__(self):
        self.S, self.R = lax.axis_size("seq"), lax.axis_size("row")
        self.s, self.r = lax.axis_index("seq"), lax.axis_index("row")
        self.core = self.r % 2
        self.chunks = self.S
        self.members = self.S // 2
        self.member = (self.s // 4) * 2 + self.core
        self.first_half = self.s < self.S // 2
        self.places = [(s, r) for s in range(self.S) for r in range(self.R)]

    def index(self, s, r):
        return s * self.R + r

    def send(self, x, target):
        pairs = [(self.index(s, r), self.index(*target(s, r))) for s, r in self.places]
        return lax.ppermute(x, ("seq", "row"), pairs)

    def route(self, way):
        S = self.S

        def target(s, r):
            second = (s >= S // 2) if way == 0 else (s < S // 2)
            row = 2 * (r % 2) + (1 if second else 0)
            member = min(s, S - 1 - s)
            return (row + 4 * (member // 2), r - r % 2 + member % 2)

        return [(self.index(s, r), self.index(*target(s, r))) for s, r in self.places]

    def part(self, x, way):
        return jnp.where(self.first_half == (way == 0), x[0], x[1])

    def go(self, x, way):
        return lax.ppermute(x, ("seq", "row"), self.route(way))

    def back(self, x, way):
        return lax.ppermute(x, ("seq", "row"), [(t, f) for f, t in self.route(way)])

    def two_rows(self, a, b):
        return jnp.where(self.first_half, a, b), jnp.where(self.first_half, b, a)

    def peer(self, x, distance):
        return self.send(x, lambda s, r: (s ^ (4 * (distance >> 1)), r ^ (distance & 1)))

    def peers(self, x):
        return [x] + [self.peer(x, p) for p in range(1, self.members)]

    def core_swap(self, x):
        return self.send(x, lambda s, r: (s, r ^ 1))

    def sum_axes(self):
        sizes = [("row", self.R), ("seq", self.S)]
        return [(axis, bit) for axis, size in sizes for bit in range(size.bit_length() - 1)]

    def names(self):
        top = self.S.bit_length() - 2
        row_bits = list(range(1, self.R.bit_length() - 1))
        return [("seq", k) for k in reversed(range(top))] + [("row", k) for k in reversed(row_bits)] + [("row", 0)]

    def bits(self):
        values = [((self.s if kind == "seq" else self.r) >> bit) & 1 for kind, bit in self.names()[:-1]]
        return jnp.stack(values + [self.s >> (self.S.bit_length() - 2)]).astype(jnp.int32)

    def swap(self, give, name):
        size = self.S if name[0] == "seq" else self.R
        return lax.ppermute(give, name[0], [(i, i ^ (1 << name[1])) for i in range(size)])

    def last_sends(self, straight, crossed):
        half = self.S // 2
        one = self.send(straight, lambda s, r: ((r % 2) * half + s % half, (r - r % 2) + s // half))
        two = self.send(crossed, lambda s, r: ((r % 2) * half + s % half, (r - r % 2) + 1 - s // half))
        return one, two


def grad_kernel(jobs, blocks, rows_in, half_ref, *refs):
    out_ref = refs[2 * len(jobs)]
    step = pl.program_id(0)
    rows_out = -(-rows_in // 16) * 16

    def one(left_ref, right_ref, count, paired):
        total = tn(left_ref[...], right_ref[:, :count * CHUNK])
        for chunk in range(count):
            block = total[:, chunk * CHUNK:(chunk + 1) * CHUNK].reshape(blocks, rows_in, CHUNK)
            if paired:
                block = block.reshape(-1, 2, 2, 64 // rows_in, rows_in, CHUNK)
                block = jnp.swapaxes(block, 1, 2).reshape(blocks, rows_in, CHUNK)
            if rows_out > rows_in:
                block = jnp.concatenate([block, jnp.zeros((blocks, rows_out - rows_in, CHUNK), F32)], axis=1)
            out_ref[:, chunk * rows_out:(chunk + 1) * rows_out, :] = block.astype(BF16)

    for k, (start, full, rest, paired) in enumerate(jobs):
        if full:
            run = functools.partial(one, refs[2 * k], refs[2 * k + 1], 2, paired)
            pl.when((step >= start) & (step < start + full))(run)
        if rest:
            run = functools.partial(one, refs[2 * k], refs[2 * k + 1], 1, paired)
            pl.when(step == start + full)(run)


def grad_part(half, pairs, blocks, rows_in, total, offset=0, before=None, hold=(), after=(), holds=False):
    rows_out = -(-rows_in // 16) * 16
    jobs, inputs, in_specs = [], [half], []
    start = 0
    for left, right, *paired in pairs:
        full, rest = divmod(right.shape[1] // CHUNK, 2)
        steps = full + rest
        tokens, side = left.shape[0], left.shape[1] // 2
        jobs.append((start, full, rest, bool(paired)))
        inputs += [left, right]
        in_specs += [
            pl.BlockSpec((tokens, side), lambda i, h: (0, h[0])),
            pl.BlockSpec((tokens, 2 * CHUNK), lambda i, h, start=start, steps=steps: (0, jnp.clip(i - start, 0, steps - 1))),
        ]
        start += steps
    first = offset // (2 * rows_out)
    kernel, inputs, in_specs, alias = with_before(
        functools.partial(grad_kernel, tuple(jobs), blocks, rows_in), inputs, in_specs, before)
    (out,), kept = call(
        kernel, inputs, in_specs,
        [jax.ShapeDtypeStruct((blocks, total, CHUNK), BF16)],
        [pl.BlockSpec((blocks, 2 * rows_out, CHUNK), lambda i, h: (0, first + i, 0))],
        "weight_grads", 1e9, grid=(start,), prefetch=1, hold=hold, after=after, alias=alias,
    )
    return (out, kept) if holds else out


def stage_kernel(plan, bits_ref, *refs):
    count = max(max(terms) for _, terms, _ in plan) + 1
    for out, terms, at in plan:
        total = sum((refs[t][...].astype(F32) for t in terms[1:]), refs[terms[0]][...].astype(F32))
        refs[count + out][:, at, :] = total.astype(BF16)


class Stream:
    def __init__(self, terms, names, order, rows_in):
        self.terms, self.names, self.order, self.rows_in = terms, names, list(order), rows_in

    def got(self, array, names):
        self.terms.append((array, names, 0))


def stage(group, bits, streams, keep=True, join=False, after=(), hold=()):
    all_names = group.names()
    inputs, in_specs, shapes, out_specs, plan = [bits], [], [], [], []
    grid = 2 ** (len(streams[0].names) - 1)
    lead = 2 if streams[0].order[0] != all_names[-1] and grid > 1 else 1
    for number, stream in enumerate(streams):
        axis = stream.order[0]
        rest = [name for name in stream.names if name != axis]

        def spec(names, part, give, rest=rest, axis=axis, rows_in=stream.rows_in):
            def place(i, b):
                index = 0
                for name in names if lead == 1 else names[:-1]:
                    own = b[all_names.index(name)]
                    if name == axis:
                        value = 1 - own if give else own
                    elif name in rest:
                        value = (i * lead >> (len(rest) - 1 - rest.index(name))) & 1
                    else:
                        value = own
                    index = index * 2 + value
                return (index, part, 0)

            return pl.BlockSpec((lead, rows_in, CHUNK), place)

        sides = (True, False) if keep else (True,)
        for give in sides:
            terms = []
            for array, names, part in stream.terms:
                terms.append(len(inputs) - 1)
                inputs.append(array)
                in_specs.append(spec(names, part, give))
            count = stream.rows_in
            if join:
                plan.append((0 if give else 1, tuple(terms), slice(number * count, (number + 1) * count)))
            else:
                plan.append((len(shapes), tuple(terms), slice(0, count)))
            if not join or number == 0:
                full = count * (len(streams) if join else 1)
                shapes.append(jax.ShapeDtypeStruct((grid, full, CHUNK), BF16))
                out_specs.append(pl.BlockSpec((lead, full, CHUNK), lambda i, b: (i, 0, 0)))
    return call(functools.partial(stage_kernel, tuple(plan)), tuple(inputs), in_specs, shapes, out_specs, "stage", 1e9,
                grid=(grid // lead,), prefetch=1, after=after, hold=hold)


class Bundle:
    def __init__(self, group, bits):
        self.group, self.bits = group, bits

    def swap(self, theirs):
        self.other = self.group.core_swap(theirs)

    def begin(self, mine, after=(), hold=()):
        names = self.group.names()
        rows_axes = [name for name in names if name[0] == "row" and name[1]]
        seq_axes = [name for name in names if name[0] == "seq"][::-1]
        half = mine.shape[1] // 2
        self.streams = [
            Stream([(mine, names, n), (self.other, names, n)], names, (rows_axes[::-1], rows_axes)[n] + seq_axes + [("row", 0)], half)
            for n in range(2)
        ]
        self.gives, kept = stage(self.group, self.bits, self.streams, keep=False, after=after, hold=hold)
        self.send()
        return kept

    def send(self):
        self.fly = [self.group.swap(give, s.order[0]) for give, s in zip(self.gives, self.streams)]

    def step(self, after=(), hold=()):
        if not self.streams[0].order[1:]:
            return list(hold)
        for stream, got in zip(self.streams, self.fly):
            axis = stream.order.pop(0)
            stream.names = [name for name in stream.names if name != axis]
            stream.got(got, list(stream.names))
        one = self.streams[0]
        join = len(self.streams) == 2 and one.names == self.streams[1].names and one.order == self.streams[1].order
        outs, kept = stage(self.group, self.bits, self.streams, join=join, after=after, hold=hold)
        axis = one.order[0]
        if join:
            self.streams = [Stream([], list(one.names), one.order, 2 * one.rows_in)]
        if axis == ("row", 0):
            crossed, straight = outs
            self.gives = [crossed]
            self.ends = self.group.last_sends(straight, crossed)
            return kept
        self.gives = []
        for n, stream in enumerate(self.streams):
            self.gives.append(outs[2 * n])
            rest = [name for name in stream.names if name != stream.order[0]]
            stream.terms = [(outs[2 * n + 1], rest, 0)]
        self.send()
        return kept

    def finish(self):
        while self.streams[0].order[1:]:
            self.step()

    def result(self):
        return self.ends[0][0].astype(F32) + self.ends[1][0].astype(F32)


def by_pairs(weight, axis):
    shape = weight.shape
    split = shape[:axis] + (shape[axis] // 256, 2, 2, 64) + shape[axis + 1:]
    return jnp.swapaxes(weight.reshape(split), axis + 1, axis + 2).reshape(shape)


def bias_rows(bias_table, sub):
    table = by_heads((bias_table - bias_table[BUCKETS - 1:]).T)
    levels = np.array([bucket_level(d) for d in range(2 * NEAR)])
    values = jnp.dot(table, jnp.asarray(np.eye(BUCKETS, dtype=np.float32)[levels].T), precision=HIGHEST)
    near = values[:, :sub] if sub <= 2 * NEAR else jnp.pad(values, ((0, 0), (0, sub - 2 * NEAR)))
    near = jnp.concatenate([near, jnp.full((HEADS, sub), MASK, F32)], axis=1)
    corner = jnp.concatenate([values[:, NEAR:], jnp.zeros((HEADS, 1), F32), values[:, 1:NEAR]], axis=1)
    return [jnp.broadcast_to(a[:, None], (HEADS, 8, a.shape[1])) for a in (near, corner)]


def by_heads(x):
    return jnp.swapaxes(x.reshape((4, 2, 2) + x.shape[1:]), 1, 2).reshape(x.shape)


def bias_table_sums(near, corner):
    def fold(wide, distances):
        matrix = np.zeros((8, wide, BUCKETS), np.float32)
        for row in range(8):
            for lane in range(wide):
                distance = distances((lane - row) % wide)
                if distance is not None:
                    matrix[row, lane, bucket_level(distance)] = 1.0
        return jnp.asarray(matrix.reshape(8 * wide, BUCKETS))

    sub = near.shape[2] // 2
    first = fold(2 * sub, lambda d: d if d < sub else None)
    second = fold(2 * NEAR, lambda d: NEAR + d if d < NEAR else (d - NEAR if d > NEAR else None))
    total = jnp.dot(near.reshape(HEADS, -1), first, precision=HIGHEST)
    total = total + jnp.dot(corner.reshape(HEADS, -1), second, precision=HIGHEST)
    rest = -jnp.sum(total[:, :BUCKETS - 1], axis=1, keepdims=True)
    return by_heads(jnp.concatenate([total[:, :BUCKETS - 1], rest], axis=1)).T


def on_device(tokens, segment_ids, memory, cotangent, gain_attend, gain_cross, gain_feed, bias_table,
              self_query, self_keyvalue, self_output, cross_query, cross_keyvalue, cross_output,
              feed_gate, feed_up, feed_down):
    group = Group()
    size, width = tokens.shape[1:]
    span = memory.shape[1]
    hidden_width = feed_gate.shape[1]
    chunks = group.chunks
    sub = min(256, size)
    bits = group.bits()
    core = group.core.astype(jnp.int32)[None]
    devices = group.S * group.R
    blocks = devices // 2

    def token_part(way):
        numbers = group.part(segment_ids, way).astype(BF16)
        numbers = jnp.pad(numbers[None], ((0, PAD - 1), (0, width - size)))
        return jnp.concatenate([group.part(tokens, way), numbers], axis=0)

    way_a = group.go(token_part(0), 0)
    way_b = group.go(token_part(1), 1)

    memory_rows = memory.reshape(-1, width)
    pairs = nn(memory_rows, cross_keyvalue).astype(BF16).reshape(2, span, width)
    own_query, own_output = by_pairs(self_query, 1), by_pairs(self_output, 0)
    other_query, other_output = by_pairs(cross_query, 1), by_pairs(cross_output, 0)
    near, near_back, corner, corner_back = bias_tiles(*bias_rows(bias_table, sub), sub)
    second = [jnp.concatenate([group.part(cotangent, way), group.part(pairs, way)], axis=0) for way in range(2)]

    (x, n1, message), (second_a,) = entry(
        way_a, way_b, gain_attend[None], self_keyvalue, hold=[second[0]],
        after=[own_query, own_output, other_query, other_output, near, second[1]])
    messages = group.peers(message)
    second_a = group.go(second_a, 0)
    second_b = group.go(second[1], 1)
    (q,), _ = by_rows(query_kernel, "query", 2e9, [(n1, True), (own_query, False)], [BF16], width)
    (kv, key_marks, query_marks, meta), _ = gather(
        (2 * group.member + group.s % 2).astype(jnp.int32)[None], messages, after=[q])
    (o, lse), _ = self_forward(meta, q, kv, query_marks, key_marks, near, corner, chunks, 0, 1, None)
    memory_own, g = unpack(second_a, second_b, size, [o])
    memories = group.peers(memory_own)
    (h1, n2, c), _ = by_rows(
        middle_kernel, "middle", 5e9,
        [(x, True), (o, True), (own_output, False), (gain_cross[None], False), (other_query, False)],
        [F32, BF16, BF16], width, after=[memory_own])
    (co, cross_lse), _ = cross_forward(c, memories)
    (out, n3, hidden, dgu, dh2, r2, dco, dgain_feed), _ = feed_forward(
        h1, co, other_output, g, gain_feed[None], feed_gate, feed_up, feed_down)

    feed_rows = hidden.shape[1] // devices
    if feed_rows % 8:
        padded = -(-feed_rows // 16) * 16
        hidden = jnp.pad(hidden.reshape(-1, devices, feed_rows), ((0, 0), (0, 0), (0, padded - feed_rows)))
        hidden = hidden.reshape(-1, devices * padded)
    down_rows = hidden.shape[1] // devices
    down_out = -(-down_rows // 16) * 16
    square_rows = width // devices
    square_out = -(-square_rows // 16) * 16
    down_total = down_out * (width // CHUNK)
    feed_total = -(-(down_total + square_out * (dgu.shape[1] // CHUNK)) // 32) * 32

    def feed_half(which, after=(), hold=()):
        base = grad_part(which, [(hidden, g)], blocks, down_rows, feed_total, after=after)
        return grad_part(which, [(n3, dgu)], blocks, square_rows, feed_total, down_total, [base], hold=hold, holds=True)

    out_a, out_b = out[:size], out[size:]
    theirs, (out_b,) = feed_half(1 - core, after=[out_a], hold=[out_b])
    out_a = group.back(out_a, 0)
    feed = Bundle(group, bits)
    feed.swap(theirs)
    mine, (out_b,) = feed_half(core, after=[theirs], hold=[out_b])
    out_a, = feed.begin(mine, hold=[out_a])
    out_b = group.back(out_b, 1)

    (dc, dm, *dm_peers), _ = cross_backward(c, dco, co, cross_lse, memories, after=feed.gives)
    (dh1, r1, do, dgain_cross), _ = by_rows(
        back_middle_kernel, "back_middle", 5e9,
        [(dc, True), (other_query, False), (h1, True), (gain_cross[None], False), (dh2, True), (own_output, False)],
        [F32, BF16, BF16], width, dgain=True)
    cross_pairs = [(co, r2, True), (n2, dc), (o, r1, True)]
    cross_total = 3 * square_out * (width // CHUNK)
    theirs, (out_b, *dm_peers) = grad_part(
        1 - core, cross_pairs, blocks, square_rows, cross_total, hold=[out_b] + dm_peers, holds=True)
    theirs, = feed.step(hold=[theirs], after=[out_b])
    cross = Bundle(group, bits)
    cross.swap(theirs)
    dm_peers = [group.peer(term, p + 1) for p, term in enumerate(dm_peers)]
    mine, (dm,) = grad_part(
        core, cross_pairs, blocks, square_rows, cross_total, after=[theirs] + feed.gives, hold=[dm], holds=True)
    dm_a, dm_b, _ = add_memory([dm] + dm_peers)

    def backward(part, before, after, hold=()):
        return self_backward(meta, q, do, o, lse, kv, query_marks, key_marks, near_back, corner_back, chunks,
                             part, 4, before, after=after, hold=hold)

    back, (dm_b, mine) = backward(0, None, [dm_a, cross.other], [dm_b, mine])
    dm_a = group.back(dm_a, 0)
    dm_a, = feed.step(after=[back[0], mine], hold=[dm_a])
    cross.begin(mine, after=feed.gives)
    back, (dm_b,) = backward(1, back, feed.gives + cross.gives, [dm_b])
    feed.step(after=[back[0]])
    cross.step(after=[back[0]] + feed.gives)
    back, (dm_b,) = backward(2, back, feed.gives + cross.gives, [dm_b])
    feed.finish()
    cross.step(after=[back[0]] + list(feed.ends))
    dm_b = group.back(dm_b, 1)
    back, _ = backward(3, back, cross.gives)
    dq, dkv_own, dkv_peers, near_sum, corner_sum = back
    dm_b, dkv_peers = cross.step(after=[dq], hold=[dm_b, dkv_peers])
    cross.finish()
    dkv_peers = [group.peer(dkv_peers[p - 1], p) for p in range(1, group.members)]
    dm = rows(*group.two_rows(dm_a, dm_b))
    own_total = 3 * square_out * (width // CHUNK)
    step = square_out * (width // CHUNK)
    theirs = grad_part(1 - core, [(n1, dq), (memory_rows, dm)], blocks, square_rows, own_total, after=cross.gives)
    (tokens_grad, dkv, dgain_attend), (theirs,) = by_rows(
        exit_kernel, "exit", 5e9,
        [(dq, True), (own_query, False), (dkv_own, True)] + [(y, True) for y in dkv_peers]
        + [(self_keyvalue, False), (x, True), (gain_attend[None], False), (dh1, True)],
        [BF16, BF16], width, dgain=True, hold=[theirs])
    token_a, token_b = tokens_grad[:size], tokens_grad[size:]
    theirs, (token_b,) = grad_part(1 - core, [(n1, dkv)], blocks, square_rows, own_total, 2 * step, [theirs],
                                   after=[token_a], hold=[token_b], holds=True)
    token_a = group.back(token_a, 0)
    own = Bundle(group, bits)
    own.swap(theirs)
    mine, (out_a, out_b, *ends) = grad_part(
        core, [(n1, dq), (memory_rows, dm), (n1, dkv)], blocks, square_rows, own_total, after=[theirs],
        hold=[out_a, out_b, near_sum, dgain_attend, dm] + list(feed.ends) + list(cross.ends), holds=True)
    near_sum, dgain_attend, dm_late, *ends = ends
    feed.ends, cross.ends = ends[:2], ends[2:]
    dbias = bias_table_sums(near_sum, corner_sum)
    small = jnp.stack([jnp.sum(dgain_attend, axis=0), jnp.sum(dgain_cross, axis=0), jnp.sum(dgain_feed, axis=0),
                       jnp.pad(dbias.reshape(-1), (0, width - dbias.size))])
    sum_axes = group.sum_axes()

    def small_step(x):
        return x + group.swap(x, sum_axes.pop(0))

    small = small_step(small)
    layer_output = jnp.stack(group.two_rows(out_a, out_b))
    memory_grad = nt(dm_late, cross_keyvalue).astype(BF16).reshape(memory.shape)
    token_b, token_a, small, *ends = own.begin(
        mine, after=[layer_output, memory_grad], hold=[token_b, token_a, small] + list(feed.ends) + list(cross.ends))
    feed.ends, cross.ends = ends[:2], ends[2:]
    token_b = group.back(token_b, 1)
    small = small_step(small)

    def squares(bundle, start, columns):
        rest = bundle[start:start + square_out * (columns // CHUNK)].reshape(columns // CHUNK, square_out, CHUNK)
        return jnp.swapaxes(rest[:, :square_rows], 0, 1).reshape(square_rows, columns)

    feed_sum, cross_sum = feed.result(), cross.result()
    grad_cross = [squares(cross_sum, n * step, width) for n in range(3)]
    grad_cross[1] = by_pairs(grad_cross[1], 1)
    grad_dgu = squares(feed_sum, down_total, dgu.shape[1])
    whole = hidden_width // FEED * FEED
    grad_dgu, grad_rest = grad_dgu[:, :2 * whole].reshape(square_rows, -1, 2, FEED), grad_dgu[:, 2 * whole:]
    grad_rest = grad_rest.reshape(square_rows, 2, hidden_width - whole)
    grad_gate, grad_up = [
        jnp.concatenate([grad_dgu[:, :, n].reshape(square_rows, -1), grad_rest[:, n]], axis=1) for n in range(2)]
    grad_down = feed_sum[:down_total].reshape(width // CHUNK, down_out, CHUNK)[:, :feed_rows]
    grad_down = jnp.swapaxes(grad_down, 0, 1).reshape(feed_rows, width)

    token_a, token_b, small = own.step(hold=[token_a, token_b, small], after=grad_cross + [grad_gate, grad_up, grad_down])
    small = small_step(small)
    tokens_grad = jnp.stack(group.two_rows(token_a, token_b))
    small, = own.step(hold=[small], after=[tokens_grad])
    small = small_step(small)
    small, = own.step(hold=[small])
    own.finish()
    while sum_axes:
        small = small_step(small)
    own_sum = own.result()
    grad_own = [squares(own_sum, n * step, width) for n in (0, 2, 1)]

    return (
        layer_output,
        tokens_grad,
        memory_grad,
        by_pairs(grad_own[0], 1),
        grad_own[1],
        grad_cross[2],
        grad_cross[1],
        grad_own[2],
        grad_cross[0],
        grad_gate,
        grad_up,
        grad_down,
        small[0],
        small[1],
        small[2],
        small[3, :dbias.size].reshape(dbias.shape),
    )


def solution(mesh):
    data, whole, grads = P("row", "seq", None), P(), P(("seq", "row"), None)
    in_specs = (data, P("row", "seq"), data, data) + (whole,) * 13
    out_specs = (data,) * 3 + (grads,) * 9 + (whole,) * 4
    return jax.shard_map(on_device, mesh=mesh, in_specs=in_specs, out_specs=out_specs, check_vma=False)
```

```python
import functools
import math

import jax
import jax.numpy as jnp
import numpy as np
from jax import lax
from jax.experimental import pallas as pl
from jax.experimental.pallas import tpu as pltpu
from jax.sharding import PartitionSpec as P

HEADS = 16
BUCKETS = 32
MAX_DIST = 128
HIGHEST = lax.Precision.HIGHEST
F32, BF16 = jnp.float32, jnp.bfloat16
MASK = -float(2.0**100)
NEAR = 128
VMEM = 56 * 1024 * 1024
CHUNK = 512
PAD = 16
SELF_SPLIT = 1
SELF_AHEAD = 1
EAGER = True
AHEAD = 3
SPLIT = 2
BACK_SPLIT = 1
FEED = 512
COST = {
    "entry": 6, "query": 6, "gather": 5, "self_forward": 23, "middle": 9, "cross_forward": 20, "feed_forward": 70,
    "weight_grads": 9, "stage": 4, "cross_backward": 31, "back_middle": 12, "self_backward": 18, "exit": 11,
}
COST_SCALE = 0.001e9
GELU_A = math.sqrt(2.0 / math.pi)
GELU_B = GELU_A * 0.044715


def bucket_level(distance):
    exact_part = BUCKETS // 2
    if distance < exact_part:
        return distance
    which_bucket = exact_part + math.floor(
        math.log(distance / exact_part) / math.log(MAX_DIST / exact_part) * (BUCKETS - exact_part)
    )
    return min(BUCKETS - 1, which_bucket)


def call(kernel, inputs, in_specs, out_shape, out_specs, name, flops, grid=(), scratch=(), prefetch=0,
         hold=(), after=(), alias=None):
    hold, after = list(hold), list(after)
    count_in, count_out = len(inputs), len(out_shape)
    anywhere = pl.BlockSpec(memory_space=pl.ANY)

    def body(*refs):
        kept = count_in + len(hold) + len(after)
        kernel(*refs[:count_in], *refs[kept:kept + count_out], *refs[kept + count_out + len(hold):])

    aliases = {count_in + i: count_out + i for i in range(len(hold))}
    aliases.update(alias or {})
    outs = pl.pallas_call(
        body,
        grid_spec=pltpu.PrefetchScalarGridSpec(
            num_scalar_prefetch=prefetch,
            grid=grid,
            in_specs=list(in_specs) + [anywhere] * (len(hold) + len(after)),
            out_specs=list(out_specs) + [anywhere] * len(hold),
            scratch_shapes=list(scratch),
        ),
        out_shape=list(out_shape) + [jax.ShapeDtypeStruct(x.shape, x.dtype) for x in hold],
        input_output_aliases=aliases,
        compiler_params=pltpu.CompilerParams(vmem_limit_bytes=VMEM),
        cost_estimate=pl.CostEstimate(flops=int(COST.get(name, 5) * COST_SCALE), bytes_accessed=10**4, transcendentals=0),
        name=name,
    )(*inputs, *hold, *after)
    return list(outs[:count_out]), list(outs[count_out:])


def nt(a, b):
    return lax.dot_general(a, b, (((1,), (1,)), ((), ())), preferred_element_type=F32)


def nn(a, b):
    return jnp.dot(a, b, preferred_element_type=F32)


def tn(a, b):
    return lax.dot_general(a, b, (((0,), (0,)), ((), ())), preferred_element_type=F32)


def halves(block):
    low = lax.broadcasted_iota(jnp.int32, block.shape, 1) < 64
    zero = jnp.zeros_like(block)
    return jnp.where(low, block, zero), jnp.where(low, zero, block)


def lanes(a, b):
    return jnp.concatenate([a, b], axis=1)


def rows(a, b):
    return jnp.concatenate([a, b], axis=0)


def chunk_of(member, part, chunks):
    high = jnp.bitwise_xor(part, member % 2)
    return jnp.where(high == 0, member // 2, chunks - 1 - member // 2)


def slot_of(member, chunk, chunks):
    high = (chunk >= chunks // 2).astype(jnp.int32)
    other = jnp.where(chunk >= chunks // 2, chunks - 1 - chunk, chunk)
    return 2 * jnp.bitwise_xor(other, member // 2) + jnp.bitwise_xor(high, member % 2)


def first_block(meta, member, chunk, chunks):
    mine = meta[1 + slot_of(member, chunk, chunks)]

    def skip(block, start):
        last = meta[1 + chunks + slot_of(member, block, chunks)]
        return start + jnp.where((block < chunk) & (last < mine), 1, 0)

    return lax.fori_loop(0, chunks, skip, jnp.int32(0))


def in_turn(count, ahead, issue, process):
    waiting = [issue(i) for i in range(min(ahead, count))]
    for i in range(count):
        if i + ahead < count:
            waiting.append(issue(i + ahead))
        process(i, waiting.pop(0))


def self_forward_kernel(chunks, sub, meta, q_ref, k_ref, v_ref, qf_ref, kf_ref, near_ref, corner_ref,
                        o_ref, lse_ref, acc_ref, m_ref):
    size = q_ref.shape[0]
    member = meta[0]
    chunk = chunk_of(member, pl.program_id(1), chunks)
    q_both = [lanes(part, qf_ref[...]) for part in halves(q_ref[...])]

    def values(at, length):
        low, high = halves(v_ref[pl.ds(at, length), :])
        one_low, one_high = halves(jnp.ones((length, 128), BF16))
        return rows(lanes(low, one_low), lanes(high, one_high))

    own = pl.multiple_of(slot_of(member, chunk, chunks) * size, size)
    chains = [(strip, head) for strip in range(size // sub) for head in range(2)]
    weights = {}

    def near_issue(i):
        strip, head = chains[i]
        span = (strip + 1) * sub
        return nt(q_both[head][strip * sub:span], lanes(k_ref[pl.ds(own, span), :], kf_ref[pl.ds(own, span), :]))

    def near_process(i, s):
        strip, head = chains[i]
        span = (strip + 1) * sub
        here = slice(strip * sub, span)
        last = s[:, span - sub:] + near_ref[head]
        if strip:
            edge = s[:, span - sub - NEAR:span - sub]
            edge = rows(edge[:NEAR] + corner_ref[head], edge[NEAR:])
            s = jnp.concatenate([s[:, :span - sub - NEAR], edge, last], axis=1)
        else:
            s = last
        top = jnp.max(s, axis=1, keepdims=True)
        m_ref[head, here, :] = jnp.broadcast_to(top, (sub, 128))
        weights[head] = jnp.exp(s - top).astype(BF16)
        if head:
            acc_ref[here, :] = nn(lanes(weights[0], weights[1]), values(own, span))

    in_turn(len(chains), AHEAD, near_issue, near_process)

    def far(block, carry):
        at = pl.multiple_of(slot_of(member, block, chunks) * size, size)
        keys = lanes(k_ref[pl.ds(at, size), :], kf_ref[pl.ds(at, size), :])
        vals = values(at, size)
        flag = jnp.where(block == chunk - 1, 1.0, 0.0).astype(F32)
        part = size // SPLIT
        chains = [(piece, head) for piece in range(SPLIT) for head in range(2)]
        weights, scales = {}, {}

        def issue(i):
            piece, head = chains[i]
            return nt(q_both[head][piece * part:(piece + 1) * part], keys)

        def process(i, s):
            piece, head = chains[i]
            here = slice(piece * part, (piece + 1) * part)
            if piece == 0:
                edge = s[:NEAR, size - NEAR:] + corner_ref[head] * flag
                edge = lanes(s[:NEAR, :size - NEAR], edge)
                s = rows(edge, s[NEAR:]) if part > NEAR else edge
            old = m_ref[head, here, :]
            top = jnp.maximum(old, jnp.max(s, axis=1, keepdims=True))
            scales[head] = jnp.exp(old - top)
            m_ref[head, here, :] = top
            weights[head] = jnp.exp(s - top[:, :1]).astype(BF16)
            if head:
                low = lax.broadcasted_iota(jnp.int32, (part, 128), 1) < 64
                scale = jnp.where(low, scales[0], scales[1])
                acc_ref[here, :] = acc_ref[here, :] * lanes(scale, scale) + nn(lanes(weights[0], weights[1]), vals)

        in_turn(len(chains), AHEAD, issue, process)
        return carry

    lax.fori_loop(first_block(meta, member, chunk, chunks), chunk, far, 0)
    low = lax.broadcasted_iota(jnp.int32, (size, 128), 1) < 64
    total = acc_ref[:, 128:]
    o_ref[...] = (acc_ref[:, :128] / total).astype(BF16)
    lse_ref[...] = jnp.where(low, m_ref[0], m_ref[1]) + jnp.log(total)


def pieces(column, shape):
    lane = lax.broadcasted_iota(jnp.int32, shape, 1)
    high = column.astype(BF16).astype(F32)
    rest = column - high
    middle = rest.astype(BF16).astype(F32)
    low = rest - middle
    full = jnp.where(lane == 4, high, jnp.where(lane == 5, middle, jnp.where(lane == 6, low, 0.0)))
    return full.astype(BF16)


def back_operands(q_ref, do_ref, o_ref, lse_ref, qf):
    shape = q_ref.shape
    q_both = halves(q_ref[...])
    do_both = halves(do_ref[...])
    product = do_ref[...].astype(F32) * o_ref[...].astype(F32)
    low = lax.broadcasted_iota(jnp.int32, shape, 1) < 64
    deltas = [jnp.sum(jnp.where(low, product, 0.0), axis=1, keepdims=True),
              jnp.sum(jnp.where(low, 0.0, product), axis=1, keepdims=True)]
    logs = [lse_ref[:, 0:1], lse_ref[:, 64:65]]
    extra = [pieces(log, shape) for log in logs]
    if qf is not None:
        extra = [part + qf for part in extra]
    q_wide = [lanes(part, more) for part, more in zip(q_both, extra)]
    do_wide = [lanes(part, pieces(delta, shape)) for part, delta in zip(do_both, deltas)]
    return q_both, do_both, q_wide, do_wide


def diagonal_sums(block):
    count, wide = block.shape[0], 2 * block.shape[1]
    block = lanes(block, jnp.zeros_like(block))
    while count > 8:
        count = count // 2
        block = block[:count] + pltpu.roll(block[count:], wide - count, 1)
    return block


def self_backward_kernel(chunks, sub, meta, q_ref, do_ref, o_ref, lse_ref, k_ref, v_ref, qf_ref, kf_ref,
                         near_ref, corner_ref, dq_ref, own_ref, peer_ref, near_out, corner_out,
                         dq_acc, dk_acc, dv_acc, near_acc, corner_acc):
    size = q_ref.shape[0]
    member = meta[0]
    chunk = chunk_of(member, pl.program_id(2), chunks)
    first = (pl.program_id(1) == 0) & (pl.program_id(2) == 0)
    last = (pl.program_id(1) == 1) & (pl.program_id(2) == 1)

    @pl.when(first)
    def _():
        dk_acc[...] = jnp.zeros_like(dk_acc)
        dv_acc[...] = jnp.zeros_like(dv_acc)

    @pl.when(pl.program_id(2) == 0)
    def _():
        near_acc[...] = jnp.zeros_like(near_acc)
        corner_acc[...] = jnp.zeros_like(corner_acc)

    q_both, do_both, q_wide, do_wide = back_operands(q_ref, do_ref, o_ref, lse_ref, qf_ref[...])
    own = pl.multiple_of(slot_of(member, chunk, chunks) * size, size)
    dq_acc[...] = jnp.zeros_like(dq_acc)

    def add(at, length, here, weights, grads, keys):
        dv_acc[pl.ds(at, length), :] += nn(lanes(*weights), rows(do_both[0][here], do_both[1][here]))
        dk_acc[pl.ds(at, length), :] += nn(lanes(*grads), rows(q_both[0][here], q_both[1][here]))
        dq_acc[here, :] += tn(rows(*grads), rows(*halves(keys)))

    for strip in range(size // sub):
        at = pl.multiple_of(own + strip * sub, sub)
        here = slice(strip * sub, size)
        k, v, kf = (ref[pl.ds(at, sub), :] for ref in (k_ref, v_ref, kf_ref))
        keys, vals = lanes(k, kf), lanes(v, kf)
        weights, grads = [], []
        for head in range(2):
            s = nt(keys, q_wide[head][here])
            dp = nt(vals, do_wide[head][here])
            block = s[:, :sub] + near_ref[head]
            more = (strip + 1) * sub < size
            if more:
                edge = s[sub - NEAR:, sub:sub + NEAR] + corner_ref[head]
                rest = s[:, sub:]
                rest = rows(rest[:sub - NEAR], lanes(edge, rest[sub - NEAR:, NEAR:]))
                s = lanes(block, rest)
            else:
                s = block
            p = jnp.exp(s)
            ds = p * dp
            near_acc[head] += ds[:, :sub]
            if more:
                corner_acc[head] += ds[sub - NEAR:, sub:sub + NEAR]
            weights.append(p.astype(BF16))
            grads.append(ds.astype(BF16))
        add(at, sub, here, weights, grads, k)

    def far(block, carry):
        at = pl.multiple_of(slot_of(member, block, chunks) * size, size)
        k, v, kf = (ref[pl.ds(at, size), :] for ref in (k_ref, v_ref, kf_ref))
        keys, vals = lanes(k, kf), lanes(v, kf)
        flag = jnp.where(block == chunk - 1, 1.0, 0.0).astype(F32)
        part = size // SELF_SPLIT
        chains = [(piece, head) for piece in range(SELF_SPLIT) for head in range(2)]
        weights, grads = {}, {}

        def issue(i):
            piece, head = chains[i]
            here = slice(piece * part, (piece + 1) * part)
            return nt(keys, q_wide[head][here]), nt(vals, do_wide[head][here])

        def process(i, products):
            piece, head = chains[i]
            s, dp = products
            if piece == 0:
                edge = s[size - NEAR:, :NEAR] + corner_ref[head] * flag
                edge = lanes(edge, s[size - NEAR:, NEAR:]) if part > NEAR else edge
                s = rows(s[:size - NEAR], edge)
            p = jnp.exp(s)
            ds = p * dp
            if piece == 0:
                corner_acc[head] += ds[size - NEAR:, :NEAR] * flag
            weights[head] = p.astype(BF16)
            grads[head] = ds.astype(BF16)
            if head and (SELF_SPLIT == 1 or EAGER):
                add(at, size, slice(piece * part, (piece + 1) * part), [weights[0], weights[1]], [grads[0], grads[1]], k)

        in_turn(len(chains), SELF_AHEAD, issue, process)
        return carry

    lax.fori_loop(first_block(meta, member, chunk, chunks), chunk, far, 0)
    dq_ref[...] = (dq_acc[...] * 0.125).astype(BF16)

    @pl.when(last)
    def _():
        for side, acc in enumerate((dk_acc, dv_acc)):
            own_ref[side] = acc[: 2 * size, :].astype(BF16)
            for other in range(peer_ref.shape[0]):
                at = 2 * size * (other + 1)
                peer_ref[other, side] = acc[at:at + 2 * size, :].astype(BF16)

    @pl.when(pl.program_id(2) == 1)
    def _():
        for head in range(2):
            near_out[head] = diagonal_sums(near_acc[head])
            corner_out[head] = diagonal_sums(corner_acc[head])


def with_before(kernel, inputs, in_specs, before):
    if before is None:
        return kernel, tuple(inputs), list(in_specs), None
    count = len(inputs)

    def body(*refs):
        kernel(*refs[:count], *refs[count + len(before):])

    specs = list(in_specs) + [pl.BlockSpec(memory_space=pl.ANY)] * len(before)
    return body, tuple(inputs) + tuple(before), specs, {count + i: i for i in range(len(before))}


def self_forward(meta, q, kv, qf, kf, near, corner, chunks, part, parts, before, hold=(), after=()):
    size = q.shape[0] // 2
    sub = min(256, size)
    length = kv.shape[0]
    blocks = 8 // parts
    shift = blocks * part
    own = pl.BlockSpec((size, 128), lambda b, c, m: (c, b + shift))
    kernel, inputs, in_specs, alias = with_before(
        functools.partial(self_forward_kernel, chunks, sub),
        (meta, q, kv, kv, qf, kf, near, corner),
        [
            own,
            pl.BlockSpec((length, 128), lambda b, c, m: (0, (b + shift) // 2)),
            pl.BlockSpec((length, 128), lambda b, c, m: (0, 4 + (b + shift) // 2)),
            pl.BlockSpec((size, 128), lambda b, c, m: (c, 0)),
            pl.BlockSpec((length, 128), lambda b, c, m: (0, 0)),
            pl.BlockSpec((2, sub, sub), lambda b, c, m: (b + shift, 0, 0)),
            pl.BlockSpec((2, NEAR, NEAR), lambda b, c, m: (b + shift, 0, 0)),
        ], before)
    return call(
        kernel, inputs, in_specs,
        [jax.ShapeDtypeStruct(q.shape, BF16), jax.ShapeDtypeStruct(q.shape, F32)],
        [own, own],
        "self_forward", 4e10 / parts, grid=(blocks, 2), prefetch=1, hold=hold, after=after, alias=alias,
        scratch=[pltpu.VMEM((size, 256), F32), pltpu.VMEM((2, size, 128), F32)],
    )


def self_backward(meta, q, do, o, lse, kv, qf, kf, near, corner, chunks, part, parts, before, hold=(), after=()):
    pairs = 4 // parts
    shift = pairs * part
    size = q.shape[0] // 2
    sub = min(256, size)
    length = kv.shape[0]
    own = pl.BlockSpec((size, 128), lambda g, b, c, m: (c, 2 * (g + shift) + b))
    inputs = [meta, q, do, o, lse, kv, kv, qf, kf, near, corner]
    in_specs = [
        own, own, own, own,
        pl.BlockSpec((length, 128), lambda g, b, c, m: (0, g + shift)),
        pl.BlockSpec((length, 128), lambda g, b, c, m: (0, 4 + g + shift)),
        pl.BlockSpec((size, 128), lambda g, b, c, m: (c, 0)),
        pl.BlockSpec((length, 128), lambda g, b, c, m: (0, 0)),
        pl.BlockSpec((2, sub, sub), lambda g, b, c, m: (2 * (g + shift) + b, 0, 0)),
        pl.BlockSpec((2, NEAR, NEAR), lambda g, b, c, m: (2 * (g + shift) + b, 0, 0)),
    ]
    kernel, inputs, in_specs, alias = with_before(
        functools.partial(self_backward_kernel, chunks, sub), inputs, in_specs, before)
    others = length // (2 * size) - 1
    return call(
        kernel, inputs, in_specs,
        [
            jax.ShapeDtypeStruct(q.shape, BF16),
            jax.ShapeDtypeStruct((2, 2 * size, 512), BF16),
            jax.ShapeDtypeStruct((others, 2, 2 * size, 512), BF16),
            jax.ShapeDtypeStruct((16, 8, 2 * sub), F32),
            jax.ShapeDtypeStruct((16, 8, 2 * NEAR), F32),
        ],
        [
            own,
            pl.BlockSpec((2, 2 * size, 128), lambda g, b, c, m: (0, 0, g + shift)),
            pl.BlockSpec((others, 2, 2 * size, 128), lambda g, b, c, m: (0, 0, 0, g + shift)),
            pl.BlockSpec((2, 8, 2 * sub), lambda g, b, c, m: (2 * (g + shift) + b, 0, 0)),
            pl.BlockSpec((2, 8, 2 * NEAR), lambda g, b, c, m: (2 * (g + shift) + b, 0, 0)),
        ],
        "self_backward", 6e10 / parts, grid=(pairs, 2, 2), prefetch=1, hold=hold, after=after, alias=alias,
        scratch=[
            pltpu.VMEM((size, 128), F32),
            pltpu.VMEM((length, 128), F32),
            pltpu.VMEM((length, 128), F32),
            pltpu.VMEM((2, sub, sub), F32),
            pltpu.VMEM((2, NEAR, NEAR), F32),
        ],
    )


def stacked(refs):
    return refs[0][...] if len(refs) == 1 else jnp.concatenate([ref[...] for ref in refs], axis=0)


def cross_forward_kernel(count, q_ref, *refs):
    keys, v = stacked(refs[:count]), stacked(refs[count:2 * count])
    o_ref, lse_ref = refs[2 * count:]
    length = keys.shape[0]
    low, high = halves(v)
    one_low, one_high = halves(jnp.ones((length, 128), BF16))
    values = rows(lanes(low, one_low), lanes(high, one_high))
    q_both = halves(q_ref[...])
    part = q_ref.shape[0] // SPLIT
    chains = [(piece, head) for piece in range(SPLIT) for head in range(2)]
    weights, tops = {}, {}

    def issue(i):
        piece, head = chains[i]
        return nt(q_both[head][piece * part:(piece + 1) * part], keys)

    def process(i, s):
        piece, head = chains[i]
        tops[head] = jnp.max(s, axis=1, keepdims=True)
        weights[head] = jnp.exp(s - tops[head]).astype(BF16)
        if head:
            here = slice(piece * part, (piece + 1) * part)
            acc = nn(lanes(weights[0], weights[1]), values)
            is_low = lax.broadcasted_iota(jnp.int32, (part, 128), 1) < 64
            total = acc[:, 128:]
            o_ref[here, :] = (acc[:, :128] / total).astype(BF16)
            lse_ref[here, :] = jnp.where(is_low, tops[0], tops[1]) + jnp.log(total)

    in_turn(len(chains), AHEAD, issue, process)


def cross_backward_kernel(count, q_ref, do_ref, o_ref, lse_ref, *refs):
    k, v = stacked(refs[:count]), stacked(refs[count:2 * count])
    dq_ref, dkv_refs, (dk_acc, dv_acc) = refs[2 * count], refs[2 * count + 1:3 * count + 1], refs[3 * count + 1:]
    first = (pl.program_id(1) == 0) & (pl.program_id(2) == 0)
    last = (pl.program_id(1) == 1) & (pl.program_id(2) == 1)

    @pl.when(first)
    def _():
        dk_acc[...] = jnp.zeros_like(dk_acc)
        dv_acc[...] = jnp.zeros_like(dv_acc)

    q_both, do_both, q_wide, do_wide = back_operands(q_ref, do_ref, o_ref, lse_ref, None)
    lane = lax.broadcasted_iota(jnp.int32, k.shape, 1)
    minus = jnp.where((lane >= 4) & (lane < 7), -1.0, 0.0).astype(BF16)
    keys, vals = lanes(k, minus), lanes(v, minus)
    size = q_ref.shape[0] // BACK_SPLIT
    chains = [(piece, head) for piece in range(BACK_SPLIT) for head in range(2)]
    weights, grads = {}, {}

    def issue(i):
        piece, head = chains[i]
        here = slice(piece * size, (piece + 1) * size)
        return nt(keys, q_wide[head][here]), nt(vals, do_wide[head][here])

    def process(i, products):
        head = chains[i][1]
        p = jnp.exp(products[0])
        weights[chains[i]] = p.astype(BF16)
        grads[chains[i]] = (p * products[1]).astype(BF16)

    in_turn(len(chains), AHEAD, issue, process)

    def both(x):
        return jnp.concatenate([x[piece, head] for head in range(2) for piece in range(BACK_SPLIT)], axis=1)

    dv_acc[...] += nn(both(weights), rows(*do_both))
    dk_acc[...] += nn(both(grads), rows(*q_both))
    for piece in range(BACK_SPLIT):
        here = slice(piece * size, (piece + 1) * size)
        dq_ref[here, :] = (tn(rows(grads[piece, 0], grads[piece, 1]), rows(*halves(k))) * 0.125).astype(BF16)

    @pl.when(last)
    def _():
        part = dk_acc.shape[0] // count
        for number, ref in enumerate(dkv_refs):
            at = slice(number * part, (number + 1) * part)
            ref[0] = dk_acc[at, :].astype(BF16)
            ref[1] = dv_acc[at, :].astype(BF16)


def cross_forward(q, memories, hold=(), after=()):
    size, part, count = q.shape[0] // 2, memories[0].shape[0], len(memories)
    own = pl.BlockSpec((size, 128), lambda b, c: (c, b))
    return call(
        functools.partial(cross_forward_kernel, count), (q, *memories, *memories),
        [own] + [pl.BlockSpec((part, 128), lambda b, c: (0, b // 2))] * count
        + [pl.BlockSpec((part, 128), lambda b, c: (0, 4 + b // 2))] * count,
        [jax.ShapeDtypeStruct(q.shape, BF16), jax.ShapeDtypeStruct(q.shape, F32)],
        [own, own],
        "cross_forward", 15e9, grid=(8, 2), hold=hold, after=after,
    )


def cross_backward(q, do, o, lse, memories, hold=(), after=()):
    size, part, count = q.shape[0] // 2, memories[0].shape[0], len(memories)
    own = pl.BlockSpec((size, 128), lambda g, b, c: (c, 2 * g + b))
    return call(
        functools.partial(cross_backward_kernel, count), (q, do, o, lse, *memories, *memories),
        [own, own, own, own] + [pl.BlockSpec((part, 128), lambda g, b, c: (0, g))] * count
        + [pl.BlockSpec((part, 128), lambda g, b, c: (0, 4 + g))] * count,
        [jax.ShapeDtypeStruct(q.shape, BF16)] + [jax.ShapeDtypeStruct((2, part, 512), BF16)] * count,
        [own] + [pl.BlockSpec((2, part, 128), lambda g, b, c: (0, 0, g))] * count,
        "cross_backward", 30e9, grid=(4, 2, 2), hold=hold, after=after,
        scratch=[pltpu.VMEM((part * count, 128), F32), pltpu.VMEM((part * count, 128), F32)],
    )


def add_kernel(*refs):
    terms, outs = refs[:-2], refs[-2:]
    for number, out in enumerate(outs):
        at = slice(number * out.shape[0], (number + 1) * out.shape[0])
        sides = [sum((ref[side, at, :].astype(F32) for ref in terms[1:]), terms[0][side, at, :].astype(F32)) for side in range(2)]
        out[...] = lanes(*sides).astype(BF16)


def add_memory(terms, hold=(), after=()):
    shape = jax.ShapeDtypeStruct((terms[0].shape[1] // 2, 2 * terms[0].shape[2]), BF16)
    (low, high), kept = call(
        add_kernel, tuple(terms), [pl.BlockSpec(x.shape, lambda: (0, 0, 0)) for x in terms],
        [shape] * 2, [pl.BlockSpec(shape.shape, lambda: (0, 0))] * 2, "add_memory", 1e9, hold=hold, after=after)
    return low, high, kept


def bias_kernel(sub, near_ref, corner_ref, near_out, back_out, corner_out, corner_back):
    for head in range(2):
        wide = jnp.broadcast_to(near_ref[head, :1], (sub, 2 * sub))
        block = pltpu.roll(wide, 0, 1, stride=1, stride_axis=0)[:, :sub]
        back_out[head] = block
        near_out[head] = block.T
        wide = jnp.broadcast_to(corner_ref[head, :1], (NEAR, 2 * NEAR))
        block = pltpu.roll(wide, 0, 1, stride=1, stride_axis=0)[:, :NEAR]
        corner_back[head] = block
        corner_out[head] = block.T


def bias_tiles(near, corner, sub):
    def spec(a, b):
        return pl.BlockSpec((2, a, b), lambda h: (h, 0, 0))

    def shape(a):
        return jax.ShapeDtypeStruct((16, a, a), F32)

    return pl.pallas_call(
        functools.partial(bias_kernel, sub),
        grid=(8,),
        in_specs=[spec(8, 2 * sub), spec(8, 2 * NEAR)],
        out_specs=[spec(sub, sub), spec(sub, sub), spec(NEAR, NEAR), spec(NEAR, NEAR)],
        out_shape=[shape(sub), shape(sub), shape(NEAR), shape(NEAR)],
        compiler_params=pltpu.CompilerParams(vmem_limit_bytes=VMEM),
        name="bias_tiles",
    )(near, corner)


def inverse_rms(h):
    return lax.rsqrt(jnp.mean(h * h, axis=1, keepdims=True) + 1e-06)


def norm(values, gain):
    return (values * inverse_rms(values) * gain).astype(BF16)


def norm_back(h, dn, gain):
    scale = inverse_rms(h)
    unit = h * scale
    spread = dn * unit
    share = jnp.mean(spread * gain, axis=1, keepdims=True)
    gain_part = jnp.sum(spread.reshape(-1, 8, spread.shape[1]), axis=0)
    return scale * (dn * gain - unit * share), gain_part


def entry_kernel(a_ref, b_ref, gain_ref, weight_ref, x_ref, n_ref, message_ref):
    tokens = x_ref.shape[0]
    size = tokens // 2
    tile = min(256, size)
    for side, ref in enumerate((a_ref, b_ref)):
        for i in range(size // tile):
            at = slice(side * size + i * tile, side * size + (i + 1) * tile)
            x = ref[i * tile:(i + 1) * tile, :]
            x_ref[at, :] = x
            n_ref[at, :] = norm(x.astype(F32), gain_ref[...])
            message_ref[at, :] = nn(n_ref[at, :], weight_ref[...]).astype(BF16)
        message_ref[tokens + side * PAD:tokens + (side + 1) * PAD, :] = ref[size:, :]


def entry(way_a, way_b, gain, weight, hold=(), after=()):
    tokens, width = 2 * (way_a.shape[0] - PAD), way_a.shape[1]
    inputs = (way_a, way_b, gain, weight)
    shapes = [jax.ShapeDtypeStruct((count, width), BF16) for count in (tokens, tokens, tokens + 2 * PAD)]
    return call(entry_kernel, inputs, [pl.BlockSpec(y.shape, lambda: (0, 0)) for y in inputs], shapes,
                [pl.BlockSpec(s.shape, lambda: (0, 0)) for s in shapes], "entry", 2e9, hold=hold, after=after)


def unpack_kernel(a_ref, b_ref, memory_ref, g_ref):
    span, size = memory_ref.shape[0] // 2, g_ref.shape[0] // 2
    for side, ref in enumerate((a_ref, b_ref)):
        g_ref[side * size:(side + 1) * size, :] = ref[:size, :]
        memory_ref[side * span:(side + 1) * span, :] = ref[size:, :]


def unpack(second_a, second_b, size, after):
    count, width = second_a.shape
    whole = pl.BlockSpec((count, width), lambda: (0, 0))
    shapes = [jax.ShapeDtypeStruct((2 * (count - size), width), BF16), jax.ShapeDtypeStruct((2 * size, width), BF16)]
    outs, _ = call(unpack_kernel, (second_a, second_b), [whole, whole], shapes,
                   [pl.BlockSpec(s.shape, lambda: (0, 0)) for s in shapes], "unpack", 1e9, after=after)
    return outs


def query_kernel(n_ref, weight_ref, q_ref):
    q_ref[...] = nn(n_ref[...], weight_ref[...]).astype(BF16) * BF16(0.125)


def gather_kernel(member_ref, *refs):
    messages = refs[:len(refs) - 4]
    kv_ref, key_ref, query_ref, meta_ref = refs[len(refs) - 4:]
    step = pl.program_id(0)
    tokens = messages[0].shape[0] - 2 * PAD
    size = tokens // 2
    for p, message in enumerate(messages):
        @pl.when(step == p)
        def _(p=p, message=message):
            kv_ref[...] = message[:tokens, :]
            shape = (size, 128)
            lane = lax.broadcasted_iota(jnp.int32, shape, 1)
            place = lax.broadcasted_iota(jnp.int32, (8, 128), 1)
            chunks = 2 * len(messages)
            meta = meta_ref[...]
            if p == 0:
                meta = jnp.where(place == 0, member_ref[0], 0)
            for side in range(2):
                at = tokens + side * PAD
                numbers = message[at:at + PAD, :size].astype(F32)[:1]
                column = jnp.broadcast_to(numbers, (128, size)).T.astype(jnp.int32)
                same = (column == lane) & (lane < 4)
                marks = jnp.where(lane < 4, jnp.where(same, 0.0, MASK), jnp.where(lane < 7, -1.0, 0.0))
                key_ref[side * size:(side + 1) * size, :] = marks.astype(BF16)
                if p == 0:
                    query_ref[side * size:(side + 1) * size, :] = jnp.where(same, 1.0, 0.0).astype(BF16)
                slot = 2 * p + side
                meta = jnp.where(place == 1 + slot, column[:1, :], meta)
                meta = jnp.where(place == 1 + chunks + slot, column[size - 1:, :], meta)
            meta_ref[...] = meta


def gather(member, messages, hold=(), after=()):
    tokens, width = messages[0].shape[0] - 2 * PAD, messages[0].shape[1]
    count = len(messages)
    shapes = [
        jax.ShapeDtypeStruct((count * tokens, width), BF16),
        jax.ShapeDtypeStruct((count * tokens, 128), BF16),
        jax.ShapeDtypeStruct((tokens, 128), BF16),
        jax.ShapeDtypeStruct((8, 128), jnp.int32),
    ]
    outs, kept = call(
        gather_kernel, (member,) + tuple(messages),
        [pl.BlockSpec(m.shape, lambda i, s: (0, 0)) for m in messages], shapes,
        [
            pl.BlockSpec((tokens, width), lambda i, s: (i, 0)),
            pl.BlockSpec((tokens, 128), lambda i, s: (i, 0)),
            pl.BlockSpec((tokens, 128), lambda i, s: (0, 0)),
            pl.BlockSpec((8, 128), lambda i, s: (0, 0)),
        ],
        "gather", 1e9, grid=(count,), prefetch=1, hold=hold, after=after)
    return (outs[0], outs[1], outs[2], outs[3][0]), kept


def middle_kernel(x_ref, o_ref, out_ref, gain_ref, query_ref, h_ref, n_ref, c_ref):
    h = x_ref[...].astype(F32) + nn(o_ref[...], out_ref[...])
    h_ref[...] = h
    n_ref[...] = norm(h, gain_ref[...])
    c_ref[...] = nn(n_ref[...], query_ref[...]).astype(BF16) * BF16(0.125)


def back_middle_kernel(dc_ref, query_ref, h_ref, gain_ref, dh_ref, out_ref, dh1_ref, r_ref, do_ref, dgain_ref):
    @pl.when(pl.program_id(0) == 0)
    def _():
        dgain_ref[...] = jnp.zeros_like(dgain_ref)

    back, part = norm_back(h_ref[...], nt(dc_ref[...], query_ref[...]), gain_ref[...])
    dgain_ref[...] += part
    dh1 = dh_ref[...] + back
    dh1_ref[...] = dh1
    r_ref[...] = dh1.astype(BF16)
    do_ref[...] = nt(r_ref[...], out_ref[...]).astype(BF16)


def exit_kernel(dq_ref, query_ref, own_ref, *refs):
    peers = refs[:len(refs) - 8]
    keyvalue_ref, x_ref, gain_ref, dh_ref, dx_a_ref, dx_b_ref, dkv_ref, dgain_ref = refs[len(refs) - 8:]
    half = pl.num_programs(0) // 2

    @pl.when(pl.program_id(0) == 0)
    def _():
        dgain_ref[...] = jnp.zeros_like(dgain_ref)

    sides = [sum((ref[side].astype(F32) for ref in peers), own_ref[side].astype(F32)) for side in range(2)]
    dkv_ref[...] = lanes(sides[0], sides[1]).astype(BF16)
    dn = nt(dq_ref[...], query_ref[...]) + nt(dkv_ref[...], keyvalue_ref[...])
    back, part = norm_back(x_ref[...].astype(F32), dn, gain_ref[...])
    dgain_ref[...] += part
    dx = (dh_ref[...] + back).astype(BF16)

    @pl.when(pl.program_id(0) < half)
    def _():
        dx_a_ref[...] = dx

    @pl.when(pl.program_id(0) >= half)
    def _():
        dx_b_ref[...] = dx


def by_rows(kernel, name, flops, arrays, outs, width, dgain=False, hold=(), after=()):
    tokens = next(x.shape[0] for x, cut in arrays if cut)
    tile = min(256, tokens)
    blocks = pl.BlockSpec((tile, width), lambda i: (i, 0))

    def spec(x, cut):
        if x.ndim == 3:
            return pl.BlockSpec((x.shape[0], tile, x.shape[2]), lambda i: (0, i, 0))
        return blocks if cut else pl.BlockSpec(x.shape, lambda i: (0, 0))

    in_specs = [spec(x, cut) for x, cut in arrays]
    shapes, specs = [], []
    steps = tokens // tile
    for kind in outs:
        if kind == "halves":
            shapes += [jax.ShapeDtypeStruct((tokens // 2, width), BF16)] * 2
            specs += [pl.BlockSpec((tile, width), lambda i: (jnp.minimum(i, steps // 2 - 1), 0)),
                      pl.BlockSpec((tile, width), lambda i: (jnp.maximum(i - steps // 2, 0), 0))]
        else:
            shapes.append(jax.ShapeDtypeStruct((tokens, width), kind))
            specs.append(blocks)
    if dgain:
        shapes.append(jax.ShapeDtypeStruct((8, width), F32))
        specs.append(pl.BlockSpec((8, width), lambda i: (0, 0)))
    return call(kernel, tuple(x for x, _ in arrays), in_specs, shapes, specs, name, flops,
                grid=(tokens // tile,), hold=hold, after=after)


def feed_kernel(rest, h1_ref, co_ref, cross_ref, g_ref, gain_ref, gate_ref, up_ref, down_ref,
                out_a_ref, out_b_ref, n_ref, hidden_ref, dgu_ref, dh_ref, low_ref, dco_ref, dgain_ref,
                out_acc, dn_acc, h_acc):
    size = out_a_ref.shape[0]
    step, steps = pl.program_id(0), pl.num_programs(0)

    @pl.when(step == 0)
    def _():
        h = h1_ref[...] + nn(co_ref[...], cross_ref[...])
        h_acc[...] = h
        n_ref[...] = norm(h, gain_ref[...])
        out_acc[...] = jnp.zeros_like(out_acc)
        dn_acc[...] = jnp.zeros_like(dn_acc)

    def main(tile):
        n = n_ref[...]
        gate = nn(n, gate_ref[:, :tile])
        up = nn(n, up_ref[:, :tile])
        dhidden = nt(g_ref[...], down_ref[:tile, :])
        square = gate * gate
        bend = jnp.tanh(gate * (GELU_A + GELU_B * square))
        half = 0.5 + 0.5 * bend
        gelu = gate * half
        slope = half + gate * (0.5 - 0.5 * bend * bend) * (GELU_A + 3.0 * GELU_B * square)
        hidden = (gelu * up).astype(BF16)
        dgate = (dhidden * up * slope).astype(BF16)
        dup = (dhidden * gelu).astype(BF16)
        hidden_ref[:, :tile] = hidden
        dgu_ref[:, :tile] = dgate
        dgu_ref[:, tile:2 * tile] = dup
        out_acc[...] += nn(hidden, down_ref[:tile, :])
        dn_acc[...] += nt(dgate, gate_ref[:, :tile]) + nt(dup, up_ref[:, :tile])

    tile = gate_ref.shape[1]
    if rest == tile:
        main(tile)
    else:
        pl.when(step < steps - 1)(lambda: main(tile))
        pl.when(step == steps - 1)(lambda: main(rest))

    @pl.when(step == steps - 1)
    def _():
        h = h_acc[...]
        out = (h + out_acc[...]).astype(BF16)
        out_a_ref[...] = out[:size]
        out_b_ref[...] = out[size:]
        back, dgain_ref[...] = norm_back(h, dn_acc[...], gain_ref[...])
        dh = g_ref[...].astype(F32) + back
        dh_ref[...] = dh
        low_ref[...] = dh.astype(BF16)
        dco_ref[...] = nt(low_ref[...], cross_ref[...]).astype(BF16)


def feed_forward(h, co, cross_output, g, gain, feed_gate, feed_up, feed_down, hold=(), after=()):
    tokens, width = h.shape
    hidden = feed_gate.shape[1]
    tile = FEED
    rest = hidden - (hidden - 1) // tile * tile
    whole = pl.BlockSpec((tokens, width), lambda i: (0, 0), pipeline_mode=pl.Buffered(1))
    square = pl.BlockSpec((width, width), lambda i: (0, 0), pipeline_mode=pl.Buffered(1))
    row = pl.BlockSpec((1, width), lambda i: (0, 0))
    low, wide = jax.ShapeDtypeStruct(h.shape, BF16), jax.ShapeDtypeStruct(h.shape, F32)
    chunk = jax.ShapeDtypeStruct((tokens // 2, width), BF16)
    part = pl.BlockSpec(chunk.shape, lambda i: (0, 0), pipeline_mode=pl.Buffered(1))
    return call(
        functools.partial(feed_kernel, rest),
        (h, co, cross_output, g, gain, feed_gate, feed_up, feed_down),
        [
            whole, whole, square, whole, row,
            pl.BlockSpec((width, tile), lambda i: (0, i)),
            pl.BlockSpec((width, tile), lambda i: (0, i)),
            pl.BlockSpec((tile, width), lambda i: (i, 0)),
        ],
        [chunk, chunk, low, jax.ShapeDtypeStruct((tokens, hidden), BF16), jax.ShapeDtypeStruct((tokens, 2 * hidden), BF16),
         wide, low, low, jax.ShapeDtypeStruct((8, width), F32)],
        [part, part, whole, pl.BlockSpec((tokens, tile), lambda i: (0, i)), pl.BlockSpec((tokens, 2 * tile), lambda i: (0, i)),
         whole, whole, whole, pl.BlockSpec((8, width), lambda i: (0, 0))],
        "feed_forward", 45e9, grid=(pl.cdiv(hidden, tile),), hold=hold, after=after,
        scratch=[pltpu.VMEM((tokens, width), F32) for _ in range(3)],
    )


class Group:
    def __init__(self):
        self.S, self.R = lax.axis_size("seq"), lax.axis_size("row")
        self.s, self.r = lax.axis_index("seq"), lax.axis_index("row")
        self.core = self.r % 2
        self.chunks = self.S
        self.members = self.S // 2
        self.member = (self.s // 4) * 2 + self.core
        self.first_half = self.s < self.S // 2
        self.places = [(s, r) for s in range(self.S) for r in range(self.R)]

    def index(self, s, r):
        return s * self.R + r

    def send(self, x, target):
        pairs = [(self.index(s, r), self.index(*target(s, r))) for s, r in self.places]
        return lax.ppermute(x, ("seq", "row"), pairs)

    def route(self, way):
        S = self.S

        def target(s, r):
            second = (s >= S // 2) if way == 0 else (s < S // 2)
            row = 2 * (r % 2) + (1 if second else 0)
            member = min(s, S - 1 - s)
            return (row + 4 * (member // 2), r - r % 2 + member % 2)

        return [(self.index(s, r), self.index(*target(s, r))) for s, r in self.places]

    def part(self, x, way):
        return jnp.where(self.first_half == (way == 0), x[0], x[1])

    def go(self, x, way):
        return lax.ppermute(x, ("seq", "row"), self.route(way))

    def back(self, x, way):
        return lax.ppermute(x, ("seq", "row"), [(t, f) for f, t in self.route(way)])

    def two_rows(self, a, b):
        return jnp.where(self.first_half, a, b), jnp.where(self.first_half, b, a)

    def peer(self, x, distance):
        return self.send(x, lambda s, r: (s ^ (4 * (distance >> 1)), r ^ (distance & 1)))

    def peers(self, x):
        return [x] + [self.peer(x, p) for p in range(1, self.members)]

    def core_swap(self, x):
        return self.send(x, lambda s, r: (s, r ^ 1))

    def sum_axes(self):
        sizes = [("row", self.R), ("seq", self.S)]
        return [(axis, bit) for axis, size in sizes for bit in range(size.bit_length() - 1)]

    def names(self):
        top = self.S.bit_length() - 2
        row_bits = list(range(1, self.R.bit_length() - 1))
        return [("seq", k) for k in reversed(range(top))] + [("row", k) for k in reversed(row_bits)] + [("row", 0)]

    def bits(self):
        values = [((self.s if kind == "seq" else self.r) >> bit) & 1 for kind, bit in self.names()[:-1]]
        return jnp.stack(values + [self.s >> (self.S.bit_length() - 2)]).astype(jnp.int32)

    def swap(self, give, name):
        size = self.S if name[0] == "seq" else self.R
        return lax.ppermute(give, name[0], [(i, i ^ (1 << name[1])) for i in range(size)])

    def last_sends(self, straight, crossed):
        half = self.S // 2
        one = self.send(straight, lambda s, r: ((r % 2) * half + s % half, (r - r % 2) + s // half))
        two = self.send(crossed, lambda s, r: ((r % 2) * half + s % half, (r - r % 2) + 1 - s // half))
        return one, two


    def all_sends(self, pieces):
        half = self.S // 2
        sent = []
        for piece, (low, top) in zip(pieces, self.last_changes()):
            sent.append(self.send(piece, lambda s, r: (
                (r % 2) * half + (s % half ^ low), (r - r % 2) + (s // half ^ top))))
        return sent

    def last_changes(self):
        return [(low, top) for low in range(self.S // 2) for top in range(2)]


def grad_kernel(jobs, blocks, half_ref, *refs):
    inputs = sum(1 + job[-1] for job in jobs)
    out_ref, scratch = refs[inputs], refs[inputs + 1:]
    step = pl.program_id(0)
    place = 0

    def chunks_of(total, rows_in, paired):
        rows_out = -(-rows_in // 16) * 16
        for chunk in range(total.shape[1] // CHUNK):
            block = total[:, chunk * CHUNK:(chunk + 1) * CHUNK].reshape(blocks, rows_in, CHUNK)
            if paired:
                block = block.reshape(-1, 2, 2, 64 // rows_in, rows_in, CHUNK)
                block = jnp.swapaxes(block, 1, 2).reshape(blocks, rows_in, CHUNK)
            if rows_out > rows_in:
                block = jnp.concatenate([block, jnp.zeros((blocks, rows_out - rows_in, CHUNK), F32)], axis=1)
            yield slice(chunk * rows_out, (chunk + 1) * rows_out), block.astype(BF16)

    def direct(left_ref, right_refs, count, rows_in, paired):
        if len(right_refs) == 1:
            right = right_refs[0][:, :count * CHUNK]
        else:
            sides = [sum((ref[n].astype(F32) for ref in right_refs[1:]), right_refs[0][n].astype(F32)) for n in range(2)]
            right = lanes(*sides).astype(BF16)
        for at, block in chunks_of(tn(left_ref[...], right), rows_in, paired):
            out_ref[:, at, :] = block

    for start, full, rest, rows_in, paired, slabs, terms in jobs:
        left_ref, right_refs = refs[place], refs[place + 1:place + 1 + terms]
        right_ref = right_refs[0]
        place += 1 + terms
        if slabs:
            @pl.when(step == start)
            def _(left_ref=left_ref, right_ref=right_ref, rows_in=rows_in, paired=paired):
                for at, block in chunks_of(tn(left_ref[...], right_ref[...]), rows_in, paired):
                    scratch[0][:, at, :] = block

            deep = out_ref.shape[1]
            for slab in range(slabs):
                @pl.when(step == start + slab)
                def _(slab=slab):
                    out_ref[...] = scratch[0][:, slab * deep:(slab + 1) * deep, :]
            continue
        if full:
            run = functools.partial(direct, left_ref, right_refs, 2, rows_in, paired)
            pl.when((step >= start) & (step < start + full))(run)
        if rest:
            run = functools.partial(direct, left_ref, right_refs, 1, rows_in, paired)
            pl.when(step == start + full)(run)


def grad_part(half, pairs, blocks, rows_in, total, first=0, before=None, hold=(), after=(), holds=False):
    rows_out = -(-rows_in // 16) * 16
    jobs, inputs, in_specs, scratch = [], [half], [], []
    start = 0
    for left, right, *more in pairs:
        paired, own_rows = (more + [False, rows_in][len(more):])
        terms = list(right) if isinstance(right, (list, tuple)) else [right]
        full, rest = (1, 0) if len(terms) > 1 else divmod(right.shape[1] // CHUNK, 2)
        tokens, side = left.shape[0], left.shape[1] // 2
        slabs = 0
        steps = full + rest
        if own_rows != rows_in:
            deep = 2 * (-(-own_rows // 16) * 16)
            slabs = steps = deep // (2 * rows_out)
            scratch.append(pltpu.VMEM((blocks, deep, CHUNK), BF16))
            index = lambda i, h: (0, 0)
        else:
            index = lambda i, h, start=start, steps=steps: (0, jnp.clip(i - start, 0, steps - 1))
        jobs.append((start, full, rest, own_rows, bool(paired), slabs, len(terms)))
        inputs += [left] + terms
        in_specs.append(pl.BlockSpec((tokens, side), lambda i, h: (0, h[0])))
        if len(terms) > 1:
            in_specs += [pl.BlockSpec((2, tokens, CHUNK), lambda i, h: (0, 0, 0))] * len(terms)
        else:
            in_specs.append(pl.BlockSpec((tokens, 2 * CHUNK), index))
        start += steps
    kernel, inputs, in_specs, alias = with_before(
        functools.partial(grad_kernel, tuple(jobs), blocks), inputs, in_specs, before)
    (out,), kept = call(
        kernel, inputs, in_specs,
        [jax.ShapeDtypeStruct((blocks, total, CHUNK), BF16)],
        [pl.BlockSpec((blocks, 2 * rows_out, CHUNK), lambda i, h: (0, first + i, 0))],
        "weight_grads", 1e9, grid=(start,), prefetch=1, hold=hold, after=after, alias=alias, scratch=scratch,
    )
    return (out, kept) if holds else out


def stage_kernel(plan, bits_ref, *refs):
    count = max(max(terms) for _, terms, _ in plan) + 1
    for out, terms, at in plan:
        total = sum((refs[t][...].astype(F32) for t in terms[1:]), refs[terms[0]][...].astype(F32))
        refs[count + out][:, at, :] = total.astype(BF16)


def last_kernel(changes, counts, place_ref, *refs):
    inputs, outs = refs[:sum(counts)], refs[sum(counts):]
    for (low, top), out in zip(changes, outs):
        at = 2 * jnp.bitwise_xor(place_ref[0], low) + jnp.bitwise_xor(place_ref[1], top)
        start, first = 0, 0
        for count in counts:
            terms = inputs[start:start + count]
            block = sum((ref[pl.ds(at, 1)].astype(F32) for ref in terms[1:]), terms[0][pl.ds(at, 1)].astype(F32))
            out[first:first + block.shape[1], :] = block[0].astype(BF16)
            start, first = start + count, first + block.shape[1]


def last_stage(group, streams, after=(), hold=()):
    half = group.S // 2
    place = jnp.stack([group.s % half, group.s // half]).astype(jnp.int32)
    changes = group.last_changes()
    terms = [array for stream in streams for array, _, _ in stream.terms]
    shape = jax.ShapeDtypeStruct((sum(stream.rows_in for stream in streams), CHUNK), BF16)
    return call(
        functools.partial(last_kernel, changes, [len(stream.terms) for stream in streams]), (place, *terms),
        [pl.BlockSpec(x.shape, lambda p: (0, 0, 0)) for x in terms],
        [shape] * len(changes), [pl.BlockSpec(shape.shape, lambda p: (0, 0))] * len(changes),
        "last_stage", 1e9, prefetch=1, after=after, hold=hold)


class Stream:
    def __init__(self, terms, names, order, rows_in):
        self.terms, self.names, self.order, self.rows_in = terms, names, list(order), rows_in

    def got(self, array, names):
        self.terms.append((array, names, 0))


def stage(group, bits, streams, keep=True, join=False, after=(), hold=()):
    all_names = group.names()
    inputs, in_specs, shapes, out_specs, plan = [bits], [], [], [], []
    grid = 2 ** (len(streams[0].names) - 1)
    lead = 2 if streams[0].order[0] != all_names[-1] and grid > 1 else 1
    for number, stream in enumerate(streams):
        axis = stream.order[0]
        rest = [name for name in stream.names if name != axis]

        def spec(names, part, give, rest=rest, axis=axis, rows_in=stream.rows_in):
            def place(i, b):
                index = 0
                for name in names if lead == 1 else names[:-1]:
                    own = b[all_names.index(name)]
                    if name == axis:
                        value = 1 - own if give else own
                    elif name in rest:
                        value = (i * lead >> (len(rest) - 1 - rest.index(name))) & 1
                    else:
                        value = own
                    index = index * 2 + value
                return (index, part, 0)

            return pl.BlockSpec((lead, rows_in, CHUNK), place)

        sides = (True, False) if keep else (True,)
        for give in sides:
            terms = []
            for array, names, part in stream.terms:
                terms.append(len(inputs) - 1)
                inputs.append(array)
                in_specs.append(spec(names, part, give))
            count = stream.rows_in
            if join:
                plan.append((0 if give else 1, tuple(terms), slice(number * count, (number + 1) * count)))
            else:
                plan.append((len(shapes), tuple(terms), slice(0, count)))
            if not join or number == 0:
                full = count * (len(streams) if join else 1)
                shapes.append(jax.ShapeDtypeStruct((grid, full, CHUNK), BF16))
                out_specs.append(pl.BlockSpec((lead, full, CHUNK), lambda i, b: (i, 0, 0)))
    return call(functools.partial(stage_kernel, tuple(plan)), tuple(inputs), in_specs, shapes, out_specs, "stage", 1e9,
                grid=(grid // lead,), prefetch=1, after=after, hold=hold)


class Bundle:
    def __init__(self, group, bits):
        self.group, self.bits, self.ends = group, bits, []

    def swap(self, theirs):
        self.other = self.group.core_swap(theirs)

    def begin(self, mine, after=(), hold=()):
        names = self.group.names()
        rows_axes = [name for name in names if name[0] == "row" and name[1]]
        seq_axes = [name for name in names if name[0] == "seq"][::-1]
        half = mine.shape[1] // 2
        self.streams = [
            Stream([(mine, names, n), (self.other, names, n)], names, (rows_axes[::-1], rows_axes)[n] + seq_axes + [("row", 0)], half)
            for n in range(2)
        ]
        self.gives, kept = stage(self.group, self.bits, self.streams, keep=False, after=after, hold=hold)
        self.send()
        return kept

    def send(self):
        self.fly = [self.group.swap(give, s.order[0]) for give, s in zip(self.gives, self.streams)]

    def step(self, after=(), hold=(), direct=False):
        if self.ends:
            return list(hold)
        for stream, got in zip(self.streams, self.fly):
            axis = stream.order.pop(0)
            stream.names = [name for name in stream.names if name != axis]
            stream.got(got, list(stream.names))
        if direct:
            self.gives, kept = last_stage(self.group, self.streams, after=after, hold=hold)
            self.ends = self.group.all_sends(self.gives)
            return kept
        one = self.streams[0]
        join = len(self.streams) == 2 and one.names == self.streams[1].names and one.order == self.streams[1].order
        outs, kept = stage(self.group, self.bits, self.streams, join=join, after=after, hold=hold)
        axis = one.order[0]
        if join:
            self.streams = [Stream([], list(one.names), one.order, 2 * one.rows_in)]
        if axis == ("row", 0):
            crossed, straight = outs
            self.gives = [crossed]
            self.ends = list(self.group.last_sends(straight, crossed))
            return kept
        self.gives = []
        for n, stream in enumerate(self.streams):
            self.gives.append(outs[2 * n])
            rest = [name for name in stream.names if name != stream.order[0]]
            stream.terms = [(outs[2 * n + 1], rest, 0)]
        self.send()
        return kept

    def finish(self):
        while not self.ends:
            self.step()

    def result(self):
        return sum((x.astype(F32) for x in self.ends[1:]), self.ends[0].astype(F32)).reshape(-1, CHUNK)


def by_pairs(weight, axis):
    shape = weight.shape
    split = shape[:axis] + (shape[axis] // 256, 2, 2, 64) + shape[axis + 1:]
    return jnp.swapaxes(weight.reshape(split), axis + 1, axis + 2).reshape(shape)


def bias_rows(bias_table, sub):
    table = by_heads((bias_table - bias_table[BUCKETS - 1:]).T)
    levels = np.array([bucket_level(d) for d in range(2 * NEAR)])
    values = jnp.dot(table, jnp.asarray(np.eye(BUCKETS, dtype=np.float32)[levels].T), precision=HIGHEST)
    near = values[:, :sub] if sub <= 2 * NEAR else jnp.pad(values, ((0, 0), (0, sub - 2 * NEAR)))
    near = jnp.concatenate([near, jnp.full((HEADS, sub), MASK, F32)], axis=1)
    corner = jnp.concatenate([values[:, NEAR:], jnp.zeros((HEADS, 1), F32), values[:, 1:NEAR]], axis=1)
    return [jnp.broadcast_to(a[:, None], (HEADS, 8, a.shape[1])) for a in (near, corner)]


def by_heads(x):
    return jnp.swapaxes(x.reshape((4, 2, 2) + x.shape[1:]), 1, 2).reshape(x.shape)


def bias_table_sums(near, corner):
    def fold(wide, distances):
        matrix = np.zeros((8, wide, BUCKETS), np.float32)
        for row in range(8):
            for lane in range(wide):
                distance = distances((lane - row) % wide)
                if distance is not None:
                    matrix[row, lane, bucket_level(distance)] = 1.0
        return jnp.asarray(matrix.reshape(8 * wide, BUCKETS))

    sub = near.shape[2] // 2
    first = fold(2 * sub, lambda d: d if d < sub else None)
    second = fold(2 * NEAR, lambda d: NEAR + d if d < NEAR else (d - NEAR if d > NEAR else None))
    total = jnp.dot(near.reshape(HEADS, -1), first, precision=HIGHEST)
    total = total + jnp.dot(corner.reshape(HEADS, -1), second, precision=HIGHEST)
    rest = -jnp.sum(total[:, :BUCKETS - 1], axis=1, keepdims=True)
    return by_heads(jnp.concatenate([total[:, :BUCKETS - 1], rest], axis=1)).T


def on_device(tokens, segment_ids, memory, cotangent, gain_attend, gain_cross, gain_feed, bias_table,
              self_query, self_keyvalue, self_output, cross_query, cross_keyvalue, cross_output,
              feed_gate, feed_up, feed_down):
    group = Group()
    size, width = tokens.shape[1:]
    span = memory.shape[1]
    hidden_width = feed_gate.shape[1]
    chunks = group.chunks
    sub = min(256, size)
    bits = group.bits()
    core = group.core.astype(jnp.int32)[None]
    devices = group.S * group.R
    blocks = devices // 2

    def token_part(way):
        numbers = group.part(segment_ids, way).astype(BF16)
        numbers = jnp.pad(numbers[None], ((0, PAD - 1), (0, width - size)))
        return jnp.concatenate([group.part(tokens, way), numbers], axis=0)

    way_a = group.go(token_part(0), 0)
    way_b = group.go(token_part(1), 1)

    memory_rows = memory.reshape(-1, width)
    pairs = nn(memory_rows, cross_keyvalue).astype(BF16).reshape(2, span, width)
    own_query, own_output = by_pairs(self_query, 1), by_pairs(self_output, 0)
    other_query, other_output = by_pairs(cross_query, 1), by_pairs(cross_output, 0)
    near, near_back, corner, corner_back = bias_tiles(*bias_rows(bias_table, sub), sub)
    second = [jnp.concatenate([group.part(cotangent, way), group.part(pairs, way)], axis=0) for way in range(2)]

    (x, n1, message), (second_a,) = entry(
        way_a, way_b, gain_attend[None], self_keyvalue, hold=[second[0]],
        after=[own_query, own_output, other_query, other_output, near, second[1]])
    messages = group.peers(message)
    second_a = group.go(second_a, 0)
    second_b = group.go(second[1], 1)
    (q,), _ = by_rows(query_kernel, "query", 2e9, [(n1, True), (own_query, False)], [BF16], width)
    (kv, key_marks, query_marks, meta), _ = gather(
        (2 * group.member + group.s % 2).astype(jnp.int32)[None], messages, after=[q])
    (o, lse), _ = self_forward(meta, q, kv, query_marks, key_marks, near, corner, chunks, 0, 1, None)
    memory_own, g = unpack(second_a, second_b, size, [o])
    memories = group.peers(memory_own)
    (h1, n2, c), _ = by_rows(
        middle_kernel, "middle", 5e9,
        [(x, True), (o, True), (own_output, False), (gain_cross[None], False), (other_query, False)],
        [F32, BF16, BF16], width, after=[memory_own])
    (co, cross_lse), _ = cross_forward(c, memories)
    (out_a, out_b, n3, hidden, dgu, dh2, r2, dco, dgain_feed), _ = feed_forward(
        h1, co, other_output, g, gain_feed[None], feed_gate, feed_up, feed_down)

    feed_rows = hidden.shape[1] // devices
    if feed_rows % 8:
        padded = -(-feed_rows // 16) * 16
        hidden = jnp.pad(hidden.reshape(-1, devices, feed_rows), ((0, 0), (0, 0), (0, padded - feed_rows)))
        hidden = hidden.reshape(-1, devices * padded)
    down_rows = hidden.shape[1] // devices
    down_out = -(-down_rows // 16) * 16
    square_rows = width // devices
    square_out = -(-square_rows // 16) * 16
    down_total = down_out * (width // CHUNK)
    feed_total = -(-(down_total + square_out * (dgu.shape[1] // CHUNK)) // 32) * 32

    def feed_half(which, after=(), hold=()):
        return grad_part(which, [(hidden, g, False, down_rows), (n3, dgu)], blocks, square_rows, feed_total,
                         after=after, hold=hold, holds=True)

    theirs, (out_b,) = feed_half(1 - core, after=[out_a], hold=[out_b])
    out_a = group.back(out_a, 0)
    feed = Bundle(group, bits)
    feed.swap(theirs)
    mine, (out_b,) = feed_half(core, after=[theirs], hold=[out_b])
    out_a, = feed.begin(mine, hold=[out_a])
    out_b = group.back(out_b, 1)

    (dc, dm, *dm_peers), _ = cross_backward(c, dco, co, cross_lse, memories, after=feed.gives)
    (dh1, r1, do, dgain_cross), _ = by_rows(
        back_middle_kernel, "back_middle", 5e9,
        [(dc, True), (other_query, False), (h1, True), (gain_cross[None], False), (dh2, True), (own_output, False)],
        [F32, BF16, BF16], width, dgain=True)
    cross_pairs = [(co, r2, True), (n2, dc), (o, r1, True)]
    cross_total = 3 * square_out * (width // CHUNK)
    theirs, (out_b, *dm_peers) = grad_part(
        1 - core, cross_pairs, blocks, square_rows, cross_total, hold=[out_b] + dm_peers, holds=True)
    theirs, = feed.step(hold=[theirs], after=[out_b])
    cross = Bundle(group, bits)
    cross.swap(theirs)
    dm_peers = [group.peer(term, p + 1) for p, term in enumerate(dm_peers)]
    mine, (dm,) = grad_part(
        core, cross_pairs, blocks, square_rows, cross_total, after=[theirs] + feed.gives, hold=[dm], holds=True)
    dm_a, dm_b, _ = add_memory([dm] + dm_peers)

    def backward(part, before, after, hold=()):
        return self_backward(meta, q, do, o, lse, kv, query_marks, key_marks, near_back, corner_back, chunks,
                             part, 4, before, after=after, hold=hold)

    back, (dm_b, mine) = backward(0, None, [dm_a, cross.other], [dm_b, mine])
    dm_a = group.back(dm_a, 0)
    dm_a, = feed.step(after=[back[0], mine], hold=[dm_a])
    cross.begin(mine, after=feed.gives)
    back, (dm_b,) = backward(1, back, feed.gives + cross.gives, [dm_b])
    feed.step(after=[back[0]])
    cross.step(after=[back[0]] + feed.gives)
    back, (dm_b,) = backward(2, back, feed.gives + cross.gives, [dm_b])
    feed.finish()
    cross.step(after=[back[0]] + list(feed.ends))
    dm_b = group.back(dm_b, 1)
    back, _ = backward(3, back, cross.gives)
    dq, dkv_own, dkv_peers, near_sum, corner_sum = back
    dm_b, dkv_peers = cross.step(after=[dq], hold=[dm_b, dkv_peers])
    cross.finish()
    dkv_peers = [group.peer(dkv_peers[p - 1], p) for p in range(1, group.members)]
    dm = rows(*group.two_rows(dm_a, dm_b))
    own_total = 3 * square_out * (width // CHUNK)
    step = square_out * (width // CHUNK)
    theirs = grad_part(1 - core, [(n1, dq), (memory_rows, dm)], blocks, square_rows, own_total, after=cross.gives)
    dkv_terms = [dkv_own] + dkv_peers
    theirs = grad_part(1 - core, [(n1, dkv_terms)], blocks, square_rows, own_total, step // square_out, [theirs])
    (token_a, token_b, dkv, dgain_attend), (theirs,) = by_rows(
        exit_kernel, "exit", 5e9,
        [(dq, True), (own_query, False), (dkv_own, True)] + [(y, True) for y in dkv_peers]
        + [(self_keyvalue, False), (x, True), (gain_attend[None], False), (dh1, True)],
        ["halves", BF16], width, dgain=True, hold=[theirs])
    own = Bundle(group, bits)
    own.swap(theirs)
    token_source, token_a = token_a, group.back(token_a, 0)
    mine, (out_a, out_b, token_b, *ends) = grad_part(
        core, [(n1, dq), (memory_rows, dm), (n1, dkv)], blocks, square_rows, own_total,
        after=[token_source], hold=[out_a, out_b, token_b, near_sum, corner_sum, dgain_attend, dgain_cross, dgain_feed, dm], holds=True)
    near_sum, corner_sum, dgain_attend, dgain_cross, dgain_feed, dm_late = ends
    dbias = bias_table_sums(near_sum, corner_sum)
    small = jnp.stack([jnp.sum(dgain_attend, axis=0), jnp.sum(dgain_cross, axis=0), jnp.sum(dgain_feed, axis=0),
                       jnp.pad(dbias.reshape(-1), (0, width - dbias.size))])
    sum_axes = group.sum_axes()

    def small_step(x):
        return x + group.swap(x, sum_axes.pop(0))

    small = small_step(small)
    memory_grad = nt(dm_late, cross_keyvalue).astype(BF16).reshape(memory.shape)
    def squares(bundle, start, columns):
        rest = bundle[start:start + square_out * (columns // CHUNK)].reshape(columns // CHUNK, square_out, CHUNK)
        return jnp.swapaxes(rest[:, :square_rows], 0, 1).reshape(square_rows, columns)

    token_b, token_a, small, *ends = own.begin(
        mine, after=[memory_grad], hold=[token_b, token_a, small, out_a, out_b] + list(feed.ends) + list(cross.ends))
    out_a, out_b, *ends = ends
    count = len(feed.ends)
    feed.ends, cross.ends = ends[:count], ends[count:]
    token_b = group.back(token_b, 1)
    small = small_step(small)
    feed_sum = feed.result()
    grad_dgu = squares(feed_sum, down_total, dgu.shape[1])
    whole = hidden_width // FEED * FEED
    grad_dgu, grad_rest = grad_dgu[:, :2 * whole].reshape(square_rows, -1, 2, FEED), grad_dgu[:, 2 * whole:]
    grad_rest = grad_rest.reshape(square_rows, 2, hidden_width - whole)
    grad_gate, grad_up = [
        jnp.concatenate([grad_dgu[:, :, n].reshape(square_rows, -1), grad_rest[:, n]], axis=1) for n in range(2)]
    grad_down = feed_sum[:down_total].reshape(width // CHUNK, down_out, CHUNK)[:, :feed_rows]
    grad_down = jnp.swapaxes(grad_down, 0, 1).reshape(feed_rows, width)
    token_a, token_b, small, out_a, out_b, *cross.ends = own.step(
        hold=[token_a, token_b, small, out_a, out_b] + list(cross.ends), after=[grad_gate, grad_up, grad_down])
    small = small_step(small)
    tokens_grad = jnp.stack(group.two_rows(token_a, token_b))
    cross_sum = cross.result()
    grad_cross = [squares(cross_sum, n * step, width) for n in range(3)]
    grad_cross[1] = by_pairs(grad_cross[1], 1)
    small, out_a, out_b = own.step(hold=[small, out_a, out_b], after=[tokens_grad] + grad_cross, direct=True)
    layer_output = jnp.stack(group.two_rows(out_a, out_b))
    while sum_axes:
        small = small_step(small)
    own_sum = own.result()
    grad_own = [squares(own_sum, n * step, width) for n in (0, 2, 1)]

    return (
        layer_output,
        tokens_grad,
        memory_grad,
        by_pairs(grad_own[0], 1),
        grad_own[1],
        grad_cross[2],
        grad_cross[1],
        grad_own[2],
        grad_cross[0],
        grad_gate,
        grad_up,
        grad_down,
        small[0],
        small[1],
        small[2],
        small[3, :dbias.size].reshape(dbias.shape),
    )


def solution(mesh):
    data, whole, grads = P("row", "seq", None), P(), P(("seq", "row"), None)
    in_specs = (data, P("row", "seq"), data, data) + (whole,) * 13
    out_specs = (data,) * 3 + (grads,) * 9 + (whole,) * 4
    return jax.shard_map(on_device, mesh=mesh, in_specs=in_specs, out_specs=out_specs, check_vma=False)
```

```python
import functools
import math

import jax
import jax.numpy as jnp
import numpy as np
from jax import lax
from jax.experimental import pallas as pl
from jax.experimental.pallas import tpu as pltpu
from jax.sharding import PartitionSpec as P

HEADS = 16
BUCKETS = 32
MAX_DIST = 128
HIGHEST = lax.Precision.HIGHEST
F32, BF16 = jnp.float32, jnp.bfloat16
MASK = -float(2.0**100)
NEAR = 128
VMEM = 56 * 1024 * 1024
CHUNK = 512
PAD = 16
SELF_SPLIT = 1
SELF_AHEAD = 1
EAGER = True
AHEAD = 3
SPLIT = 2
BACK_SPLIT = 1
FEED = 512
COST = {
    "entry": 6, "query": 6, "gather": 5, "self_forward": 23, "middle": 9, "cross_forward": 20, "feed_forward": 70,
    "weight_grads": 9, "stage": 4, "cross_backward": 31, "back_middle": 12, "self_backward": 18, "exit": 11,
}
COST_SCALE = 0.001e9
GELU_A = math.sqrt(2.0 / math.pi)
GELU_B = GELU_A * 0.044715


def bucket_level(distance):
    exact_part = BUCKETS // 2
    if distance < exact_part:
        return distance
    which_bucket = exact_part + math.floor(
        math.log(distance / exact_part) / math.log(MAX_DIST / exact_part) * (BUCKETS - exact_part)
    )
    return min(BUCKETS - 1, which_bucket)


def call(kernel, inputs, in_specs, out_shape, out_specs, name, flops, grid=(), scratch=(), prefetch=0,
         hold=(), after=(), alias=None):
    hold, after = list(hold), list(after)
    count_in, count_out = len(inputs), len(out_shape)
    anywhere = pl.BlockSpec(memory_space=pl.ANY)

    def body(*refs):
        kept = count_in + len(hold) + len(after)
        kernel(*refs[:count_in], *refs[kept:kept + count_out], *refs[kept + count_out + len(hold):])

    aliases = {count_in + i: count_out + i for i in range(len(hold))}
    aliases.update(alias or {})
    outs = pl.pallas_call(
        body,
        grid_spec=pltpu.PrefetchScalarGridSpec(
            num_scalar_prefetch=prefetch,
            grid=grid,
            in_specs=list(in_specs) + [anywhere] * (len(hold) + len(after)),
            out_specs=list(out_specs) + [anywhere] * len(hold),
            scratch_shapes=list(scratch),
        ),
        out_shape=list(out_shape) + [jax.ShapeDtypeStruct(x.shape, x.dtype) for x in hold],
        input_output_aliases=aliases,
        compiler_params=pltpu.CompilerParams(vmem_limit_bytes=VMEM),
        cost_estimate=pl.CostEstimate(flops=int(COST.get(name, 5) * COST_SCALE), bytes_accessed=10**4, transcendentals=0),
        name=name,
    )(*inputs, *hold, *after)
    return list(outs[:count_out]), list(outs[count_out:])


def nt(a, b):
    return lax.dot_general(a, b, (((1,), (1,)), ((), ())), preferred_element_type=F32)


def nn(a, b):
    return jnp.dot(a, b, preferred_element_type=F32)


def tn(a, b):
    return lax.dot_general(a, b, (((0,), (0,)), ((), ())), preferred_element_type=F32)


def halves(block):
    low = lax.broadcasted_iota(jnp.int32, block.shape, 1) < 64
    zero = jnp.zeros_like(block)
    return jnp.where(low, block, zero), jnp.where(low, zero, block)


def lanes(a, b):
    return jnp.concatenate([a, b], axis=1)


def rows(a, b):
    return jnp.concatenate([a, b], axis=0)


def chunk_of(member, part, chunks):
    high = jnp.bitwise_xor(part, member % 2)
    return jnp.where(high == 0, member // 2, chunks - 1 - member // 2)


def slot_of(member, chunk, chunks):
    high = (chunk >= chunks // 2).astype(jnp.int32)
    other = jnp.where(chunk >= chunks // 2, chunks - 1 - chunk, chunk)
    return 2 * jnp.bitwise_xor(other, member // 2) + jnp.bitwise_xor(high, member % 2)


def first_block(meta, member, chunk, chunks):
    mine = meta[1 + slot_of(member, chunk, chunks)]

    def skip(block, start):
        last = meta[1 + chunks + slot_of(member, block, chunks)]
        return start + jnp.where((block < chunk) & (last < mine), 1, 0)

    return lax.fori_loop(0, chunks, skip, jnp.int32(0))


def in_turn(count, ahead, issue, process):
    waiting = [issue(i) for i in range(min(ahead, count))]
    for i in range(count):
        if i + ahead < count:
            waiting.append(issue(i + ahead))
        process(i, waiting.pop(0))


def self_forward_kernel(chunks, sub, meta, q_ref, k_ref, v_ref, qf_ref, kf_ref, near_ref, corner_ref,
                        o_ref, lse_ref, acc_ref, m_ref):
    size = q_ref.shape[0]
    member = meta[0]
    chunk = chunk_of(member, pl.program_id(1), chunks)
    q_both = [lanes(part, qf_ref[...]) for part in halves(q_ref[...])]

    def values(at, length):
        low, high = halves(v_ref[pl.ds(at, length), :])
        one_low, one_high = halves(jnp.ones((length, 128), BF16))
        return rows(lanes(low, one_low), lanes(high, one_high))

    own = pl.multiple_of(slot_of(member, chunk, chunks) * size, size)
    chains = [(strip, head) for strip in range(size // sub) for head in range(2)]
    weights = {}

    def near_issue(i):
        strip, head = chains[i]
        span = (strip + 1) * sub
        return nt(q_both[head][strip * sub:span], lanes(k_ref[pl.ds(own, span), :], kf_ref[pl.ds(own, span), :]))

    def near_process(i, s):
        strip, head = chains[i]
        span = (strip + 1) * sub
        here = slice(strip * sub, span)
        last = s[:, span - sub:] + near_ref[head]
        if strip:
            edge = s[:, span - sub - NEAR:span - sub]
            edge = rows(edge[:NEAR] + corner_ref[head], edge[NEAR:])
            s = jnp.concatenate([s[:, :span - sub - NEAR], edge, last], axis=1)
        else:
            s = last
        top = jnp.max(s, axis=1, keepdims=True)
        m_ref[head, here, :] = jnp.broadcast_to(top, (sub, 128))
        weights[head] = jnp.exp(s - top).astype(BF16)
        if head:
            acc_ref[here, :] = nn(lanes(weights[0], weights[1]), values(own, span))

    in_turn(len(chains), AHEAD, near_issue, near_process)

    def far(block, carry):
        at = pl.multiple_of(slot_of(member, block, chunks) * size, size)
        keys = lanes(k_ref[pl.ds(at, size), :], kf_ref[pl.ds(at, size), :])
        vals = values(at, size)
        flag = jnp.where(block == chunk - 1, 1.0, 0.0).astype(F32)
        part = size // SPLIT
        chains = [(piece, head) for piece in range(SPLIT) for head in range(2)]
        weights, scales = {}, {}

        def issue(i):
            piece, head = chains[i]
            return nt(q_both[head][piece * part:(piece + 1) * part], keys)

        def process(i, s):
            piece, head = chains[i]
            here = slice(piece * part, (piece + 1) * part)
            if piece == 0:
                edge = s[:NEAR, size - NEAR:] + corner_ref[head] * flag
                edge = lanes(s[:NEAR, :size - NEAR], edge)
                s = rows(edge, s[NEAR:]) if part > NEAR else edge
            old = m_ref[head, here, :]
            top = jnp.maximum(old, jnp.max(s, axis=1, keepdims=True))
            scales[head] = jnp.exp(old - top)
            m_ref[head, here, :] = top
            weights[head] = jnp.exp(s - top[:, :1]).astype(BF16)
            if head:
                low = lax.broadcasted_iota(jnp.int32, (part, 128), 1) < 64
                scale = jnp.where(low, scales[0], scales[1])
                acc_ref[here, :] = acc_ref[here, :] * lanes(scale, scale) + nn(lanes(weights[0], weights[1]), vals)

        in_turn(len(chains), AHEAD, issue, process)
        return carry

    lax.fori_loop(first_block(meta, member, chunk, chunks), chunk, far, 0)
    low = lax.broadcasted_iota(jnp.int32, (size, 128), 1) < 64
    total = acc_ref[:, 128:]
    o_ref[...] = (acc_ref[:, :128] / total).astype(BF16)
    lse_ref[...] = jnp.where(low, m_ref[0], m_ref[1]) + jnp.log(total)


def pieces(column, shape):
    lane = lax.broadcasted_iota(jnp.int32, shape, 1)
    high = column.astype(BF16).astype(F32)
    rest = column - high
    middle = rest.astype(BF16).astype(F32)
    low = rest - middle
    full = jnp.where(lane == 4, high, jnp.where(lane == 5, middle, jnp.where(lane == 6, low, 0.0)))
    return full.astype(BF16)


def back_operands(q_ref, do_ref, o_ref, lse_ref, qf):
    shape = q_ref.shape
    q_both = halves(q_ref[...])
    do_both = halves(do_ref[...])
    product = do_ref[...].astype(F32) * o_ref[...].astype(F32)
    low = lax.broadcasted_iota(jnp.int32, shape, 1) < 64
    deltas = [jnp.sum(jnp.where(low, product, 0.0), axis=1, keepdims=True),
              jnp.sum(jnp.where(low, 0.0, product), axis=1, keepdims=True)]
    logs = [lse_ref[:, 0:1], lse_ref[:, 64:65]]
    extra = [pieces(log, shape) for log in logs]
    if qf is not None:
        extra = [part + qf for part in extra]
    q_wide = [lanes(part, more) for part, more in zip(q_both, extra)]
    do_wide = [lanes(part, pieces(delta, shape)) for part, delta in zip(do_both, deltas)]
    return q_both, do_both, q_wide, do_wide


def diagonal_sums(block):
    count, wide = block.shape[0], 2 * block.shape[1]
    block = lanes(block, jnp.zeros_like(block))
    while count > 8:
        count = count // 2
        block = block[:count] + pltpu.roll(block[count:], wide - count, 1)
    return block


def self_backward_kernel(chunks, sub, meta, q_ref, do_ref, o_ref, lse_ref, k_ref, v_ref, qf_ref, kf_ref,
                         near_ref, corner_ref, dq_ref, own_ref, peer_ref, near_out, corner_out,
                         dq_acc, dk_acc, dv_acc, near_acc, corner_acc):
    size = q_ref.shape[0]
    member = meta[0]
    chunk = chunk_of(member, pl.program_id(2), chunks)
    first = (pl.program_id(1) == 0) & (pl.program_id(2) == 0)
    last = (pl.program_id(1) == 1) & (pl.program_id(2) == 1)

    @pl.when(first)
    def _():
        dk_acc[...] = jnp.zeros_like(dk_acc)
        dv_acc[...] = jnp.zeros_like(dv_acc)

    @pl.when(pl.program_id(2) == 0)
    def _():
        near_acc[...] = jnp.zeros_like(near_acc)
        corner_acc[...] = jnp.zeros_like(corner_acc)

    q_both, do_both, q_wide, do_wide = back_operands(q_ref, do_ref, o_ref, lse_ref, qf_ref[...])
    own = pl.multiple_of(slot_of(member, chunk, chunks) * size, size)
    dq_acc[...] = jnp.zeros_like(dq_acc)

    def add(at, length, here, weights, grads, keys):
        dv_acc[pl.ds(at, length), :] += nn(lanes(*weights), rows(do_both[0][here], do_both[1][here]))
        dk_acc[pl.ds(at, length), :] += nn(lanes(*grads), rows(q_both[0][here], q_both[1][here]))
        dq_acc[here, :] += tn(rows(*grads), rows(*halves(keys)))

    for strip in range(size // sub):
        at = pl.multiple_of(own + strip * sub, sub)
        here = slice(strip * sub, size)
        k, v, kf = (ref[pl.ds(at, sub), :] for ref in (k_ref, v_ref, kf_ref))
        keys, vals = lanes(k, kf), lanes(v, kf)
        weights, grads = [], []
        for head in range(2):
            s = nt(keys, q_wide[head][here])
            dp = nt(vals, do_wide[head][here])
            block = s[:, :sub] + near_ref[head]
            more = (strip + 1) * sub < size
            if more:
                edge = s[sub - NEAR:, sub:sub + NEAR] + corner_ref[head]
                rest = s[:, sub:]
                rest = rows(rest[:sub - NEAR], lanes(edge, rest[sub - NEAR:, NEAR:]))
                s = lanes(block, rest)
            else:
                s = block
            p = jnp.exp(s)
            ds = p * dp
            near_acc[head] += ds[:, :sub]
            if more:
                corner_acc[head] += ds[sub - NEAR:, sub:sub + NEAR]
            weights.append(p.astype(BF16))
            grads.append(ds.astype(BF16))
        add(at, sub, here, weights, grads, k)

    def far(block, carry):
        at = pl.multiple_of(slot_of(member, block, chunks) * size, size)
        k, v, kf = (ref[pl.ds(at, size), :] for ref in (k_ref, v_ref, kf_ref))
        keys, vals = lanes(k, kf), lanes(v, kf)
        flag = jnp.where(block == chunk - 1, 1.0, 0.0).astype(F32)
        part = size // SELF_SPLIT
        chains = [(piece, head) for piece in range(SELF_SPLIT) for head in range(2)]
        weights, grads = {}, {}

        def issue(i):
            piece, head = chains[i]
            here = slice(piece * part, (piece + 1) * part)
            return nt(keys, q_wide[head][here]), nt(vals, do_wide[head][here])

        def process(i, products):
            piece, head = chains[i]
            s, dp = products
            if piece == 0:
                edge = s[size - NEAR:, :NEAR] + corner_ref[head] * flag
                edge = lanes(edge, s[size - NEAR:, NEAR:]) if part > NEAR else edge
                s = rows(s[:size - NEAR], edge)
            p = jnp.exp(s)
            ds = p * dp
            if piece == 0:
                corner_acc[head] += ds[size - NEAR:, :NEAR] * flag
            weights[head] = p.astype(BF16)
            grads[head] = ds.astype(BF16)
            if head and (SELF_SPLIT == 1 or EAGER):
                add(at, size, slice(piece * part, (piece + 1) * part), [weights[0], weights[1]], [grads[0], grads[1]], k)

        in_turn(len(chains), SELF_AHEAD, issue, process)
        return carry

    lax.fori_loop(first_block(meta, member, chunk, chunks), chunk, far, 0)
    dq_ref[...] = (dq_acc[...] * 0.125).astype(BF16)

    @pl.when(last)
    def _():
        for side, acc in enumerate((dk_acc, dv_acc)):
            own_ref[side] = acc[: 2 * size, :].astype(BF16)
            for other in range(peer_ref.shape[0]):
                at = 2 * size * (other + 1)
                peer_ref[other, side] = acc[at:at + 2 * size, :].astype(BF16)

    @pl.when(pl.program_id(2) == 1)
    def _():
        for head in range(2):
            near_out[head] = diagonal_sums(near_acc[head])
            corner_out[head] = diagonal_sums(corner_acc[head])


def with_before(kernel, inputs, in_specs, before):
    if before is None:
        return kernel, tuple(inputs), list(in_specs), None
    count = len(inputs)

    def body(*refs):
        kernel(*refs[:count], *refs[count + len(before):])

    specs = list(in_specs) + [pl.BlockSpec(memory_space=pl.ANY)] * len(before)
    return body, tuple(inputs) + tuple(before), specs, {count + i: i for i in range(len(before))}


def self_forward(meta, q, kv, qf, kf, near, corner, chunks, part, parts, before, hold=(), after=()):
    size = q.shape[0] // 2
    sub = min(256, size)
    length = kv.shape[0]
    blocks = 8 // parts
    shift = blocks * part
    own = pl.BlockSpec((size, 128), lambda b, c, m: (c, b + shift))
    kernel, inputs, in_specs, alias = with_before(
        functools.partial(self_forward_kernel, chunks, sub),
        (meta, q, kv, kv, qf, kf, near, corner),
        [
            own,
            pl.BlockSpec((length, 128), lambda b, c, m: (0, (b + shift) // 2)),
            pl.BlockSpec((length, 128), lambda b, c, m: (0, 4 + (b + shift) // 2)),
            pl.BlockSpec((size, 128), lambda b, c, m: (c, 0)),
            pl.BlockSpec((length, 128), lambda b, c, m: (0, 0)),
            pl.BlockSpec((2, sub, sub), lambda b, c, m: (b + shift, 0, 0)),
            pl.BlockSpec((2, NEAR, NEAR), lambda b, c, m: (b + shift, 0, 0)),
        ], before)
    return call(
        kernel, inputs, in_specs,
        [jax.ShapeDtypeStruct(q.shape, BF16), jax.ShapeDtypeStruct(q.shape, F32)],
        [own, own],
        "self_forward", 4e10 / parts, grid=(blocks, 2), prefetch=1, hold=hold, after=after, alias=alias,
        scratch=[pltpu.VMEM((size, 256), F32), pltpu.VMEM((2, size, 128), F32)],
    )


def self_backward(meta, q, do, o, lse, kv, qf, kf, near, corner, chunks, part, parts, before, hold=(), after=()):
    pairs = 4 // parts
    shift = pairs * part
    size = q.shape[0] // 2
    sub = min(256, size)
    length = kv.shape[0]
    own = pl.BlockSpec((size, 128), lambda g, b, c, m: (c, 2 * (g + shift) + b))
    inputs = [meta, q, do, o, lse, kv, kv, qf, kf, near, corner]
    in_specs = [
        own, own, own, own,
        pl.BlockSpec((length, 128), lambda g, b, c, m: (0, g + shift)),
        pl.BlockSpec((length, 128), lambda g, b, c, m: (0, 4 + g + shift)),
        pl.BlockSpec((size, 128), lambda g, b, c, m: (c, 0)),
        pl.BlockSpec((length, 128), lambda g, b, c, m: (0, 0)),
        pl.BlockSpec((2, sub, sub), lambda g, b, c, m: (2 * (g + shift) + b, 0, 0)),
        pl.BlockSpec((2, NEAR, NEAR), lambda g, b, c, m: (2 * (g + shift) + b, 0, 0)),
    ]
    kernel, inputs, in_specs, alias = with_before(
        functools.partial(self_backward_kernel, chunks, sub), inputs, in_specs, before)
    others = length // (2 * size) - 1
    return call(
        kernel, inputs, in_specs,
        [
            jax.ShapeDtypeStruct(q.shape, BF16),
            jax.ShapeDtypeStruct((2, 2 * size, 512), BF16),
            jax.ShapeDtypeStruct((others, 2, 2 * size, 512), BF16),
            jax.ShapeDtypeStruct((16, 8, 2 * sub), F32),
            jax.ShapeDtypeStruct((16, 8, 2 * NEAR), F32),
        ],
        [
            own,
            pl.BlockSpec((2, 2 * size, 128), lambda g, b, c, m: (0, 0, g + shift)),
            pl.BlockSpec((others, 2, 2 * size, 128), lambda g, b, c, m: (0, 0, 0, g + shift)),
            pl.BlockSpec((2, 8, 2 * sub), lambda g, b, c, m: (2 * (g + shift) + b, 0, 0)),
            pl.BlockSpec((2, 8, 2 * NEAR), lambda g, b, c, m: (2 * (g + shift) + b, 0, 0)),
        ],
        "self_backward", 6e10 / parts, grid=(pairs, 2, 2), prefetch=1, hold=hold, after=after, alias=alias,
        scratch=[
            pltpu.VMEM((size, 128), F32),
            pltpu.VMEM((length, 128), F32),
            pltpu.VMEM((length, 128), F32),
            pltpu.VMEM((2, sub, sub), F32),
            pltpu.VMEM((2, NEAR, NEAR), F32),
        ],
    )


def stacked(refs):
    return refs[0][...] if len(refs) == 1 else jnp.concatenate([ref[...] for ref in refs], axis=0)


def cross_forward_kernel(count, q_ref, *refs):
    keys, v = stacked(refs[:count]), stacked(refs[count:2 * count])
    o_ref, lse_ref = refs[2 * count:]
    length = keys.shape[0]
    low, high = halves(v)
    one_low, one_high = halves(jnp.ones((length, 128), BF16))
    values = rows(lanes(low, one_low), lanes(high, one_high))
    q_both = halves(q_ref[...])
    part = q_ref.shape[0] // SPLIT
    chains = [(piece, head) for piece in range(SPLIT) for head in range(2)]
    weights, tops = {}, {}

    def issue(i):
        piece, head = chains[i]
        return nt(q_both[head][piece * part:(piece + 1) * part], keys)

    def process(i, s):
        piece, head = chains[i]
        tops[head] = jnp.max(s, axis=1, keepdims=True)
        weights[head] = jnp.exp(s - tops[head]).astype(BF16)
        if head:
            here = slice(piece * part, (piece + 1) * part)
            acc = nn(lanes(weights[0], weights[1]), values)
            is_low = lax.broadcasted_iota(jnp.int32, (part, 128), 1) < 64
            total = acc[:, 128:]
            o_ref[here, :] = (acc[:, :128] / total).astype(BF16)
            lse_ref[here, :] = jnp.where(is_low, tops[0], tops[1]) + jnp.log(total)

    in_turn(len(chains), AHEAD, issue, process)


def cross_backward_kernel(count, q_ref, do_ref, o_ref, lse_ref, *refs):
    k, v = stacked(refs[:count]), stacked(refs[count:2 * count])
    dq_ref, dkv_refs, (dk_acc, dv_acc) = refs[2 * count], refs[2 * count + 1:3 * count + 1], refs[3 * count + 1:]
    first = (pl.program_id(1) == 0) & (pl.program_id(2) == 0)
    last = (pl.program_id(1) == 1) & (pl.program_id(2) == 1)

    @pl.when(first)
    def _():
        dk_acc[...] = jnp.zeros_like(dk_acc)
        dv_acc[...] = jnp.zeros_like(dv_acc)

    q_both, do_both, q_wide, do_wide = back_operands(q_ref, do_ref, o_ref, lse_ref, None)
    lane = lax.broadcasted_iota(jnp.int32, k.shape, 1)
    minus = jnp.where((lane >= 4) & (lane < 7), -1.0, 0.0).astype(BF16)
    keys, vals = lanes(k, minus), lanes(v, minus)
    size = q_ref.shape[0] // BACK_SPLIT
    chains = [(piece, head) for piece in range(BACK_SPLIT) for head in range(2)]
    weights, grads = {}, {}

    def issue(i):
        piece, head = chains[i]
        here = slice(piece * size, (piece + 1) * size)
        return nt(keys, q_wide[head][here]), nt(vals, do_wide[head][here])

    def process(i, products):
        head = chains[i][1]
        p = jnp.exp(products[0])
        weights[chains[i]] = p.astype(BF16)
        grads[chains[i]] = (p * products[1]).astype(BF16)

    in_turn(len(chains), AHEAD, issue, process)

    def both(x):
        return jnp.concatenate([x[piece, head] for head in range(2) for piece in range(BACK_SPLIT)], axis=1)

    dv_acc[...] += nn(both(weights), rows(*do_both))
    dk_acc[...] += nn(both(grads), rows(*q_both))
    for piece in range(BACK_SPLIT):
        here = slice(piece * size, (piece + 1) * size)
        dq_ref[here, :] = (tn(rows(grads[piece, 0], grads[piece, 1]), rows(*halves(k))) * 0.125).astype(BF16)

    @pl.when(last)
    def _():
        part = dk_acc.shape[0] // count
        for number, ref in enumerate(dkv_refs):
            at = slice(number * part, (number + 1) * part)
            ref[0] = dk_acc[at, :].astype(BF16)
            ref[1] = dv_acc[at, :].astype(BF16)


def cross_forward(q, memories, hold=(), after=()):
    size, part, count = q.shape[0] // 2, memories[0].shape[0], len(memories)
    own = pl.BlockSpec((size, 128), lambda b, c: (c, b))
    return call(
        functools.partial(cross_forward_kernel, count), (q, *memories, *memories),
        [own] + [pl.BlockSpec((part, 128), lambda b, c: (0, b // 2))] * count
        + [pl.BlockSpec((part, 128), lambda b, c: (0, 4 + b // 2))] * count,
        [jax.ShapeDtypeStruct(q.shape, BF16), jax.ShapeDtypeStruct(q.shape, F32)],
        [own, own],
        "cross_forward", 15e9, grid=(8, 2), hold=hold, after=after,
    )


def cross_backward(q, do, o, lse, memories, hold=(), after=()):
    size, part, count = q.shape[0] // 2, memories[0].shape[0], len(memories)
    own = pl.BlockSpec((size, 128), lambda g, b, c: (c, 2 * g + b))
    return call(
        functools.partial(cross_backward_kernel, count), (q, do, o, lse, *memories, *memories),
        [own, own, own, own] + [pl.BlockSpec((part, 128), lambda g, b, c: (0, g))] * count
        + [pl.BlockSpec((part, 128), lambda g, b, c: (0, 4 + g))] * count,
        [jax.ShapeDtypeStruct(q.shape, BF16)] + [jax.ShapeDtypeStruct((2, part, 512), BF16)] * count,
        [own] + [pl.BlockSpec((2, part, 128), lambda g, b, c: (0, 0, g))] * count,
        "cross_backward", 30e9, grid=(4, 2, 2), hold=hold, after=after,
        scratch=[pltpu.VMEM((part * count, 128), F32), pltpu.VMEM((part * count, 128), F32)],
    )


def add_kernel(*refs):
    terms, outs = refs[:-2], refs[-2:]
    for number, out in enumerate(outs):
        at = slice(number * out.shape[0], (number + 1) * out.shape[0])
        sides = [sum((ref[side, at, :].astype(F32) for ref in terms[1:]), terms[0][side, at, :].astype(F32)) for side in range(2)]
        out[...] = lanes(*sides).astype(BF16)


def add_memory(terms, hold=(), after=()):
    shape = jax.ShapeDtypeStruct((terms[0].shape[1] // 2, 2 * terms[0].shape[2]), BF16)
    (low, high), kept = call(
        add_kernel, tuple(terms), [pl.BlockSpec(x.shape, lambda: (0, 0, 0)) for x in terms],
        [shape] * 2, [pl.BlockSpec(shape.shape, lambda: (0, 0))] * 2, "add_memory", 1e9, hold=hold, after=after)
    return low, high, kept


def bias_kernel(sub, near_ref, corner_ref, near_out, back_out, corner_out, corner_back):
    for head in range(2):
        wide = jnp.broadcast_to(near_ref[head, :1], (sub, 2 * sub))
        block = pltpu.roll(wide, 0, 1, stride=1, stride_axis=0)[:, :sub]
        back_out[head] = block
        near_out[head] = block.T
        wide = jnp.broadcast_to(corner_ref[head, :1], (NEAR, 2 * NEAR))
        block = pltpu.roll(wide, 0, 1, stride=1, stride_axis=0)[:, :NEAR]
        corner_back[head] = block
        corner_out[head] = block.T


def bias_tiles(near, corner, sub):
    def spec(a, b):
        return pl.BlockSpec((2, a, b), lambda h: (h, 0, 0))

    def shape(a):
        return jax.ShapeDtypeStruct((16, a, a), F32)

    return pl.pallas_call(
        functools.partial(bias_kernel, sub),
        grid=(8,),
        in_specs=[spec(8, 2 * sub), spec(8, 2 * NEAR)],
        out_specs=[spec(sub, sub), spec(sub, sub), spec(NEAR, NEAR), spec(NEAR, NEAR)],
        out_shape=[shape(sub), shape(sub), shape(NEAR), shape(NEAR)],
        compiler_params=pltpu.CompilerParams(vmem_limit_bytes=VMEM),
        name="bias_tiles",
    )(near, corner)


def inverse_rms(h):
    return lax.rsqrt(jnp.mean(h * h, axis=1, keepdims=True) + 1e-06)


def norm(values, gain):
    return (values * inverse_rms(values) * gain).astype(BF16)


def norm_back(h, dn, gain):
    scale = inverse_rms(h)
    unit = h * scale
    spread = dn * unit
    share = jnp.mean(spread * gain, axis=1, keepdims=True)
    gain_part = jnp.sum(spread.reshape(-1, 8, spread.shape[1]), axis=0)
    return scale * (dn * gain - unit * share), gain_part


def entry_kernel(a_ref, b_ref, gain_ref, weight_ref, x_ref, n_ref, message_ref):
    tokens = x_ref.shape[0]
    size = tokens // 2
    tile = min(256, size)
    for side, ref in enumerate((a_ref, b_ref)):
        for i in range(size // tile):
            at = slice(side * size + i * tile, side * size + (i + 1) * tile)
            x = ref[i * tile:(i + 1) * tile, :]
            x_ref[at, :] = x
            n_ref[at, :] = norm(x.astype(F32), gain_ref[...])
            message_ref[at, :] = nn(n_ref[at, :], weight_ref[...]).astype(BF16)
        message_ref[tokens + side * PAD:tokens + (side + 1) * PAD, :] = ref[size:, :]


def entry(way_a, way_b, gain, weight, hold=(), after=()):
    tokens, width = 2 * (way_a.shape[0] - PAD), way_a.shape[1]
    inputs = (way_a, way_b, gain, weight)
    shapes = [jax.ShapeDtypeStruct((count, width), BF16) for count in (tokens, tokens, tokens + 2 * PAD)]
    return call(entry_kernel, inputs, [pl.BlockSpec(y.shape, lambda: (0, 0)) for y in inputs], shapes,
                [pl.BlockSpec(s.shape, lambda: (0, 0)) for s in shapes], "entry", 2e9, hold=hold, after=after)


def unpack_kernel(a_ref, b_ref, memory_ref, g_ref):
    span, size = memory_ref.shape[0] // 2, g_ref.shape[0] // 2
    for side, ref in enumerate((a_ref, b_ref)):
        g_ref[side * size:(side + 1) * size, :] = ref[:size, :]
        memory_ref[side * span:(side + 1) * span, :] = ref[size:, :]


def unpack(second_a, second_b, size, after):
    count, width = second_a.shape
    whole = pl.BlockSpec((count, width), lambda: (0, 0))
    shapes = [jax.ShapeDtypeStruct((2 * (count - size), width), BF16), jax.ShapeDtypeStruct((2 * size, width), BF16)]
    outs, _ = call(unpack_kernel, (second_a, second_b), [whole, whole], shapes,
                   [pl.BlockSpec(s.shape, lambda: (0, 0)) for s in shapes], "unpack", 1e9, after=after)
    return outs


def query_kernel(n_ref, weight_ref, q_ref):
    q_ref[...] = nn(n_ref[...], weight_ref[...]).astype(BF16) * BF16(0.125)


def gather_kernel(member_ref, *refs):
    messages = refs[:len(refs) - 4]
    kv_ref, key_ref, query_ref, meta_ref = refs[len(refs) - 4:]
    step = pl.program_id(0)
    tokens = messages[0].shape[0] - 2 * PAD
    size = tokens // 2
    for p, message in enumerate(messages):
        @pl.when(step == p)
        def _(p=p, message=message):
            kv_ref[...] = message[:tokens, :]
            shape = (size, 128)
            lane = lax.broadcasted_iota(jnp.int32, shape, 1)
            place = lax.broadcasted_iota(jnp.int32, (8, 128), 1)
            chunks = 2 * len(messages)
            meta = meta_ref[...]
            if p == 0:
                meta = jnp.where(place == 0, member_ref[0], 0)
            for side in range(2):
                at = tokens + side * PAD
                numbers = message[at:at + PAD, :size].astype(F32)[:1]
                column = jnp.broadcast_to(numbers, (128, size)).T.astype(jnp.int32)
                same = (column == lane) & (lane < 4)
                marks = jnp.where(lane < 4, jnp.where(same, 0.0, MASK), jnp.where(lane < 7, -1.0, 0.0))
                key_ref[side * size:(side + 1) * size, :] = marks.astype(BF16)
                if p == 0:
                    query_ref[side * size:(side + 1) * size, :] = jnp.where(same, 1.0, 0.0).astype(BF16)
                slot = 2 * p + side
                meta = jnp.where(place == 1 + slot, column[:1, :], meta)
                meta = jnp.where(place == 1 + chunks + slot, column[size - 1:, :], meta)
            meta_ref[...] = meta


def gather(member, messages, hold=(), after=()):
    tokens, width = messages[0].shape[0] - 2 * PAD, messages[0].shape[1]
    count = len(messages)
    shapes = [
        jax.ShapeDtypeStruct((count * tokens, width), BF16),
        jax.ShapeDtypeStruct((count * tokens, 128), BF16),
        jax.ShapeDtypeStruct((tokens, 128), BF16),
        jax.ShapeDtypeStruct((8, 128), jnp.int32),
    ]
    outs, kept = call(
        gather_kernel, (member,) + tuple(messages),
        [pl.BlockSpec(m.shape, lambda i, s: (0, 0)) for m in messages], shapes,
        [
            pl.BlockSpec((tokens, width), lambda i, s: (i, 0)),
            pl.BlockSpec((tokens, 128), lambda i, s: (i, 0)),
            pl.BlockSpec((tokens, 128), lambda i, s: (0, 0)),
            pl.BlockSpec((8, 128), lambda i, s: (0, 0)),
        ],
        "gather", 1e9, grid=(count,), prefetch=1, hold=hold, after=after)
    return (outs[0], outs[1], outs[2], outs[3][0]), kept


def middle_kernel(x_ref, o_ref, out_ref, gain_ref, query_ref, h_ref, n_ref, c_ref):
    h = x_ref[...].astype(F32) + nn(o_ref[...], out_ref[...])
    h_ref[...] = h
    n_ref[...] = norm(h, gain_ref[...])
    c_ref[...] = nn(n_ref[...], query_ref[...]).astype(BF16) * BF16(0.125)


def back_middle_kernel(dc_ref, query_ref, h_ref, gain_ref, dh_ref, out_ref, dh1_ref, r_ref, do_ref, dgain_ref):
    @pl.when(pl.program_id(0) == 0)
    def _():
        dgain_ref[...] = jnp.zeros_like(dgain_ref)

    back, part = norm_back(h_ref[...], nt(dc_ref[...], query_ref[...]), gain_ref[...])
    dgain_ref[...] += part
    dh1 = dh_ref[...] + back
    dh1_ref[...] = dh1
    r_ref[...] = dh1.astype(BF16)
    do_ref[...] = nt(r_ref[...], out_ref[...]).astype(BF16)


def exit_kernel(dq_ref, query_ref, own_ref, *refs):
    peers = refs[:len(refs) - 8]
    keyvalue_ref, x_ref, gain_ref, dh_ref, dx_a_ref, dx_b_ref, dkv_ref, dgain_ref = refs[len(refs) - 8:]
    half = pl.num_programs(0) // 2

    @pl.when(pl.program_id(0) == 0)
    def _():
        dgain_ref[...] = jnp.zeros_like(dgain_ref)

    sides = [sum((ref[side].astype(F32) for ref in peers), own_ref[side].astype(F32)) for side in range(2)]
    dkv_ref[...] = lanes(sides[0], sides[1]).astype(BF16)
    dn = nt(dq_ref[...], query_ref[...]) + nt(dkv_ref[...], keyvalue_ref[...])
    back, part = norm_back(x_ref[...].astype(F32), dn, gain_ref[...])
    dgain_ref[...] += part
    dx = (dh_ref[...] + back).astype(BF16)

    @pl.when(pl.program_id(0) < half)
    def _():
        dx_a_ref[...] = dx

    @pl.when(pl.program_id(0) >= half)
    def _():
        dx_b_ref[...] = dx


def by_rows(kernel, name, flops, arrays, outs, width, dgain=False, hold=(), after=()):
    tokens = next(x.shape[0] for x, cut in arrays if cut)
    tile = min(256, tokens)
    blocks = pl.BlockSpec((tile, width), lambda i: (i, 0))

    def spec(x, cut):
        if x.ndim == 3:
            return pl.BlockSpec((x.shape[0], tile, x.shape[2]), lambda i: (0, i, 0))
        return blocks if cut else pl.BlockSpec(x.shape, lambda i: (0, 0))

    in_specs = [spec(x, cut) for x, cut in arrays]
    shapes, specs = [], []
    steps = tokens // tile
    for kind in outs:
        if kind == "halves":
            shapes += [jax.ShapeDtypeStruct((tokens // 2, width), BF16)] * 2
            specs += [pl.BlockSpec((tile, width), lambda i: (jnp.minimum(i, steps // 2 - 1), 0)),
                      pl.BlockSpec((tile, width), lambda i: (jnp.maximum(i - steps // 2, 0), 0))]
        else:
            shapes.append(jax.ShapeDtypeStruct((tokens, width), kind))
            specs.append(blocks)
    if dgain:
        shapes.append(jax.ShapeDtypeStruct((8, width), F32))
        specs.append(pl.BlockSpec((8, width), lambda i: (0, 0)))
    return call(kernel, tuple(x for x, _ in arrays), in_specs, shapes, specs, name, flops,
                grid=(tokens // tile,), hold=hold, after=after)


def feed_kernel(rest, h1_ref, co_ref, cross_ref, g_ref, gain_ref, gate_ref, up_ref, down_ref,
                out_a_ref, out_b_ref, n_ref, hidden_ref, dgu_ref, dh_ref, low_ref, dco_ref, dgain_ref,
                out_acc, dn_acc, h_acc):
    size = out_a_ref.shape[0]
    step, steps = pl.program_id(0), pl.num_programs(0)

    @pl.when(step == 0)
    def _():
        h = h1_ref[...] + nn(co_ref[...], cross_ref[...])
        h_acc[...] = h
        n_ref[...] = norm(h, gain_ref[...])
        out_acc[...] = jnp.zeros_like(out_acc)
        dn_acc[...] = jnp.zeros_like(dn_acc)

    def main(tile):
        n = n_ref[...]
        gate = nn(n, gate_ref[:, :tile])
        up = nn(n, up_ref[:, :tile])
        dhidden = nt(g_ref[...], down_ref[:tile, :])
        square = gate * gate
        bend = jnp.tanh(gate * (GELU_A + GELU_B * square))
        half = 0.5 + 0.5 * bend
        gelu = gate * half
        slope = half + gate * (0.5 - 0.5 * bend * bend) * (GELU_A + 3.0 * GELU_B * square)
        hidden = (gelu * up).astype(BF16)
        dgate = (dhidden * up * slope).astype(BF16)
        dup = (dhidden * gelu).astype(BF16)
        hidden_ref[:, :tile] = hidden
        dgu_ref[:, :tile] = dgate
        dgu_ref[:, tile:2 * tile] = dup
        out_acc[...] += nn(hidden, down_ref[:tile, :])
        dn_acc[...] += nt(dgate, gate_ref[:, :tile]) + nt(dup, up_ref[:, :tile])

    tile = gate_ref.shape[1]
    if rest == tile:
        main(tile)
    else:
        pl.when(step < steps - 1)(lambda: main(tile))
        pl.when(step == steps - 1)(lambda: main(rest))

    @pl.when(step == steps - 1)
    def _():
        h = h_acc[...]
        out = (h + out_acc[...]).astype(BF16)
        out_a_ref[...] = out[:size]
        out_b_ref[...] = out[size:]
        back, dgain_ref[...] = norm_back(h, dn_acc[...], gain_ref[...])
        dh = g_ref[...].astype(F32) + back
        dh_ref[...] = dh
        low_ref[...] = dh.astype(BF16)
        dco_ref[...] = nt(low_ref[...], cross_ref[...]).astype(BF16)


def feed_forward(h, co, cross_output, g, gain, feed_gate, feed_up, feed_down, hold=(), after=()):
    tokens, width = h.shape
    hidden = feed_gate.shape[1]
    tile = FEED
    rest = hidden - (hidden - 1) // tile * tile
    whole = pl.BlockSpec((tokens, width), lambda i: (0, 0), pipeline_mode=pl.Buffered(1))
    square = pl.BlockSpec((width, width), lambda i: (0, 0), pipeline_mode=pl.Buffered(1))
    row = pl.BlockSpec((1, width), lambda i: (0, 0))
    low, wide = jax.ShapeDtypeStruct(h.shape, BF16), jax.ShapeDtypeStruct(h.shape, F32)
    chunk = jax.ShapeDtypeStruct((tokens // 2, width), BF16)
    part = pl.BlockSpec(chunk.shape, lambda i: (0, 0), pipeline_mode=pl.Buffered(1))
    return call(
        functools.partial(feed_kernel, rest),
        (h, co, cross_output, g, gain, feed_gate, feed_up, feed_down),
        [
            whole, whole, square, whole, row,
            pl.BlockSpec((width, tile), lambda i: (0, i)),
            pl.BlockSpec((width, tile), lambda i: (0, i)),
            pl.BlockSpec((tile, width), lambda i: (i, 0)),
        ],
        [chunk, chunk, low, jax.ShapeDtypeStruct((tokens, hidden), BF16), jax.ShapeDtypeStruct((tokens, 2 * hidden), BF16),
         wide, low, low, jax.ShapeDtypeStruct((8, width), F32)],
        [part, part, whole, pl.BlockSpec((tokens, tile), lambda i: (0, i)), pl.BlockSpec((tokens, 2 * tile), lambda i: (0, i)),
         whole, whole, whole, pl.BlockSpec((8, width), lambda i: (0, 0))],
        "feed_forward", 45e9, grid=(pl.cdiv(hidden, tile),), hold=hold, after=after,
        scratch=[pltpu.VMEM((tokens, width), F32) for _ in range(3)],
    )


class Group:
    def __init__(self):
        self.S, self.R = lax.axis_size("seq"), lax.axis_size("row")
        self.s, self.r = lax.axis_index("seq"), lax.axis_index("row")
        self.core = self.r % 2
        self.chunks = self.S
        self.members = self.S // 2
        self.member = (self.s // 4) * 2 + self.core
        self.first_half = self.s < self.S // 2
        self.places = [(s, r) for s in range(self.S) for r in range(self.R)]

    def index(self, s, r):
        return s * self.R + r

    def send(self, x, target):
        pairs = [(self.index(s, r), self.index(*target(s, r))) for s, r in self.places]
        return lax.ppermute(x, ("seq", "row"), pairs)

    def route(self, way):
        S = self.S

        def target(s, r):
            second = (s >= S // 2) if way == 0 else (s < S // 2)
            row = 2 * (r % 2) + (1 if second else 0)
            member = min(s, S - 1 - s)
            return (row + 4 * (member // 2), r - r % 2 + member % 2)

        return [(self.index(s, r), self.index(*target(s, r))) for s, r in self.places]

    def part(self, x, way):
        return jnp.where(self.first_half == (way == 0), x[0], x[1])

    def go(self, x, way):
        return lax.ppermute(x, ("seq", "row"), self.route(way))

    def back(self, x, way):
        return lax.ppermute(x, ("seq", "row"), [(t, f) for f, t in self.route(way)])

    def two_rows(self, a, b):
        return jnp.where(self.first_half, a, b), jnp.where(self.first_half, b, a)

    def peer(self, x, distance):
        return self.send(x, lambda s, r: (s ^ (4 * (distance >> 1)), r ^ (distance & 1)))

    def peers(self, x):
        return [x] + [self.peer(x, p) for p in range(1, self.members)]

    def core_swap(self, x):
        return self.send(x, lambda s, r: (s, r ^ 1))

    def sum_axes(self):
        sizes = [("row", self.R), ("seq", self.S)]
        return [(axis, bit) for axis, size in sizes for bit in range(size.bit_length() - 1)]

    def names(self):
        top = self.S.bit_length() - 2
        row_bits = list(range(1, self.R.bit_length() - 1))
        return [("seq", k) for k in reversed(range(top))] + [("row", k) for k in reversed(row_bits)] + [("row", 0)]

    def bits(self):
        values = [((self.s if kind == "seq" else self.r) >> bit) & 1 for kind, bit in self.names()[:-1]]
        return jnp.stack(values + [self.s >> (self.S.bit_length() - 2)]).astype(jnp.int32)

    def swap(self, give, name):
        size = self.S if name[0] == "seq" else self.R
        return lax.ppermute(give, name[0], [(i, i ^ (1 << name[1])) for i in range(size)])

    def last_sends(self, straight, crossed):
        half = self.S // 2
        one = self.send(straight, lambda s, r: ((r % 2) * half + s % half, (r - r % 2) + s // half))
        two = self.send(crossed, lambda s, r: ((r % 2) * half + s % half, (r - r % 2) + 1 - s // half))
        return one, two


    def all_sends(self, pieces):
        half = self.S // 2
        sent = []
        for piece, (low, top) in zip(pieces, self.last_changes()):
            sent.append(self.send(piece, lambda s, r: (
                (r % 2) * half + (s % half ^ low), (r - r % 2) + (s // half ^ top))))
        return sent

    def last_changes(self):
        return [(low, top) for low in range(self.S // 2) for top in range(2)]


def grad_kernel(jobs, blocks, half_ref, *refs):
    inputs = sum(1 + job[-1] for job in jobs)
    out_ref, scratch = refs[inputs], refs[inputs + 1:]
    step = pl.program_id(0)
    place = 0

    def chunks_of(total, rows_in, paired):
        rows_out = -(-rows_in // 16) * 16
        for chunk in range(total.shape[1] // CHUNK):
            block = total[:, chunk * CHUNK:(chunk + 1) * CHUNK].reshape(blocks, rows_in, CHUNK)
            if paired:
                block = block.reshape(-1, 2, 2, 64 // rows_in, rows_in, CHUNK)
                block = jnp.swapaxes(block, 1, 2).reshape(blocks, rows_in, CHUNK)
            if rows_out > rows_in:
                block = jnp.concatenate([block, jnp.zeros((blocks, rows_out - rows_in, CHUNK), F32)], axis=1)
            yield slice(chunk * rows_out, (chunk + 1) * rows_out), block.astype(BF16)

    def direct(left_ref, right_refs, count, rows_in, paired):
        if len(right_refs) == 1:
            right = right_refs[0][:, :count * CHUNK]
        else:
            sides = [sum((ref[n].astype(F32) for ref in right_refs[1:]), right_refs[0][n].astype(F32)) for n in range(2)]
            right = lanes(*sides).astype(BF16)
        for at, block in chunks_of(tn(left_ref[...], right), rows_in, paired):
            out_ref[:, at, :] = block

    for start, full, rest, rows_in, paired, slabs, terms in jobs:
        left_ref, right_refs = refs[place], refs[place + 1:place + 1 + terms]
        right_ref = right_refs[0]
        place += 1 + terms
        if slabs:
            @pl.when(step == start)
            def _(left_ref=left_ref, right_ref=right_ref, rows_in=rows_in, paired=paired):
                for at, block in chunks_of(tn(left_ref[...], right_ref[...]), rows_in, paired):
                    scratch[0][:, at, :] = block

            deep = out_ref.shape[1]
            for slab in range(slabs):
                @pl.when(step == start + slab)
                def _(slab=slab):
                    out_ref[...] = scratch[0][:, slab * deep:(slab + 1) * deep, :]
            continue
        if full:
            run = functools.partial(direct, left_ref, right_refs, 2, rows_in, paired)
            pl.when((step >= start) & (step < start + full))(run)
        if rest:
            run = functools.partial(direct, left_ref, right_refs, 1, rows_in, paired)
            pl.when(step == start + full)(run)


def grad_part(half, pairs, blocks, rows_in, total, first=0, before=None, hold=(), after=(), holds=False):
    rows_out = -(-rows_in // 16) * 16
    jobs, inputs, in_specs, scratch = [], [half], [], []
    start = 0
    for left, right, *more in pairs:
        paired, own_rows = (more + [False, rows_in][len(more):])
        terms = list(right) if isinstance(right, (list, tuple)) else [right]
        full, rest = (1, 0) if len(terms) > 1 else divmod(right.shape[1] // CHUNK, 2)
        tokens, side = left.shape[0], left.shape[1] // 2
        slabs = 0
        steps = full + rest
        if own_rows != rows_in:
            deep = 2 * (-(-own_rows // 16) * 16)
            slabs = steps = deep // (2 * rows_out)
            scratch.append(pltpu.VMEM((blocks, deep, CHUNK), BF16))
            index = lambda i, h: (0, 0)
        else:
            index = lambda i, h, start=start, steps=steps: (0, jnp.clip(i - start, 0, steps - 1))
        jobs.append((start, full, rest, own_rows, bool(paired), slabs, len(terms)))
        inputs += [left] + terms
        in_specs.append(pl.BlockSpec((tokens, side), lambda i, h: (0, h[0])))
        if len(terms) > 1:
            in_specs += [pl.BlockSpec((2, tokens, CHUNK), lambda i, h: (0, 0, 0))] * len(terms)
        else:
            in_specs.append(pl.BlockSpec((tokens, 2 * CHUNK), index))
        start += steps
    kernel, inputs, in_specs, alias = with_before(
        functools.partial(grad_kernel, tuple(jobs), blocks), inputs, in_specs, before)
    (out,), kept = call(
        kernel, inputs, in_specs,
        [jax.ShapeDtypeStruct((blocks, total, CHUNK), BF16)],
        [pl.BlockSpec((blocks, 2 * rows_out, CHUNK), lambda i, h: (0, first + i, 0))],
        "weight_grads", 1e9, grid=(start,), prefetch=1, hold=hold, after=after, alias=alias, scratch=scratch,
    )
    return (out, kept) if holds else out


def stage_kernel(plan, bits_ref, *refs):
    count = max(max(terms) for _, terms, _ in plan) + 1
    for out, terms, at in plan:
        total = sum((refs[t][...].astype(F32) for t in terms[1:]), refs[terms[0]][...].astype(F32))
        refs[count + out][:, at, :] = total.astype(BF16)


def last_kernel(changes, counts, place_ref, *refs):
    inputs, outs = refs[:sum(counts)], refs[sum(counts):]
    for (low, top), out in zip(changes, outs):
        at = 2 * jnp.bitwise_xor(place_ref[0], low) + jnp.bitwise_xor(place_ref[1], top)
        start, first = 0, 0
        for count in counts:
            terms = inputs[start:start + count]
            block = sum((ref[pl.ds(at, 1)].astype(F32) for ref in terms[1:]), terms[0][pl.ds(at, 1)].astype(F32))
            out[first:first + block.shape[1], :] = block[0].astype(BF16)
            start, first = start + count, first + block.shape[1]


def last_stage(group, streams, after=(), hold=()):
    half = group.S // 2
    place = jnp.stack([group.s % half, group.s // half]).astype(jnp.int32)
    changes = group.last_changes()
    terms = [array for stream in streams for array, _, _ in stream.terms]
    shape = jax.ShapeDtypeStruct((sum(stream.rows_in for stream in streams), CHUNK), BF16)
    return call(
        functools.partial(last_kernel, changes, [len(stream.terms) for stream in streams]), (place, *terms),
        [pl.BlockSpec(x.shape, lambda p: (0, 0, 0)) for x in terms],
        [shape] * len(changes), [pl.BlockSpec(shape.shape, lambda p: (0, 0))] * len(changes),
        "last_stage", 1e9, prefetch=1, after=after, hold=hold)


class Stream:
    def __init__(self, terms, names, order, rows_in):
        self.terms, self.names, self.order, self.rows_in = terms, names, list(order), rows_in

    def got(self, array, names):
        self.terms.append((array, names, 0))


def stage(group, bits, streams, keep=True, join=False, after=(), hold=()):
    all_names = group.names()
    inputs, in_specs, shapes, out_specs, plan = [bits], [], [], [], []
    grid = 2 ** (len(streams[0].names) - 1)
    lead = 2 if streams[0].order[0] != all_names[-1] and grid > 1 else 1
    for number, stream in enumerate(streams):
        axis = stream.order[0]
        rest = [name for name in stream.names if name != axis]

        def spec(names, part, give, rest=rest, axis=axis, rows_in=stream.rows_in):
            def place(i, b):
                index = 0
                for name in names if lead == 1 else names[:-1]:
                    own = b[all_names.index(name)]
                    if name == axis:
                        value = 1 - own if give else own
                    elif name in rest:
                        value = (i * lead >> (len(rest) - 1 - rest.index(name))) & 1
                    else:
                        value = own
                    index = index * 2 + value
                return (index, part, 0)

            return pl.BlockSpec((lead, rows_in, CHUNK), place)

        sides = (True, False) if keep else (True,)
        for give in sides:
            terms = []
            for array, names, part in stream.terms:
                terms.append(len(inputs) - 1)
                inputs.append(array)
                in_specs.append(spec(names, part, give))
            count = stream.rows_in
            if join:
                plan.append((0 if give else 1, tuple(terms), slice(number * count, (number + 1) * count)))
            else:
                plan.append((len(shapes), tuple(terms), slice(0, count)))
            if not join or number == 0:
                full = count * (len(streams) if join else 1)
                shapes.append(jax.ShapeDtypeStruct((grid, full, CHUNK), BF16))
                out_specs.append(pl.BlockSpec((lead, full, CHUNK), lambda i, b: (i, 0, 0)))
    return call(functools.partial(stage_kernel, tuple(plan)), tuple(inputs), in_specs, shapes, out_specs, "stage", 1e9,
                grid=(grid // lead,), prefetch=1, after=after, hold=hold)


class Bundle:
    def __init__(self, group, bits):
        self.group, self.bits, self.ends = group, bits, []

    def swap(self, theirs):
        self.other = self.group.core_swap(theirs)

    def begin(self, mine, after=(), hold=()):
        names = self.group.names()
        rows_axes = [name for name in names if name[0] == "row" and name[1]]
        seq_axes = [name for name in names if name[0] == "seq"][::-1]
        half = mine.shape[1] // 2
        self.streams = [
            Stream([(mine, names, n), (self.other, names, n)], names, (rows_axes[::-1], rows_axes)[n] + seq_axes + [("row", 0)], half)
            for n in range(2)
        ]
        self.gives, kept = stage(self.group, self.bits, self.streams, keep=False, after=after, hold=hold)
        self.send()
        return kept

    def send(self):
        self.fly = [self.group.swap(give, s.order[0]) for give, s in zip(self.gives, self.streams)]

    def step(self, after=(), hold=(), direct=False):
        if self.ends:
            return list(hold)
        for stream, got in zip(self.streams, self.fly):
            axis = stream.order.pop(0)
            stream.names = [name for name in stream.names if name != axis]
            stream.got(got, list(stream.names))
        if direct:
            self.gives, kept = last_stage(self.group, self.streams, after=after, hold=hold)
            self.ends = self.group.all_sends(self.gives)
            return kept
        one = self.streams[0]
        join = len(self.streams) == 2 and one.names == self.streams[1].names and one.order == self.streams[1].order
        outs, kept = stage(self.group, self.bits, self.streams, join=join, after=after, hold=hold)
        axis = one.order[0]
        if join:
            self.streams = [Stream([], list(one.names), one.order, 2 * one.rows_in)]
        if axis == ("row", 0):
            crossed, straight = outs
            self.gives = [crossed]
            self.ends = list(self.group.last_sends(straight, crossed))
            return kept
        self.gives = []
        for n, stream in enumerate(self.streams):
            self.gives.append(outs[2 * n])
            rest = [name for name in stream.names if name != stream.order[0]]
            stream.terms = [(outs[2 * n + 1], rest, 0)]
        self.send()
        return kept

    def finish(self):
        while not self.ends:
            self.step()

    def result(self):
        return sum((x.astype(F32) for x in self.ends[1:]), self.ends[0].astype(F32)).reshape(-1, CHUNK)


def by_pairs(weight, axis):
    shape = weight.shape
    split = shape[:axis] + (shape[axis] // 256, 2, 2, 64) + shape[axis + 1:]
    return jnp.swapaxes(weight.reshape(split), axis + 1, axis + 2).reshape(shape)


def bias_rows(bias_table, sub):
    table = by_heads((bias_table - bias_table[BUCKETS - 1:]).T)
    levels = np.array([bucket_level(d) for d in range(2 * NEAR)])
    values = jnp.dot(table, jnp.asarray(np.eye(BUCKETS, dtype=np.float32)[levels].T), precision=HIGHEST)
    near = values[:, :sub] if sub <= 2 * NEAR else jnp.pad(values, ((0, 0), (0, sub - 2 * NEAR)))
    near = jnp.concatenate([near, jnp.full((HEADS, sub), MASK, F32)], axis=1)
    corner = jnp.concatenate([values[:, NEAR:], jnp.zeros((HEADS, 1), F32), values[:, 1:NEAR]], axis=1)
    return [jnp.broadcast_to(a[:, None], (HEADS, 8, a.shape[1])) for a in (near, corner)]


def by_heads(x):
    return jnp.swapaxes(x.reshape((4, 2, 2) + x.shape[1:]), 1, 2).reshape(x.shape)


def bias_table_sums(near, corner):
    def fold(wide, distances):
        matrix = np.zeros((8, wide, BUCKETS), np.float32)
        for row in range(8):
            for lane in range(wide):
                distance = distances((lane - row) % wide)
                if distance is not None:
                    matrix[row, lane, bucket_level(distance)] = 1.0
        return jnp.asarray(matrix.reshape(8 * wide, BUCKETS))

    sub = near.shape[2] // 2
    first = fold(2 * sub, lambda d: d if d < sub else None)
    second = fold(2 * NEAR, lambda d: NEAR + d if d < NEAR else (d - NEAR if d > NEAR else None))
    total = jnp.dot(near.reshape(HEADS, -1), first, precision=HIGHEST)
    total = total + jnp.dot(corner.reshape(HEADS, -1), second, precision=HIGHEST)
    rest = -jnp.sum(total[:, :BUCKETS - 1], axis=1, keepdims=True)
    return by_heads(jnp.concatenate([total[:, :BUCKETS - 1], rest], axis=1)).T


def on_device(tokens, segment_ids, memory, cotangent, gain_attend, gain_cross, gain_feed, bias_table,
              self_query, self_keyvalue, self_output, cross_query, cross_keyvalue, cross_output,
              feed_gate, feed_up, feed_down):
    group = Group()
    size, width = tokens.shape[1:]
    span = memory.shape[1]
    hidden_width = feed_gate.shape[1]
    chunks = group.chunks
    sub = min(256, size)
    bits = group.bits()
    core = group.core.astype(jnp.int32)[None]
    devices = group.S * group.R
    blocks = devices // 2

    def token_part(way):
        numbers = group.part(segment_ids, way).astype(BF16)
        numbers = jnp.pad(numbers[None], ((0, PAD - 1), (0, width - size)))
        return jnp.concatenate([group.part(tokens, way), numbers], axis=0)

    way_a = group.go(token_part(0), 0)
    way_b = group.go(token_part(1), 1)

    memory_rows = memory.reshape(-1, width)
    pairs = nn(memory_rows, cross_keyvalue).astype(BF16).reshape(2, span, width)
    own_query, own_output = by_pairs(self_query, 1), by_pairs(self_output, 0)
    other_query, other_output = by_pairs(cross_query, 1), by_pairs(cross_output, 0)
    near, near_back, corner, corner_back = bias_tiles(*bias_rows(bias_table, sub), sub)
    second = [jnp.concatenate([group.part(cotangent, way), group.part(pairs, way)], axis=0) for way in range(2)]

    (x, n1, message), (second_a,) = entry(
        way_a, way_b, gain_attend[None], self_keyvalue, hold=[second[0]],
        after=[own_query, own_output, other_query, other_output, near, second[1]])
    messages = group.peers(message)
    second_a = group.go(second_a, 0)
    second_b = group.go(second[1], 1)
    (q,), _ = by_rows(query_kernel, "query", 2e9, [(n1, True), (own_query, False)], [BF16], width)
    (kv, key_marks, query_marks, meta), _ = gather(
        (2 * group.member + group.s % 2).astype(jnp.int32)[None], messages, after=[q])
    (o, lse), _ = self_forward(meta, q, kv, query_marks, key_marks, near, corner, chunks, 0, 1, None)
    memory_own, g = unpack(second_a, second_b, size, [o])
    memories = group.peers(memory_own)
    (h1, n2, c), _ = by_rows(
        middle_kernel, "middle", 5e9,
        [(x, True), (o, True), (own_output, False), (gain_cross[None], False), (other_query, False)],
        [F32, BF16, BF16], width, after=[memory_own])
    (co, cross_lse), _ = cross_forward(c, memories)
    (out_a, out_b, n3, hidden, dgu, dh2, r2, dco, dgain_feed), _ = feed_forward(
        h1, co, other_output, g, gain_feed[None], feed_gate, feed_up, feed_down)

    feed_rows = hidden.shape[1] // devices
    if feed_rows % 8:
        padded = -(-feed_rows // 16) * 16
        hidden = jnp.pad(hidden.reshape(-1, devices, feed_rows), ((0, 0), (0, 0), (0, padded - feed_rows)))
        hidden = hidden.reshape(-1, devices * padded)
    down_rows = hidden.shape[1] // devices
    down_out = -(-down_rows // 16) * 16
    square_rows = width // devices
    square_out = -(-square_rows // 16) * 16
    down_total = down_out * (width // CHUNK)
    feed_total = -(-(down_total + square_out * (dgu.shape[1] // CHUNK)) // 32) * 32

    def feed_half(which, after=(), hold=()):
        return grad_part(which, [(hidden, g, False, down_rows), (n3, dgu)], blocks, square_rows, feed_total,
                         after=after, hold=hold, holds=True)

    theirs, (out_b,) = feed_half(1 - core, after=[out_a], hold=[out_b])
    out_a = group.back(out_a, 0)
    feed = Bundle(group, bits)
    feed.swap(theirs)
    mine, (out_b,) = feed_half(core, after=[theirs], hold=[out_b])
    feed.begin(mine)
    out_b = group.back(out_b, 1)

    (dc, dm, *dm_peers), _ = cross_backward(c, dco, co, cross_lse, memories, after=feed.gives)
    (dh1, r1, do, dgain_cross), _ = by_rows(
        back_middle_kernel, "back_middle", 5e9,
        [(dc, True), (other_query, False), (h1, True), (gain_cross[None], False), (dh2, True), (own_output, False)],
        [F32, BF16, BF16], width, dgain=True)
    cross_pairs = [(co, r2, True), (n2, dc), (o, r1, True)]
    cross_total = 3 * square_out * (width // CHUNK)
    theirs, dm_peers = grad_part(
        1 - core, cross_pairs, blocks, square_rows, cross_total, hold=dm_peers, holds=True)
    theirs, out_a, out_b = feed.step(hold=[theirs, out_a, out_b])
    cross = Bundle(group, bits)
    cross.swap(theirs)
    dm_peers = [group.peer(term, p + 1) for p, term in enumerate(dm_peers)]
    mine, (dm,) = grad_part(
        core, cross_pairs, blocks, square_rows, cross_total, after=[theirs] + feed.gives, hold=[dm], holds=True)
    dm_a, dm_b, _ = add_memory([dm] + dm_peers)

    def backward(part, before, after, hold=()):
        return self_backward(meta, q, do, o, lse, kv, query_marks, key_marks, near_back, corner_back, chunks,
                             part, 4, before, after=after, hold=hold)

    back, (dm_b, mine) = backward(0, None, [dm_a, cross.other], [dm_b, mine])
    dm_a = group.back(dm_a, 0)
    dm_a, = feed.step(after=[back[0], mine], hold=[dm_a])
    cross.begin(mine, after=feed.gives)
    back, (dm_b,) = backward(1, back, feed.gives + cross.gives, [dm_b])
    feed.step(after=[back[0]])
    cross.step(after=[back[0]] + feed.gives)
    back, (dm_b,) = backward(2, back, feed.gives + cross.gives, [dm_b])
    feed.finish()
    cross.step(after=[back[0]] + list(feed.ends))
    dm_b = group.back(dm_b, 1)
    back, _ = backward(3, back, cross.gives)
    dq, dkv_own, dkv_peers, near_sum, corner_sum = back
    dm_b, dkv_peers = cross.step(after=[dq], hold=[dm_b, dkv_peers])
    cross.finish()
    dkv_peers = [group.peer(dkv_peers[p - 1], p) for p in range(1, group.members)]
    dm = rows(*group.two_rows(dm_a, dm_b))
    own_total = 3 * square_out * (width // CHUNK)
    step = square_out * (width // CHUNK)
    theirs = grad_part(1 - core, [(n1, dq), (memory_rows, dm)], blocks, square_rows, own_total, after=cross.gives)
    dkv_terms = [dkv_own] + dkv_peers
    theirs = grad_part(1 - core, [(n1, dkv_terms)], blocks, square_rows, own_total, step // square_out, [theirs])
    (token_a, token_b, dkv, dgain_attend), (theirs, *cross.ends) = by_rows(
        exit_kernel, "exit", 5e9,
        [(dq, True), (own_query, False), (dkv_own, True)] + [(y, True) for y in dkv_peers]
        + [(self_keyvalue, False), (x, True), (gain_attend[None], False), (dh1, True)],
        ["halves", BF16], width, dgain=True, hold=[theirs] + list(cross.ends))
    own = Bundle(group, bits)
    own.swap(theirs)
    token_source, token_a = token_a, group.back(token_a, 0)
    mine, (out_a, out_b, token_b, *ends) = grad_part(
        core, [(n1, dq), (memory_rows, dm), (n1, dkv)], blocks, square_rows, own_total,
        after=[token_source], hold=[out_a, out_b, token_b, near_sum, corner_sum, dgain_attend, dgain_cross, dgain_feed, dm], holds=True)
    near_sum, corner_sum, dgain_attend, dgain_cross, dgain_feed, dm_late = ends
    dbias = bias_table_sums(near_sum, corner_sum)
    small = jnp.stack([jnp.sum(dgain_attend, axis=0), jnp.sum(dgain_cross, axis=0), jnp.sum(dgain_feed, axis=0),
                       jnp.pad(dbias.reshape(-1), (0, width - dbias.size))])
    sum_axes = group.sum_axes()

    def small_step(x):
        return x + group.swap(x, sum_axes.pop(0))

    small = small_step(small)
    memory_grad = nt(dm_late, cross_keyvalue).astype(BF16).reshape(memory.shape)
    def squares(bundle, start, columns):
        rest = bundle[start:start + square_out * (columns // CHUNK)].reshape(columns // CHUNK, square_out, CHUNK)
        return jnp.swapaxes(rest[:, :square_rows], 0, 1).reshape(square_rows, columns)

    token_b, token_a, small, *ends = own.begin(
        mine, after=[memory_grad], hold=[token_b, token_a, small, out_a, out_b] + list(feed.ends) + list(cross.ends))
    out_a, out_b, *ends = ends
    count = len(feed.ends)
    feed.ends, cross.ends = ends[:count], ends[count:]
    token_b = group.back(token_b, 1)
    small = small_step(small)
    feed_sum = feed.result()
    grad_dgu = squares(feed_sum, down_total, dgu.shape[1])
    whole = hidden_width // FEED * FEED
    grad_dgu, grad_rest = grad_dgu[:, :2 * whole].reshape(square_rows, -1, 2, FEED), grad_dgu[:, 2 * whole:]
    grad_rest = grad_rest.reshape(square_rows, 2, hidden_width - whole)
    grad_gate, grad_up = [
        jnp.concatenate([grad_dgu[:, :, n].reshape(square_rows, -1), grad_rest[:, n]], axis=1) for n in range(2)]
    grad_down = feed_sum[:down_total].reshape(width // CHUNK, down_out, CHUNK)[:, :feed_rows]
    grad_down = jnp.swapaxes(grad_down, 0, 1).reshape(feed_rows, width)
    token_a, token_b, small, out_a, out_b, *cross.ends = own.step(
        hold=[token_a, token_b, small, out_a, out_b] + list(cross.ends), after=[grad_gate, grad_up, grad_down])
    small = small_step(small)
    tokens_grad = jnp.stack(group.two_rows(token_a, token_b))
    cross_sum = cross.result()
    grad_cross = [squares(cross_sum, n * step, width) for n in range(3)]
    grad_cross[1] = by_pairs(grad_cross[1], 1)
    small, out_a, out_b = own.step(hold=[small, out_a, out_b], after=[tokens_grad] + grad_cross, direct=True)
    layer_output = jnp.stack(group.two_rows(out_a, out_b))
    while sum_axes:
        small = small_step(small)
    own_sum = own.result()
    grad_own = [squares(own_sum, n * step, width) for n in (0, 2, 1)]

    return (
        layer_output,
        tokens_grad,
        memory_grad,
        by_pairs(grad_own[0], 1),
        grad_own[1],
        grad_cross[2],
        grad_cross[1],
        grad_own[2],
        grad_cross[0],
        grad_gate,
        grad_up,
        grad_down,
        small[0],
        small[1],
        small[2],
        small[3, :dbias.size].reshape(dbias.shape),
    )


def solution(mesh):
    data, whole, grads = P("row", "seq", None), P(), P(("seq", "row"), None)
    in_specs = (data, P("row", "seq"), data, data) + (whole,) * 13
    out_specs = (data,) * 3 + (grads,) * 9 + (whole,) * 4
    return jax.shard_map(on_device, mesh=mesh, in_specs=in_specs, out_specs=out_specs, check_vma=False)
```

```python
import functools
import math

import jax
import jax.numpy as jnp
import numpy as np
from jax import lax
from jax.experimental import pallas as pl
from jax.experimental.pallas import tpu as pltpu
from jax.sharding import PartitionSpec as P

HEADS = 16
BUCKETS = 32
MAX_DIST = 128
HIGHEST = lax.Precision.HIGHEST
F32, BF16 = jnp.float32, jnp.bfloat16
MASK = -float(2.0**100)
NEAR = 128
VMEM = 56 * 1024 * 1024
CHUNK = 512
PAD = 16
SELF_SPLIT = 1
SELF_AHEAD = 1
EAGER = True
AHEAD = 3
SPLIT = 2
BACK_SPLIT = 1
FEED = 512
COST = {
    "entry": 6, "query": 6, "gather": 5, "self_forward": 23, "middle": 9, "cross_forward": 20, "feed_forward": 70,
    "weight_grads": 9, "stage": 4, "cross_backward": 31, "back_middle": 12, "self_backward": 18, "exit": 11,
}
COST_SCALE = 0.001e9
GELU_A = math.sqrt(2.0 / math.pi)
GELU_B = GELU_A * 0.044715


def bucket_level(distance):
    exact_part = BUCKETS // 2
    if distance < exact_part:
        return distance
    which_bucket = exact_part + math.floor(
        math.log(distance / exact_part) / math.log(MAX_DIST / exact_part) * (BUCKETS - exact_part)
    )
    return min(BUCKETS - 1, which_bucket)


def call(kernel, inputs, in_specs, out_shape, out_specs, name, flops, grid=(), scratch=(), prefetch=0,
         hold=(), after=(), alias=None):
    hold, after = list(hold), list(after)
    count_in, count_out = len(inputs), len(out_shape)
    anywhere = pl.BlockSpec(memory_space=pl.ANY)

    def body(*refs):
        kept = count_in + len(hold) + len(after)
        kernel(*refs[:count_in], *refs[kept:kept + count_out], *refs[kept + count_out + len(hold):])

    aliases = {count_in + i: count_out + i for i in range(len(hold))}
    aliases.update(alias or {})
    outs = pl.pallas_call(
        body,
        grid_spec=pltpu.PrefetchScalarGridSpec(
            num_scalar_prefetch=prefetch,
            grid=grid,
            in_specs=list(in_specs) + [anywhere] * (len(hold) + len(after)),
            out_specs=list(out_specs) + [anywhere] * len(hold),
            scratch_shapes=list(scratch),
        ),
        out_shape=list(out_shape) + [jax.ShapeDtypeStruct(x.shape, x.dtype) for x in hold],
        input_output_aliases=aliases,
        compiler_params=pltpu.CompilerParams(vmem_limit_bytes=VMEM),
        cost_estimate=pl.CostEstimate(flops=int(COST.get(name, 5) * COST_SCALE), bytes_accessed=10**4, transcendentals=0),
        name=name,
    )(*inputs, *hold, *after)
    return list(outs[:count_out]), list(outs[count_out:])


def nt(a, b):
    return lax.dot_general(a, b, (((1,), (1,)), ((), ())), preferred_element_type=F32)


def nn(a, b):
    return jnp.dot(a, b, preferred_element_type=F32)


def tn(a, b):
    return lax.dot_general(a, b, (((0,), (0,)), ((), ())), preferred_element_type=F32)


def halves(block):
    low = lax.broadcasted_iota(jnp.int32, block.shape, 1) < 64
    zero = jnp.zeros_like(block)
    return jnp.where(low, block, zero), jnp.where(low, zero, block)


def lanes(a, b):
    return jnp.concatenate([a, b], axis=1)


def rows(a, b):
    return jnp.concatenate([a, b], axis=0)


def chunk_of(member, part, chunks):
    high = jnp.bitwise_xor(part, member % 2)
    return jnp.where(high == 0, member // 2, chunks - 1 - member // 2)


def slot_of(member, chunk, chunks):
    high = (chunk >= chunks // 2).astype(jnp.int32)
    other = jnp.where(chunk >= chunks // 2, chunks - 1 - chunk, chunk)
    return 2 * jnp.bitwise_xor(other, member // 2) + jnp.bitwise_xor(high, member % 2)


def first_block(meta, member, chunk, chunks):
    mine = meta[1 + slot_of(member, chunk, chunks)]

    def skip(block, start):
        last = meta[1 + chunks + slot_of(member, block, chunks)]
        return start + jnp.where((block < chunk) & (last < mine), 1, 0)

    return lax.fori_loop(0, chunks, skip, jnp.int32(0))


def in_turn(count, ahead, issue, process):
    waiting = [issue(i) for i in range(min(ahead, count))]
    for i in range(count):
        if i + ahead < count:
            waiting.append(issue(i + ahead))
        process(i, waiting.pop(0))


def self_forward_kernel(chunks, sub, meta, q_ref, k_ref, v_ref, qf_ref, kf_ref, near_ref, corner_ref,
                        o_ref, lse_ref, acc_ref, m_ref):
    size = q_ref.shape[0]
    member = meta[0]
    chunk = chunk_of(member, pl.program_id(1), chunks)
    q_both = [lanes(part, qf_ref[...]) for part in halves(q_ref[...])]

    def values(at, length):
        low, high = halves(v_ref[pl.ds(at, length), :])
        one_low, one_high = halves(jnp.ones((length, 128), BF16))
        return rows(lanes(low, one_low), lanes(high, one_high))

    own = pl.multiple_of(slot_of(member, chunk, chunks) * size, size)
    chains = [(strip, head) for strip in range(size // sub) for head in range(2)]
    weights = {}

    def near_issue(i):
        strip, head = chains[i]
        span = (strip + 1) * sub
        return nt(q_both[head][strip * sub:span], lanes(k_ref[pl.ds(own, span), :], kf_ref[pl.ds(own, span), :]))

    def near_process(i, s):
        strip, head = chains[i]
        span = (strip + 1) * sub
        here = slice(strip * sub, span)
        last = s[:, span - sub:] + near_ref[head]
        if strip:
            edge = s[:, span - sub - NEAR:span - sub]
            edge = rows(edge[:NEAR] + corner_ref[head], edge[NEAR:])
            s = jnp.concatenate([s[:, :span - sub - NEAR], edge, last], axis=1)
        else:
            s = last
        top = jnp.max(s, axis=1, keepdims=True)
        m_ref[head, here, :] = jnp.broadcast_to(top, (sub, 128))
        weights[head] = jnp.exp(s - top).astype(BF16)
        if head:
            acc_ref[here, :] = nn(lanes(weights[0], weights[1]), values(own, span))

    in_turn(len(chains), AHEAD, near_issue, near_process)

    def far(block, carry):
        at = pl.multiple_of(slot_of(member, block, chunks) * size, size)
        keys = lanes(k_ref[pl.ds(at, size), :], kf_ref[pl.ds(at, size), :])
        vals = values(at, size)
        flag = jnp.where(block == chunk - 1, 1.0, 0.0).astype(F32)
        part = size // SPLIT
        chains = [(piece, head) for piece in range(SPLIT) for head in range(2)]
        weights, scales = {}, {}

        def issue(i):
            piece, head = chains[i]
            return nt(q_both[head][piece * part:(piece + 1) * part], keys)

        def process(i, s):
            piece, head = chains[i]
            here = slice(piece * part, (piece + 1) * part)
            if piece == 0:
                edge = s[:NEAR, size - NEAR:] + corner_ref[head] * flag
                edge = lanes(s[:NEAR, :size - NEAR], edge)
                s = rows(edge, s[NEAR:]) if part > NEAR else edge
            old = m_ref[head, here, :]
            top = jnp.maximum(old, jnp.max(s, axis=1, keepdims=True))
            scales[head] = jnp.exp(old - top)
            m_ref[head, here, :] = top
            weights[head] = jnp.exp(s - top[:, :1]).astype(BF16)
            if head:
                low = lax.broadcasted_iota(jnp.int32, (part, 128), 1) < 64
                scale = jnp.where(low, scales[0], scales[1])
                acc_ref[here, :] = acc_ref[here, :] * lanes(scale, scale) + nn(lanes(weights[0], weights[1]), vals)

        in_turn(len(chains), AHEAD, issue, process)
        return carry

    lax.fori_loop(first_block(meta, member, chunk, chunks), chunk, far, 0)
    low = lax.broadcasted_iota(jnp.int32, (size, 128), 1) < 64
    total = acc_ref[:, 128:]
    o_ref[...] = (acc_ref[:, :128] / total).astype(BF16)
    lse_ref[...] = jnp.where(low, m_ref[0], m_ref[1]) + jnp.log(total)


def pieces(column, shape):
    lane = lax.broadcasted_iota(jnp.int32, shape, 1)
    high = column.astype(BF16).astype(F32)
    rest = column - high
    middle = rest.astype(BF16).astype(F32)
    low = rest - middle
    full = jnp.where(lane == 4, high, jnp.where(lane == 5, middle, jnp.where(lane == 6, low, 0.0)))
    return full.astype(BF16)


def back_operands(q_ref, do_ref, o_ref, lse_ref, qf):
    shape = q_ref.shape
    q_both = halves(q_ref[...])
    do_both = halves(do_ref[...])
    product = do_ref[...].astype(F32) * o_ref[...].astype(F32)
    low = lax.broadcasted_iota(jnp.int32, shape, 1) < 64
    deltas = [jnp.sum(jnp.where(low, product, 0.0), axis=1, keepdims=True),
              jnp.sum(jnp.where(low, 0.0, product), axis=1, keepdims=True)]
    logs = [lse_ref[:, 0:1], lse_ref[:, 64:65]]
    extra = [pieces(log, shape) for log in logs]
    if qf is not None:
        extra = [part + qf for part in extra]
    q_wide = [lanes(part, more) for part, more in zip(q_both, extra)]
    do_wide = [lanes(part, pieces(delta, shape)) for part, delta in zip(do_both, deltas)]
    return q_both, do_both, q_wide, do_wide


def diagonal_sums(block):
    count, wide = block.shape[0], 2 * block.shape[1]
    block = lanes(block, jnp.zeros_like(block))
    while count > 8:
        count = count // 2
        block = block[:count] + pltpu.roll(block[count:], wide - count, 1)
    return block


def self_backward_kernel(chunks, sub, meta, q_ref, do_ref, o_ref, lse_ref, k_ref, v_ref, qf_ref, kf_ref,
                         near_ref, corner_ref, dq_ref, own_ref, peer_ref, near_out, corner_out,
                         dq_acc, dk_acc, dv_acc, near_acc, corner_acc):
    size = q_ref.shape[0]
    member = meta[0]
    chunk = chunk_of(member, pl.program_id(2), chunks)
    first = (pl.program_id(1) == 0) & (pl.program_id(2) == 0)
    last = (pl.program_id(1) == 1) & (pl.program_id(2) == 1)

    @pl.when(first)
    def _():
        dk_acc[...] = jnp.zeros_like(dk_acc)
        dv_acc[...] = jnp.zeros_like(dv_acc)

    @pl.when(pl.program_id(2) == 0)
    def _():
        near_acc[...] = jnp.zeros_like(near_acc)
        corner_acc[...] = jnp.zeros_like(corner_acc)

    q_both, do_both, q_wide, do_wide = back_operands(q_ref, do_ref, o_ref, lse_ref, qf_ref[...])
    own = pl.multiple_of(slot_of(member, chunk, chunks) * size, size)
    dq_acc[...] = jnp.zeros_like(dq_acc)

    def add(at, length, here, weights, grads, keys):
        dv_acc[pl.ds(at, length), :] += nn(lanes(*weights), rows(do_both[0][here], do_both[1][here]))
        dk_acc[pl.ds(at, length), :] += nn(lanes(*grads), rows(q_both[0][here], q_both[1][here]))
        dq_acc[here, :] += tn(rows(*grads), rows(*halves(keys)))

    for strip in range(size // sub):
        at = pl.multiple_of(own + strip * sub, sub)
        here = slice(strip * sub, size)
        k, v, kf = (ref[pl.ds(at, sub), :] for ref in (k_ref, v_ref, kf_ref))
        keys, vals = lanes(k, kf), lanes(v, kf)
        weights, grads = [], []
        for head in range(2):
            s = nt(keys, q_wide[head][here])
            dp = nt(vals, do_wide[head][here])
            block = s[:, :sub] + near_ref[head]
            more = (strip + 1) * sub < size
            if more:
                edge = s[sub - NEAR:, sub:sub + NEAR] + corner_ref[head]
                rest = s[:, sub:]
                rest = rows(rest[:sub - NEAR], lanes(edge, rest[sub - NEAR:, NEAR:]))
                s = lanes(block, rest)
            else:
                s = block
            p = jnp.exp(s)
            ds = p * dp
            near_acc[head] += ds[:, :sub]
            if more:
                corner_acc[head] += ds[sub - NEAR:, sub:sub + NEAR]
            weights.append(p.astype(BF16))
            grads.append(ds.astype(BF16))
        add(at, sub, here, weights, grads, k)

    def far(block, carry):
        at = pl.multiple_of(slot_of(member, block, chunks) * size, size)
        k, v, kf = (ref[pl.ds(at, size), :] for ref in (k_ref, v_ref, kf_ref))
        keys, vals = lanes(k, kf), lanes(v, kf)
        flag = jnp.where(block == chunk - 1, 1.0, 0.0).astype(F32)
        part = size // SELF_SPLIT
        chains = [(piece, head) for piece in range(SELF_SPLIT) for head in range(2)]
        weights, grads = {}, {}

        def issue(i):
            piece, head = chains[i]
            here = slice(piece * part, (piece + 1) * part)
            return nt(keys, q_wide[head][here]), nt(vals, do_wide[head][here])

        def process(i, products):
            piece, head = chains[i]
            s, dp = products
            if piece == 0:
                edge = s[size - NEAR:, :NEAR] + corner_ref[head] * flag
                edge = lanes(edge, s[size - NEAR:, NEAR:]) if part > NEAR else edge
                s = rows(s[:size - NEAR], edge)
            p = jnp.exp(s)
            ds = p * dp
            if piece == 0:
                corner_acc[head] += ds[size - NEAR:, :NEAR] * flag
            weights[head] = p.astype(BF16)
            grads[head] = ds.astype(BF16)
            if head and (SELF_SPLIT == 1 or EAGER):
                add(at, size, slice(piece * part, (piece + 1) * part), [weights[0], weights[1]], [grads[0], grads[1]], k)

        in_turn(len(chains), SELF_AHEAD, issue, process)
        return carry

    lax.fori_loop(first_block(meta, member, chunk, chunks), chunk, far, 0)
    dq_ref[...] = (dq_acc[...] * 0.125).astype(BF16)

    @pl.when(last)
    def _():
        for side, acc in enumerate((dk_acc, dv_acc)):
            own_ref[side] = acc[: 2 * size, :].astype(BF16)
            for other in range(peer_ref.shape[0]):
                at = 2 * size * (other + 1)
                peer_ref[other, side] = acc[at:at + 2 * size, :].astype(BF16)

    @pl.when(pl.program_id(2) == 1)
    def _():
        for head in range(2):
            near_out[head] = diagonal_sums(near_acc[head])
            corner_out[head] = diagonal_sums(corner_acc[head])


def with_before(kernel, inputs, in_specs, before):
    if before is None:
        return kernel, tuple(inputs), list(in_specs), None
    count = len(inputs)

    def body(*refs):
        kernel(*refs[:count], *refs[count + len(before):])

    specs = list(in_specs) + [pl.BlockSpec(memory_space=pl.ANY)] * len(before)
    return body, tuple(inputs) + tuple(before), specs, {count + i: i for i in range(len(before))}


def self_forward(meta, q, kv, qf, kf, near, corner, chunks, part, parts, before, hold=(), after=()):
    size = q.shape[0] // 2
    sub = min(256, size)
    length = kv.shape[0]
    blocks = 8 // parts
    shift = blocks * part
    own = pl.BlockSpec((size, 128), lambda b, c, m: (c, b + shift))
    kernel, inputs, in_specs, alias = with_before(
        functools.partial(self_forward_kernel, chunks, sub),
        (meta, q, kv, kv, qf, kf, near, corner),
        [
            own,
            pl.BlockSpec((length, 128), lambda b, c, m: (0, (b + shift) // 2)),
            pl.BlockSpec((length, 128), lambda b, c, m: (0, 4 + (b + shift) // 2)),
            pl.BlockSpec((size, 128), lambda b, c, m: (c, 0)),
            pl.BlockSpec((length, 128), lambda b, c, m: (0, 0)),
            pl.BlockSpec((2, sub, sub), lambda b, c, m: (b + shift, 0, 0)),
            pl.BlockSpec((2, NEAR, NEAR), lambda b, c, m: (b + shift, 0, 0)),
        ], before)
    return call(
        kernel, inputs, in_specs,
        [jax.ShapeDtypeStruct(q.shape, BF16), jax.ShapeDtypeStruct(q.shape, F32)],
        [own, own],
        "self_forward", 4e10 / parts, grid=(blocks, 2), prefetch=1, hold=hold, after=after, alias=alias,
        scratch=[pltpu.VMEM((size, 256), F32), pltpu.VMEM((2, size, 128), F32)],
    )


def self_backward(meta, q, do, o, lse, kv, qf, kf, near, corner, chunks, part, parts, before, hold=(), after=()):
    pairs = 4 // parts
    shift = pairs * part
    size = q.shape[0] // 2
    sub = min(256, size)
    length = kv.shape[0]
    own = pl.BlockSpec((size, 128), lambda g, b, c, m: (c, 2 * (g + shift) + b))
    inputs = [meta, q, do, o, lse, kv, kv, qf, kf, near, corner]
    in_specs = [
        own, own, own, own,
        pl.BlockSpec((length, 128), lambda g, b, c, m: (0, g + shift)),
        pl.BlockSpec((length, 128), lambda g, b, c, m: (0, 4 + g + shift)),
        pl.BlockSpec((size, 128), lambda g, b, c, m: (c, 0)),
        pl.BlockSpec((length, 128), lambda g, b, c, m: (0, 0)),
        pl.BlockSpec((2, sub, sub), lambda g, b, c, m: (2 * (g + shift) + b, 0, 0)),
        pl.BlockSpec((2, NEAR, NEAR), lambda g, b, c, m: (2 * (g + shift) + b, 0, 0)),
    ]
    kernel, inputs, in_specs, alias = with_before(
        functools.partial(self_backward_kernel, chunks, sub), inputs, in_specs, before)
    others = length // (2 * size) - 1
    return call(
        kernel, inputs, in_specs,
        [
            jax.ShapeDtypeStruct(q.shape, BF16),
            jax.ShapeDtypeStruct((2, 2 * size, 512), BF16),
            jax.ShapeDtypeStruct((others, 2, 2 * size, 512), BF16),
            jax.ShapeDtypeStruct((16, 8, 2 * sub), F32),
            jax.ShapeDtypeStruct((16, 8, 2 * NEAR), F32),
        ],
        [
            own,
            pl.BlockSpec((2, 2 * size, 128), lambda g, b, c, m: (0, 0, g + shift)),
            pl.BlockSpec((others, 2, 2 * size, 128), lambda g, b, c, m: (0, 0, 0, g + shift)),
            pl.BlockSpec((2, 8, 2 * sub), lambda g, b, c, m: (2 * (g + shift) + b, 0, 0)),
            pl.BlockSpec((2, 8, 2 * NEAR), lambda g, b, c, m: (2 * (g + shift) + b, 0, 0)),
        ],
        "self_backward", 6e10 / parts, grid=(pairs, 2, 2), prefetch=1, hold=hold, after=after, alias=alias,
        scratch=[
            pltpu.VMEM((size, 128), F32),
            pltpu.VMEM((length, 128), F32),
            pltpu.VMEM((length, 128), F32),
            pltpu.VMEM((2, sub, sub), F32),
            pltpu.VMEM((2, NEAR, NEAR), F32),
        ],
    )


def stacked(refs):
    return refs[0][...] if len(refs) == 1 else jnp.concatenate([ref[...] for ref in refs], axis=0)


def cross_forward_kernel(count, q_ref, *refs):
    keys, v = stacked(refs[:count]), stacked(refs[count:2 * count])
    o_ref, lse_ref = refs[2 * count:]
    length = keys.shape[0]
    low, high = halves(v)
    one_low, one_high = halves(jnp.ones((length, 128), BF16))
    values = rows(lanes(low, one_low), lanes(high, one_high))
    q_both = halves(q_ref[...])
    part = q_ref.shape[0] // SPLIT
    chains = [(piece, head) for piece in range(SPLIT) for head in range(2)]
    weights, tops = {}, {}

    def issue(i):
        piece, head = chains[i]
        return nt(q_both[head][piece * part:(piece + 1) * part], keys)

    def process(i, s):
        piece, head = chains[i]
        tops[head] = jnp.max(s, axis=1, keepdims=True)
        weights[head] = jnp.exp(s - tops[head]).astype(BF16)
        if head:
            here = slice(piece * part, (piece + 1) * part)
            acc = nn(lanes(weights[0], weights[1]), values)
            is_low = lax.broadcasted_iota(jnp.int32, (part, 128), 1) < 64
            total = acc[:, 128:]
            o_ref[here, :] = (acc[:, :128] / total).astype(BF16)
            lse_ref[here, :] = jnp.where(is_low, tops[0], tops[1]) + jnp.log(total)

    in_turn(len(chains), AHEAD, issue, process)


def cross_backward_kernel(count, q_ref, do_ref, o_ref, lse_ref, *refs):
    k, v = stacked(refs[:count]), stacked(refs[count:2 * count])
    dq_ref, dkv_refs, (dk_acc, dv_acc) = refs[2 * count], refs[2 * count + 1:3 * count + 1], refs[3 * count + 1:]
    first = (pl.program_id(1) == 0) & (pl.program_id(2) == 0)
    last = (pl.program_id(1) == 1) & (pl.program_id(2) == 1)

    @pl.when(first)
    def _():
        dk_acc[...] = jnp.zeros_like(dk_acc)
        dv_acc[...] = jnp.zeros_like(dv_acc)

    q_both, do_both, q_wide, do_wide = back_operands(q_ref, do_ref, o_ref, lse_ref, None)
    lane = lax.broadcasted_iota(jnp.int32, k.shape, 1)
    minus = jnp.where((lane >= 4) & (lane < 7), -1.0, 0.0).astype(BF16)
    keys, vals = lanes(k, minus), lanes(v, minus)
    size = q_ref.shape[0] // BACK_SPLIT
    chains = [(piece, head) for piece in range(BACK_SPLIT) for head in range(2)]
    weights, grads = {}, {}

    def issue(i):
        piece, head = chains[i]
        here = slice(piece * size, (piece + 1) * size)
        return nt(keys, q_wide[head][here]), nt(vals, do_wide[head][here])

    def process(i, products):
        head = chains[i][1]
        p = jnp.exp(products[0])
        weights[chains[i]] = p.astype(BF16)
        grads[chains[i]] = (p * products[1]).astype(BF16)

    in_turn(len(chains), AHEAD, issue, process)

    def both(x):
        return jnp.concatenate([x[piece, head] for head in range(2) for piece in range(BACK_SPLIT)], axis=1)

    dv_acc[...] += nn(both(weights), rows(*do_both))
    dk_acc[...] += nn(both(grads), rows(*q_both))
    for piece in range(BACK_SPLIT):
        here = slice(piece * size, (piece + 1) * size)
        dq_ref[here, :] = (tn(rows(grads[piece, 0], grads[piece, 1]), rows(*halves(k))) * 0.125).astype(BF16)

    @pl.when(last)
    def _():
        part = dk_acc.shape[0] // count
        for number, ref in enumerate(dkv_refs):
            at = slice(number * part, (number + 1) * part)
            ref[0] = dk_acc[at, :].astype(BF16)
            ref[1] = dv_acc[at, :].astype(BF16)


def cross_forward(q, memories, hold=(), after=()):
    size, part, count = q.shape[0] // 2, memories[0].shape[0], len(memories)
    own = pl.BlockSpec((size, 128), lambda b, c: (c, b))
    return call(
        functools.partial(cross_forward_kernel, count), (q, *memories, *memories),
        [own] + [pl.BlockSpec((part, 128), lambda b, c: (0, b // 2))] * count
        + [pl.BlockSpec((part, 128), lambda b, c: (0, 4 + b // 2))] * count,
        [jax.ShapeDtypeStruct(q.shape, BF16), jax.ShapeDtypeStruct(q.shape, F32)],
        [own, own],
        "cross_forward", 15e9, grid=(8, 2), hold=hold, after=after,
    )


def cross_backward(q, do, o, lse, memories, hold=(), after=()):
    size, part, count = q.shape[0] // 2, memories[0].shape[0], len(memories)
    own = pl.BlockSpec((size, 128), lambda g, b, c: (c, 2 * g + b))
    return call(
        functools.partial(cross_backward_kernel, count), (q, do, o, lse, *memories, *memories),
        [own, own, own, own] + [pl.BlockSpec((part, 128), lambda g, b, c: (0, g))] * count
        + [pl.BlockSpec((part, 128), lambda g, b, c: (0, 4 + g))] * count,
        [jax.ShapeDtypeStruct(q.shape, BF16)] + [jax.ShapeDtypeStruct((2, part, 512), BF16)] * count,
        [own] + [pl.BlockSpec((2, part, 128), lambda g, b, c: (0, 0, g))] * count,
        "cross_backward", 30e9, grid=(4, 2, 2), hold=hold, after=after,
        scratch=[pltpu.VMEM((part * count, 128), F32), pltpu.VMEM((part * count, 128), F32)],
    )


def add_kernel(*refs):
    terms, outs = refs[:-2], refs[-2:]
    for number, out in enumerate(outs):
        at = slice(number * out.shape[0], (number + 1) * out.shape[0])
        sides = [sum((ref[side, at, :].astype(F32) for ref in terms[1:]), terms[0][side, at, :].astype(F32)) for side in range(2)]
        out[...] = lanes(*sides).astype(BF16)


def add_memory(terms, hold=(), after=()):
    shape = jax.ShapeDtypeStruct((terms[0].shape[1] // 2, 2 * terms[0].shape[2]), BF16)
    (low, high), kept = call(
        add_kernel, tuple(terms), [pl.BlockSpec(x.shape, lambda: (0, 0, 0)) for x in terms],
        [shape] * 2, [pl.BlockSpec(shape.shape, lambda: (0, 0))] * 2, "add_memory", 1e9, hold=hold, after=after)
    return low, high, kept


def bias_kernel(sub, near_ref, corner_ref, near_out, back_out, corner_out, corner_back):
    for head in range(2):
        wide = jnp.broadcast_to(near_ref[head, :1], (sub, 2 * sub))
        block = pltpu.roll(wide, 0, 1, stride=1, stride_axis=0)[:, :sub]
        back_out[head] = block
        near_out[head] = block.T
        wide = jnp.broadcast_to(corner_ref[head, :1], (NEAR, 2 * NEAR))
        block = pltpu.roll(wide, 0, 1, stride=1, stride_axis=0)[:, :NEAR]
        corner_back[head] = block
        corner_out[head] = block.T


def bias_tiles(near, corner, sub):
    def spec(a, b):
        return pl.BlockSpec((2, a, b), lambda h: (h, 0, 0))

    def shape(a):
        return jax.ShapeDtypeStruct((16, a, a), F32)

    return pl.pallas_call(
        functools.partial(bias_kernel, sub),
        grid=(8,),
        in_specs=[spec(8, 2 * sub), spec(8, 2 * NEAR)],
        out_specs=[spec(sub, sub), spec(sub, sub), spec(NEAR, NEAR), spec(NEAR, NEAR)],
        out_shape=[shape(sub), shape(sub), shape(NEAR), shape(NEAR)],
        compiler_params=pltpu.CompilerParams(vmem_limit_bytes=VMEM),
        name="bias_tiles",
    )(near, corner)


def inverse_rms(h):
    return lax.rsqrt(jnp.mean(h * h, axis=1, keepdims=True) + 1e-06)


def norm(values, gain):
    return (values * inverse_rms(values) * gain).astype(BF16)


def norm_back(h, dn, gain):
    scale = inverse_rms(h)
    unit = h * scale
    spread = dn * unit
    share = jnp.mean(spread * gain, axis=1, keepdims=True)
    gain_part = jnp.sum(spread.reshape(-1, 8, spread.shape[1]), axis=0)
    return scale * (dn * gain - unit * share), gain_part


def entry_kernel(a_ref, b_ref, gain_ref, weight_ref, x_ref, n_ref, message_ref):
    tokens = x_ref.shape[0]
    size = tokens // 2
    tile = min(256, size)
    for side, ref in enumerate((a_ref, b_ref)):
        for i in range(size // tile):
            at = slice(side * size + i * tile, side * size + (i + 1) * tile)
            x = ref[i * tile:(i + 1) * tile, :]
            x_ref[at, :] = x
            n_ref[at, :] = norm(x.astype(F32), gain_ref[...])
            message_ref[at, :] = nn(n_ref[at, :], weight_ref[...]).astype(BF16)
        message_ref[tokens + side * PAD:tokens + (side + 1) * PAD, :] = ref[size:, :]


def entry(way_a, way_b, gain, weight, hold=(), after=()):
    tokens, width = 2 * (way_a.shape[0] - PAD), way_a.shape[1]
    inputs = (way_a, way_b, gain, weight)
    shapes = [jax.ShapeDtypeStruct((count, width), BF16) for count in (tokens, tokens, tokens + 2 * PAD)]
    return call(entry_kernel, inputs, [pl.BlockSpec(y.shape, lambda: (0, 0)) for y in inputs], shapes,
                [pl.BlockSpec(s.shape, lambda: (0, 0)) for s in shapes], "entry", 2e9, hold=hold, after=after)


def unpack_kernel(a_ref, b_ref, memory_ref, g_ref):
    span, size = memory_ref.shape[0] // 2, g_ref.shape[0] // 2
    for side, ref in enumerate((a_ref, b_ref)):
        g_ref[side * size:(side + 1) * size, :] = ref[:size, :]
        memory_ref[side * span:(side + 1) * span, :] = ref[size:, :]


def unpack(second_a, second_b, size, after):
    count, width = second_a.shape
    whole = pl.BlockSpec((count, width), lambda: (0, 0))
    shapes = [jax.ShapeDtypeStruct((2 * (count - size), width), BF16), jax.ShapeDtypeStruct((2 * size, width), BF16)]
    outs, _ = call(unpack_kernel, (second_a, second_b), [whole, whole], shapes,
                   [pl.BlockSpec(s.shape, lambda: (0, 0)) for s in shapes], "unpack", 1e9, after=after)
    return outs


def query_kernel(n_ref, weight_ref, q_ref):
    q_ref[...] = nn(n_ref[...], weight_ref[...]).astype(BF16) * BF16(0.125)


def gather_kernel(member_ref, *refs):
    messages = refs[:len(refs) - 4]
    kv_ref, key_ref, query_ref, meta_ref = refs[len(refs) - 4:]
    step = pl.program_id(0)
    tokens = messages[0].shape[0] - 2 * PAD
    size = tokens // 2
    for p, message in enumerate(messages):
        @pl.when(step == p)
        def _(p=p, message=message):
            kv_ref[...] = message[:tokens, :]
            shape = (size, 128)
            lane = lax.broadcasted_iota(jnp.int32, shape, 1)
            place = lax.broadcasted_iota(jnp.int32, (8, 128), 1)
            chunks = 2 * len(messages)
            meta = meta_ref[...]
            if p == 0:
                meta = jnp.where(place == 0, member_ref[0], 0)
            for side in range(2):
                at = tokens + side * PAD
                numbers = message[at:at + PAD, :size].astype(F32)[:1]
                column = jnp.broadcast_to(numbers, (128, size)).T.astype(jnp.int32)
                same = (column == lane) & (lane < 4)
                marks = jnp.where(lane < 4, jnp.where(same, 0.0, MASK), jnp.where(lane < 7, -1.0, 0.0))
                key_ref[side * size:(side + 1) * size, :] = marks.astype(BF16)
                if p == 0:
                    query_ref[side * size:(side + 1) * size, :] = jnp.where(same, 1.0, 0.0).astype(BF16)
                slot = 2 * p + side
                meta = jnp.where(place == 1 + slot, column[:1, :], meta)
                meta = jnp.where(place == 1 + chunks + slot, column[size - 1:, :], meta)
            meta_ref[...] = meta


def gather(member, messages, hold=(), after=()):
    tokens, width = messages[0].shape[0] - 2 * PAD, messages[0].shape[1]
    count = len(messages)
    shapes = [
        jax.ShapeDtypeStruct((count * tokens, width), BF16),
        jax.ShapeDtypeStruct((count * tokens, 128), BF16),
        jax.ShapeDtypeStruct((tokens, 128), BF16),
        jax.ShapeDtypeStruct((8, 128), jnp.int32),
    ]
    outs, kept = call(
        gather_kernel, (member,) + tuple(messages),
        [pl.BlockSpec(m.shape, lambda i, s: (0, 0)) for m in messages], shapes,
        [
            pl.BlockSpec((tokens, width), lambda i, s: (i, 0)),
            pl.BlockSpec((tokens, 128), lambda i, s: (i, 0)),
            pl.BlockSpec((tokens, 128), lambda i, s: (0, 0)),
            pl.BlockSpec((8, 128), lambda i, s: (0, 0)),
        ],
        "gather", 1e9, grid=(count,), prefetch=1, hold=hold, after=after)
    return (outs[0], outs[1], outs[2], outs[3][0]), kept


def middle_kernel(x_ref, o_ref, out_ref, gain_ref, query_ref, h_ref, n_ref, c_ref):
    h = x_ref[...].astype(F32) + nn(o_ref[...], out_ref[...])
    h_ref[...] = h
    n_ref[...] = norm(h, gain_ref[...])
    c_ref[...] = nn(n_ref[...], query_ref[...]).astype(BF16) * BF16(0.125)


def back_middle_kernel(dc_ref, query_ref, h_ref, gain_ref, dh_ref, out_ref, dh1_ref, r_ref, do_ref, dgain_ref):
    @pl.when(pl.program_id(0) == 0)
    def _():
        dgain_ref[...] = jnp.zeros_like(dgain_ref)

    back, part = norm_back(h_ref[...], nt(dc_ref[...], query_ref[...]), gain_ref[...])
    dgain_ref[...] += part
    dh1 = dh_ref[...] + back
    dh1_ref[...] = dh1
    r_ref[...] = dh1.astype(BF16)
    do_ref[...] = nt(r_ref[...], out_ref[...]).astype(BF16)


def exit_kernel(dq_ref, query_ref, own_ref, *refs):
    peers = refs[:len(refs) - 8]
    keyvalue_ref, x_ref, gain_ref, dh_ref, dx_a_ref, dx_b_ref, dkv_ref, dgain_ref = refs[len(refs) - 8:]
    half = pl.num_programs(0) // 2

    @pl.when(pl.program_id(0) == 0)
    def _():
        dgain_ref[...] = jnp.zeros_like(dgain_ref)

    sides = [sum((ref[side].astype(F32) for ref in peers), own_ref[side].astype(F32)) for side in range(2)]
    dkv_ref[...] = lanes(sides[0], sides[1]).astype(BF16)
    dn = nt(dq_ref[...], query_ref[...]) + nt(dkv_ref[...], keyvalue_ref[...])
    back, part = norm_back(x_ref[...].astype(F32), dn, gain_ref[...])
    dgain_ref[...] += part
    dx = (dh_ref[...] + back).astype(BF16)

    @pl.when(pl.program_id(0) < half)
    def _():
        dx_a_ref[...] = dx

    @pl.when(pl.program_id(0) >= half)
    def _():
        dx_b_ref[...] = dx


def by_rows(kernel, name, flops, arrays, outs, width, dgain=False, hold=(), after=()):
    tokens = next(x.shape[0] for x, cut in arrays if cut)
    tile = min(256, tokens)
    blocks = pl.BlockSpec((tile, width), lambda i: (i, 0))

    def spec(x, cut):
        if x.ndim == 3:
            return pl.BlockSpec((x.shape[0], tile, x.shape[2]), lambda i: (0, i, 0))
        return blocks if cut else pl.BlockSpec(x.shape, lambda i: (0, 0))

    in_specs = [spec(x, cut) for x, cut in arrays]
    shapes, specs = [], []
    steps = tokens // tile
    for kind in outs:
        if kind == "halves":
            shapes += [jax.ShapeDtypeStruct((tokens // 2, width), BF16)] * 2
            specs += [pl.BlockSpec((tile, width), lambda i: (jnp.minimum(i, steps // 2 - 1), 0)),
                      pl.BlockSpec((tile, width), lambda i: (jnp.maximum(i - steps // 2, 0), 0))]
        else:
            shapes.append(jax.ShapeDtypeStruct((tokens, width), kind))
            specs.append(blocks)
    if dgain:
        shapes.append(jax.ShapeDtypeStruct((8, width), F32))
        specs.append(pl.BlockSpec((8, width), lambda i: (0, 0)))
    return call(kernel, tuple(x for x, _ in arrays), in_specs, shapes, specs, name, flops,
                grid=(tokens // tile,), hold=hold, after=after)


def feed_kernel(rest, h1_ref, co_ref, cross_ref, g_ref, gain_ref, gate_ref, up_ref, down_ref,
                out_a_ref, out_b_ref, n_ref, hidden_ref, dgu_ref, dh_ref, low_ref, dco_ref, dgain_ref,
                out_acc, dn_acc, h_acc):
    size = out_a_ref.shape[0]
    step, steps = pl.program_id(0), pl.num_programs(0)

    @pl.when(step == 0)
    def _():
        h = h1_ref[...] + nn(co_ref[...], cross_ref[...])
        h_acc[...] = h
        n_ref[...] = norm(h, gain_ref[...])
        out_acc[...] = jnp.zeros_like(out_acc)
        dn_acc[...] = jnp.zeros_like(dn_acc)

    def main(tile):
        n = n_ref[...]
        gate = nn(n, gate_ref[:, :tile])
        up = nn(n, up_ref[:, :tile])
        dhidden = nt(g_ref[...], down_ref[:tile, :])
        square = gate * gate
        bend = jnp.tanh(gate * (GELU_A + GELU_B * square))
        half = 0.5 + 0.5 * bend
        gelu = gate * half
        slope = half + gate * (0.5 - 0.5 * bend * bend) * (GELU_A + 3.0 * GELU_B * square)
        hidden = (gelu * up).astype(BF16)
        dgate = (dhidden * up * slope).astype(BF16)
        dup = (dhidden * gelu).astype(BF16)
        hidden_ref[:, :tile] = hidden
        dgu_ref[:, :tile] = dgate
        dgu_ref[:, tile:2 * tile] = dup
        out_acc[...] += nn(hidden, down_ref[:tile, :])
        dn_acc[...] += nt(dgate, gate_ref[:, :tile]) + nt(dup, up_ref[:, :tile])

    tile = gate_ref.shape[1]
    if rest == tile:
        main(tile)
    else:
        pl.when(step < steps - 1)(lambda: main(tile))
        pl.when(step == steps - 1)(lambda: main(rest))

    @pl.when(step == steps - 1)
    def _():
        h = h_acc[...]
        out = (h + out_acc[...]).astype(BF16)
        out_a_ref[...] = out[:size]
        out_b_ref[...] = out[size:]
        back, dgain_ref[...] = norm_back(h, dn_acc[...], gain_ref[...])
        dh = g_ref[...].astype(F32) + back
        dh_ref[...] = dh
        low_ref[...] = dh.astype(BF16)
        dco_ref[...] = nt(low_ref[...], cross_ref[...]).astype(BF16)


def feed_forward(h, co, cross_output, g, gain, feed_gate, feed_up, feed_down, hold=(), after=()):
    tokens, width = h.shape
    hidden = feed_gate.shape[1]
    tile = FEED
    rest = hidden - (hidden - 1) // tile * tile
    whole = pl.BlockSpec((tokens, width), lambda i: (0, 0), pipeline_mode=pl.Buffered(1))
    square = pl.BlockSpec((width, width), lambda i: (0, 0), pipeline_mode=pl.Buffered(1))
    row = pl.BlockSpec((1, width), lambda i: (0, 0))
    low, wide = jax.ShapeDtypeStruct(h.shape, BF16), jax.ShapeDtypeStruct(h.shape, F32)
    chunk = jax.ShapeDtypeStruct((tokens // 2, width), BF16)
    part = pl.BlockSpec(chunk.shape, lambda i: (0, 0), pipeline_mode=pl.Buffered(1))
    return call(
        functools.partial(feed_kernel, rest),
        (h, co, cross_output, g, gain, feed_gate, feed_up, feed_down),
        [
            whole, whole, square, whole, row,
            pl.BlockSpec((width, tile), lambda i: (0, i)),
            pl.BlockSpec((width, tile), lambda i: (0, i)),
            pl.BlockSpec((tile, width), lambda i: (i, 0)),
        ],
        [chunk, chunk, low, jax.ShapeDtypeStruct((tokens, hidden), BF16), jax.ShapeDtypeStruct((tokens, 2 * hidden), BF16),
         wide, low, low, jax.ShapeDtypeStruct((8, width), F32)],
        [part, part, whole, pl.BlockSpec((tokens, tile), lambda i: (0, i)), pl.BlockSpec((tokens, 2 * tile), lambda i: (0, i)),
         whole, whole, whole, pl.BlockSpec((8, width), lambda i: (0, 0))],
        "feed_forward", 45e9, grid=(pl.cdiv(hidden, tile),), hold=hold, after=after,
        scratch=[pltpu.VMEM((tokens, width), F32) for _ in range(3)],
    )


class Group:
    def __init__(self):
        self.S, self.R = lax.axis_size("seq"), lax.axis_size("row")
        self.s, self.r = lax.axis_index("seq"), lax.axis_index("row")
        self.core = self.r % 2
        self.chunks = self.S
        self.members = self.S // 2
        self.member = (self.s // 4) * 2 + self.core
        self.first_half = self.s < self.S // 2
        self.places = [(s, r) for s in range(self.S) for r in range(self.R)]

    def index(self, s, r):
        return s * self.R + r

    def send(self, x, target):
        pairs = [(self.index(s, r), self.index(*target(s, r))) for s, r in self.places]
        return lax.ppermute(x, ("seq", "row"), pairs)

    def route(self, way):
        S = self.S

        def target(s, r):
            second = (s >= S // 2) if way == 0 else (s < S // 2)
            row = 2 * (r % 2) + (1 if second else 0)
            member = min(s, S - 1 - s)
            return (row + 4 * (member // 2), r - r % 2 + member % 2)

        return [(self.index(s, r), self.index(*target(s, r))) for s, r in self.places]

    def part(self, x, way):
        return jnp.where(self.first_half == (way == 0), x[0], x[1])

    def go(self, x, way):
        return lax.ppermute(x, ("seq", "row"), self.route(way))

    def back(self, x, way):
        return lax.ppermute(x, ("seq", "row"), [(t, f) for f, t in self.route(way)])

    def two_rows(self, a, b):
        return jnp.where(self.first_half, a, b), jnp.where(self.first_half, b, a)

    def peer(self, x, distance):
        return self.send(x, lambda s, r: (s ^ (4 * (distance >> 1)), r ^ (distance & 1)))

    def peers(self, x):
        return [x] + [self.peer(x, p) for p in range(1, self.members)]

    def core_swap(self, x):
        return self.send(x, lambda s, r: (s, r ^ 1))

    def sum_axes(self):
        sizes = [("row", self.R), ("seq", self.S)]
        return [(axis, bit) for axis, size in sizes for bit in range(size.bit_length() - 1)]

    def names(self):
        top = self.S.bit_length() - 2
        row_bits = list(range(1, self.R.bit_length() - 1))
        return [("seq", k) for k in reversed(range(top))] + [("row", k) for k in reversed(row_bits)] + [("row", 0)]

    def bits(self):
        values = [((self.s if kind == "seq" else self.r) >> bit) & 1 for kind, bit in self.names()[:-1]]
        return jnp.stack(values + [self.s >> (self.S.bit_length() - 2)]).astype(jnp.int32)

    def swap(self, give, name):
        size = self.S if name[0] == "seq" else self.R
        return lax.ppermute(give, name[0], [(i, i ^ (1 << name[1])) for i in range(size)])

    def last_sends(self, straight, crossed):
        half = self.S // 2
        one = self.send(straight, lambda s, r: ((r % 2) * half + s % half, (r - r % 2) + s // half))
        two = self.send(crossed, lambda s, r: ((r % 2) * half + s % half, (r - r % 2) + 1 - s // half))
        return one, two


    def all_sends(self, pieces):
        half = self.S // 2
        sent = []
        for piece, (low, top) in zip(pieces, self.last_changes()):
            sent.append(self.send(piece, lambda s, r: (
                (r % 2) * half + (s % half ^ low), (r - r % 2) + (s // half ^ top))))
        return sent

    def last_changes(self):
        return [(low, top) for low in range(self.S // 2) for top in range(2)]


def grad_kernel(jobs, blocks, half_ref, *refs):
    inputs = sum(1 + job[-1] for job in jobs)
    out_ref, scratch = refs[inputs], refs[inputs + 1:]
    step = pl.program_id(0)
    place = 0

    def chunks_of(total, rows_in, paired):
        rows_out = -(-rows_in // 16) * 16
        for chunk in range(total.shape[1] // CHUNK):
            block = total[:, chunk * CHUNK:(chunk + 1) * CHUNK].reshape(blocks, rows_in, CHUNK)
            if paired:
                block = block.reshape(-1, 2, 2, 64 // rows_in, rows_in, CHUNK)
                block = jnp.swapaxes(block, 1, 2).reshape(blocks, rows_in, CHUNK)
            if rows_out > rows_in:
                block = jnp.concatenate([block, jnp.zeros((blocks, rows_out - rows_in, CHUNK), F32)], axis=1)
            yield slice(chunk * rows_out, (chunk + 1) * rows_out), block.astype(BF16)

    def direct(left_ref, right_refs, count, rows_in, paired):
        if len(right_refs) == 1:
            right = right_refs[0][:, :count * CHUNK]
        else:
            sides = [sum((ref[n].astype(F32) for ref in right_refs[1:]), right_refs[0][n].astype(F32)) for n in range(2)]
            right = lanes(*sides).astype(BF16)
        for at, block in chunks_of(tn(left_ref[...], right), rows_in, paired):
            out_ref[:, at, :] = block

    for start, full, rest, rows_in, paired, slabs, terms in jobs:
        left_ref, right_refs = refs[place], refs[place + 1:place + 1 + terms]
        right_ref = right_refs[0]
        place += 1 + terms
        if slabs:
            @pl.when(step == start)
            def _(left_ref=left_ref, right_ref=right_ref, rows_in=rows_in, paired=paired):
                for at, block in chunks_of(tn(left_ref[...], right_ref[...]), rows_in, paired):
                    scratch[0][:, at, :] = block

            deep = out_ref.shape[1]
            for slab in range(slabs):
                @pl.when(step == start + slab)
                def _(slab=slab):
                    out_ref[...] = scratch[0][:, slab * deep:(slab + 1) * deep, :]
            continue
        if full:
            run = functools.partial(direct, left_ref, right_refs, 2, rows_in, paired)
            pl.when((step >= start) & (step < start + full))(run)
        if rest:
            run = functools.partial(direct, left_ref, right_refs, 1, rows_in, paired)
            pl.when(step == start + full)(run)


def grad_part(half, pairs, blocks, rows_in, total, first=0, before=None, hold=(), after=(), holds=False):
    rows_out = -(-rows_in // 16) * 16
    jobs, inputs, in_specs, scratch = [], [half], [], []
    start = 0
    for left, right, *more in pairs:
        paired, own_rows = (more + [False, rows_in][len(more):])
        terms = list(right) if isinstance(right, (list, tuple)) else [right]
        full, rest = (1, 0) if len(terms) > 1 else divmod(right.shape[1] // CHUNK, 2)
        tokens, side = left.shape[0], left.shape[1] // 2
        slabs = 0
        steps = full + rest
        if own_rows != rows_in:
            deep = 2 * (-(-own_rows // 16) * 16)
            slabs = steps = deep // (2 * rows_out)
            scratch.append(pltpu.VMEM((blocks, deep, CHUNK), BF16))
            index = lambda i, h: (0, 0)
        else:
            index = lambda i, h, start=start, steps=steps: (0, jnp.clip(i - start, 0, steps - 1))
        jobs.append((start, full, rest, own_rows, bool(paired), slabs, len(terms)))
        inputs += [left] + terms
        in_specs.append(pl.BlockSpec((tokens, side), lambda i, h: (0, h[0])))
        if len(terms) > 1:
            in_specs += [pl.BlockSpec((2, tokens, CHUNK), lambda i, h: (0, 0, 0))] * len(terms)
        else:
            in_specs.append(pl.BlockSpec((tokens, 2 * CHUNK), index))
        start += steps
    kernel, inputs, in_specs, alias = with_before(
        functools.partial(grad_kernel, tuple(jobs), blocks), inputs, in_specs, before)
    (out,), kept = call(
        kernel, inputs, in_specs,
        [jax.ShapeDtypeStruct((blocks, total, CHUNK), BF16)],
        [pl.BlockSpec((blocks, 2 * rows_out, CHUNK), lambda i, h: (0, first + i, 0))],
        "weight_grads", 1e9, grid=(start,), prefetch=1, hold=hold, after=after, alias=alias, scratch=scratch,
    )
    return (out, kept) if holds else out


def stage_kernel(plan, bits_ref, *refs):
    count = max(max(terms) for _, terms, _ in plan) + 1
    for out, terms, at in plan:
        total = sum((refs[t][...].astype(F32) for t in terms[1:]), refs[terms[0]][...].astype(F32))
        refs[count + out][:, at, :] = total.astype(BF16)


def last_kernel(changes, counts, place_ref, *refs):
    inputs, outs = refs[:sum(counts)], refs[sum(counts):]
    for (low, top), out in zip(changes, outs):
        at = 2 * jnp.bitwise_xor(place_ref[0], low) + jnp.bitwise_xor(place_ref[1], top)
        start, first = 0, 0
        for count in counts:
            terms = inputs[start:start + count]
            block = sum((ref[pl.ds(at, 1)].astype(F32) for ref in terms[1:]), terms[0][pl.ds(at, 1)].astype(F32))
            out[first:first + block.shape[1], :] = block[0].astype(BF16)
            start, first = start + count, first + block.shape[1]


def last_stage(group, streams, after=(), hold=()):
    half = group.S // 2
    place = jnp.stack([group.s % half, group.s // half]).astype(jnp.int32)
    changes = group.last_changes()
    terms = [array for stream in streams for array, _, _ in stream.terms]
    shape = jax.ShapeDtypeStruct((sum(stream.rows_in for stream in streams), CHUNK), BF16)
    return call(
        functools.partial(last_kernel, changes, [len(stream.terms) for stream in streams]), (place, *terms),
        [pl.BlockSpec(x.shape, lambda p: (0, 0, 0)) for x in terms],
        [shape] * len(changes), [pl.BlockSpec(shape.shape, lambda p: (0, 0))] * len(changes),
        "last_stage", 1e9, prefetch=1, after=after, hold=hold)


class Stream:
    def __init__(self, terms, names, order, rows_in):
        self.terms, self.names, self.order, self.rows_in = terms, names, list(order), rows_in

    def got(self, array, names):
        self.terms.append((array, names, 0))


def stage(group, bits, streams, keep=True, join=False, after=(), hold=()):
    all_names = group.names()
    inputs, in_specs, shapes, out_specs, plan = [bits], [], [], [], []
    grid = 2 ** (len(streams[0].names) - 1)
    lead = 2 if streams[0].order[0] != all_names[-1] and grid > 1 else 1
    for number, stream in enumerate(streams):
        axis = stream.order[0]
        rest = [name for name in stream.names if name != axis]

        def spec(names, part, give, rest=rest, axis=axis, rows_in=stream.rows_in):
            def place(i, b):
                index = 0
                for name in names if lead == 1 else names[:-1]:
                    own = b[all_names.index(name)]
                    if name == axis:
                        value = 1 - own if give else own
                    elif name in rest:
                        value = (i * lead >> (len(rest) - 1 - rest.index(name))) & 1
                    else:
                        value = own
                    index = index * 2 + value
                return (index, part, 0)

            return pl.BlockSpec((lead, rows_in, CHUNK), place)

        sides = (True, False) if keep else (True,)
        for give in sides:
            terms = []
            for array, names, part in stream.terms:
                terms.append(len(inputs) - 1)
                inputs.append(array)
                in_specs.append(spec(names, part, give))
            count = stream.rows_in
            if join:
                plan.append((0 if give else 1, tuple(terms), slice(number * count, (number + 1) * count)))
            else:
                plan.append((len(shapes), tuple(terms), slice(0, count)))
            if not join or number == 0:
                full = count * (len(streams) if join else 1)
                shapes.append(jax.ShapeDtypeStruct((grid, full, CHUNK), BF16))
                out_specs.append(pl.BlockSpec((lead, full, CHUNK), lambda i, b: (i, 0, 0)))
    return call(functools.partial(stage_kernel, tuple(plan)), tuple(inputs), in_specs, shapes, out_specs, "stage", 1e9,
                grid=(grid // lead,), prefetch=1, after=after, hold=hold)


class Bundle:
    def __init__(self, group, bits):
        self.group, self.bits, self.ends = group, bits, []

    def swap(self, theirs):
        self.other = self.group.core_swap(theirs)

    def begin(self, mine, after=(), hold=()):
        names = self.group.names()
        rows_axes = [name for name in names if name[0] == "row" and name[1]]
        seq_axes = [name for name in names if name[0] == "seq"][::-1]
        half = mine.shape[1] // 2
        self.streams = [
            Stream([(mine, names, n), (self.other, names, n)], names, (rows_axes[::-1], rows_axes)[n] + seq_axes + [("row", 0)], half)
            for n in range(2)
        ]
        self.gives, kept = stage(self.group, self.bits, self.streams, keep=False, after=after, hold=hold)
        self.send()
        return kept

    def send(self):
        self.fly = [self.group.swap(give, s.order[0]) for give, s in zip(self.gives, self.streams)]

    def step(self, after=(), hold=(), direct=False):
        if self.ends:
            return list(hold)
        for stream, got in zip(self.streams, self.fly):
            axis = stream.order.pop(0)
            stream.names = [name for name in stream.names if name != axis]
            stream.got(got, list(stream.names))
        if direct:
            self.gives, kept = last_stage(self.group, self.streams, after=after, hold=hold)
            self.ends = self.group.all_sends(self.gives)
            return kept
        one = self.streams[0]
        join = len(self.streams) == 2 and one.names == self.streams[1].names and one.order == self.streams[1].order
        outs, kept = stage(self.group, self.bits, self.streams, join=join, after=after, hold=hold)
        axis = one.order[0]
        if join:
            self.streams = [Stream([], list(one.names), one.order, 2 * one.rows_in)]
        if axis == ("row", 0):
            crossed, straight = outs
            self.gives = [crossed]
            self.ends = list(self.group.last_sends(straight, crossed))
            return kept
        self.gives = []
        for n, stream in enumerate(self.streams):
            self.gives.append(outs[2 * n])
            rest = [name for name in stream.names if name != stream.order[0]]
            stream.terms = [(outs[2 * n + 1], rest, 0)]
        self.send()
        return kept

    def finish(self):
        while not self.ends:
            self.step()

    def result(self):
        return sum((x.astype(F32) for x in self.ends[1:]), self.ends[0].astype(F32)).reshape(-1, CHUNK)


def by_pairs(weight, axis):
    shape = weight.shape
    split = shape[:axis] + (shape[axis] // 256, 2, 2, 64) + shape[axis + 1:]
    return jnp.swapaxes(weight.reshape(split), axis + 1, axis + 2).reshape(shape)


def bias_rows(bias_table, sub):
    table = by_heads((bias_table - bias_table[BUCKETS - 1:]).T)
    levels = np.array([bucket_level(d) for d in range(2 * NEAR)])
    values = jnp.dot(table, jnp.asarray(np.eye(BUCKETS, dtype=np.float32)[levels].T), precision=HIGHEST)
    near = values[:, :sub] if sub <= 2 * NEAR else jnp.pad(values, ((0, 0), (0, sub - 2 * NEAR)))
    near = jnp.concatenate([near, jnp.full((HEADS, sub), MASK, F32)], axis=1)
    corner = jnp.concatenate([values[:, NEAR:], jnp.zeros((HEADS, 1), F32), values[:, 1:NEAR]], axis=1)
    return [jnp.broadcast_to(a[:, None], (HEADS, 8, a.shape[1])) for a in (near, corner)]


def by_heads(x):
    return jnp.swapaxes(x.reshape((4, 2, 2) + x.shape[1:]), 1, 2).reshape(x.shape)


def bias_table_sums(near, corner):
    def fold(wide, distances):
        matrix = np.zeros((8, wide, BUCKETS), np.float32)
        for row in range(8):
            for lane in range(wide):
                distance = distances((lane - row) % wide)
                if distance is not None:
                    matrix[row, lane, bucket_level(distance)] = 1.0
        return jnp.asarray(matrix.reshape(8 * wide, BUCKETS))

    sub = near.shape[2] // 2
    first = fold(2 * sub, lambda d: d if d < sub else None)
    second = fold(2 * NEAR, lambda d: NEAR + d if d < NEAR else (d - NEAR if d > NEAR else None))
    total = jnp.dot(near.reshape(HEADS, -1), first, precision=HIGHEST)
    total = total + jnp.dot(corner.reshape(HEADS, -1), second, precision=HIGHEST)
    rest = -jnp.sum(total[:, :BUCKETS - 1], axis=1, keepdims=True)
    return by_heads(jnp.concatenate([total[:, :BUCKETS - 1], rest], axis=1)).T


def on_device(tokens, segment_ids, memory, cotangent, gain_attend, gain_cross, gain_feed, bias_table,
              self_query, self_keyvalue, self_output, cross_query, cross_keyvalue, cross_output,
              feed_gate, feed_up, feed_down):
    group = Group()
    size, width = tokens.shape[1:]
    span = memory.shape[1]
    hidden_width = feed_gate.shape[1]
    chunks = group.chunks
    sub = min(256, size)
    bits = group.bits()
    core = group.core.astype(jnp.int32)[None]
    devices = group.S * group.R
    blocks = devices // 2

    def token_part(way):
        numbers = group.part(segment_ids, way).astype(BF16)
        numbers = jnp.pad(numbers[None], ((0, PAD - 1), (0, width - size)))
        return jnp.concatenate([group.part(tokens, way), numbers], axis=0)

    way_a = group.go(token_part(0), 0)
    way_b = group.go(token_part(1), 1)

    memory_rows = memory.reshape(-1, width)
    pairs = nn(memory_rows, cross_keyvalue).astype(BF16).reshape(2, span, width)
    own_query, own_output = by_pairs(self_query, 1), by_pairs(self_output, 0)
    other_query, other_output = by_pairs(cross_query, 1), by_pairs(cross_output, 0)
    near, near_back, corner, corner_back = bias_tiles(*bias_rows(bias_table, sub), sub)
    second = [jnp.concatenate([group.part(cotangent, way), group.part(pairs, way)], axis=0) for way in range(2)]

    (x, n1, message), (second_a,) = entry(
        way_a, way_b, gain_attend[None], self_keyvalue, hold=[second[0]],
        after=[own_query, own_output, other_query, other_output, near, second[1]])
    messages = group.peers(message)
    second_a = group.go(second_a, 0)
    second_b = group.go(second[1], 1)
    (q,), _ = by_rows(query_kernel, "query", 2e9, [(n1, True), (own_query, False)], [BF16], width)
    (kv, key_marks, query_marks, meta), _ = gather(
        (2 * group.member + group.s % 2).astype(jnp.int32)[None], messages, after=[q])
    (o, lse), _ = self_forward(meta, q, kv, query_marks, key_marks, near, corner, chunks, 0, 1, None)
    memory_own, g = unpack(second_a, second_b, size, [o])
    memories = group.peers(memory_own)
    (h1, n2, c), _ = by_rows(
        middle_kernel, "middle", 5e9,
        [(x, True), (o, True), (own_output, False), (gain_cross[None], False), (other_query, False)],
        [F32, BF16, BF16], width, after=[memory_own])
    (co, cross_lse), _ = cross_forward(c, memories)
    (out_a, out_b, n3, hidden, dgu, dh2, r2, dco, dgain_feed), _ = feed_forward(
        h1, co, other_output, g, gain_feed[None], feed_gate, feed_up, feed_down)

    feed_rows = hidden.shape[1] // devices
    if feed_rows % 8:
        padded = -(-feed_rows // 16) * 16
        hidden = jnp.pad(hidden.reshape(-1, devices, feed_rows), ((0, 0), (0, 0), (0, padded - feed_rows)))
        hidden = hidden.reshape(-1, devices * padded)
    down_rows = hidden.shape[1] // devices
    down_out = -(-down_rows // 16) * 16
    square_rows = width // devices
    square_out = -(-square_rows // 16) * 16
    down_total = down_out * (width // CHUNK)
    feed_total = -(-(down_total + square_out * (dgu.shape[1] // CHUNK)) // 32) * 32

    def feed_half(which, after=(), hold=()):
        return grad_part(which, [(hidden, g, False, down_rows), (n3, dgu)], blocks, square_rows, feed_total,
                         after=after, hold=hold, holds=True)

    theirs, (out_b,) = feed_half(1 - core, after=[out_a], hold=[out_b])
    out_a = group.back(out_a, 0)
    feed = Bundle(group, bits)
    feed.swap(theirs)
    mine, (out_b,) = feed_half(core, after=[theirs], hold=[out_b])
    feed.begin(mine)
    out_b = group.back(out_b, 1)

    (dc, dm, *dm_peers), _ = cross_backward(c, dco, co, cross_lse, memories, after=feed.gives)
    (dh1, r1, do, dgain_cross), _ = by_rows(
        back_middle_kernel, "back_middle", 5e9,
        [(dc, True), (other_query, False), (h1, True), (gain_cross[None], False), (dh2, True), (own_output, False)],
        [F32, BF16, BF16], width, dgain=True)
    cross_pairs = [(co, r2, True), (n2, dc), (o, r1, True)]
    cross_total = 3 * square_out * (width // CHUNK)
    theirs, dm_peers = grad_part(
        1 - core, cross_pairs, blocks, square_rows, cross_total, hold=dm_peers, holds=True)
    theirs, out_a, out_b = feed.step(hold=[theirs, out_a, out_b])
    cross = Bundle(group, bits)
    cross.swap(theirs)
    dm_peers = [group.peer(term, p + 1) for p, term in enumerate(dm_peers)]
    mine, (dm,) = grad_part(
        core, cross_pairs, blocks, square_rows, cross_total, after=[theirs] + feed.gives, hold=[dm], holds=True)
    dm_a, dm_b, _ = add_memory([dm] + dm_peers)

    def backward(part, before, after, hold=()):
        return self_backward(meta, q, do, o, lse, kv, query_marks, key_marks, near_back, corner_back, chunks,
                             part, 4, before, after=after, hold=hold)

    back, (mine,) = backward(0, None, [dm_a, dm_b, cross.other], [mine])
    dm_a, dm_b = group.back(dm_a, 0), group.back(dm_b, 1)
    dm_a, dm_b = feed.step(after=[back[0], mine], hold=[dm_a, dm_b])
    cross.begin(mine, after=feed.gives)
    back, _ = backward(1, back, feed.gives + cross.gives)
    feed.step(after=[back[0]])
    cross.step(after=[back[0]] + feed.gives)
    back, _ = backward(2, back, feed.gives + cross.gives)
    feed.finish()
    cross.step(after=[back[0]] + list(feed.ends))
    back, _ = backward(3, back, cross.gives)
    dq, dkv_own, dkv_peers, near_sum, corner_sum = back
    dm_b, dkv_peers = cross.step(after=[dq], hold=[dm_b, dkv_peers])
    cross.finish()
    dkv_peers = [group.peer(dkv_peers[p - 1], p) for p in range(1, group.members)]
    dm = rows(*group.two_rows(dm_a, dm_b))
    own_total = 3 * square_out * (width // CHUNK)
    step = square_out * (width // CHUNK)
    theirs = grad_part(1 - core, [(n1, dq), (memory_rows, dm)], blocks, square_rows, own_total, after=cross.gives)
    dkv_terms = [dkv_own] + dkv_peers
    theirs = grad_part(1 - core, [(n1, dkv_terms)], blocks, square_rows, own_total, step // square_out, [theirs])
    (token_a, token_b, dkv, dgain_attend), (theirs, *cross.ends) = by_rows(
        exit_kernel, "exit", 5e9,
        [(dq, True), (own_query, False), (dkv_own, True)] + [(y, True) for y in dkv_peers]
        + [(self_keyvalue, False), (x, True), (gain_attend[None], False), (dh1, True)],
        ["halves", BF16], width, dgain=True, hold=[theirs] + list(cross.ends))
    own = Bundle(group, bits)
    own.swap(theirs)
    token_source, token_a = token_a, group.back(token_a, 0)
    mine, (out_a, out_b, token_b, *ends) = grad_part(
        core, [(n1, dq), (memory_rows, dm), (n1, dkv)], blocks, square_rows, own_total,
        after=[token_source], hold=[out_a, out_b, token_b, near_sum, corner_sum, dgain_attend, dgain_cross, dgain_feed, dm], holds=True)
    near_sum, corner_sum, dgain_attend, dgain_cross, dgain_feed, dm_late = ends
    dbias = bias_table_sums(near_sum, corner_sum)
    small = jnp.stack([jnp.sum(dgain_attend, axis=0), jnp.sum(dgain_cross, axis=0), jnp.sum(dgain_feed, axis=0),
                       jnp.pad(dbias.reshape(-1), (0, width - dbias.size))])
    sum_axes = group.sum_axes()

    def small_step(x):
        return x + group.swap(x, sum_axes.pop(0))

    small = small_step(small)
    memory_grad = nt(dm_late, cross_keyvalue).astype(BF16).reshape(memory.shape)
    def squares(bundle, start, columns):
        rest = bundle[start:start + square_out * (columns // CHUNK)].reshape(columns // CHUNK, square_out, CHUNK)
        return jnp.swapaxes(rest[:, :square_rows], 0, 1).reshape(square_rows, columns)

    token_b, token_a, small, *ends = own.begin(
        mine, after=[memory_grad], hold=[token_b, token_a, small, out_a, out_b] + list(feed.ends) + list(cross.ends))
    out_a, out_b, *ends = ends
    count = len(feed.ends)
    feed.ends, cross.ends = ends[:count], ends[count:]
    token_b = group.back(token_b, 1)
    small = small_step(small)
    feed_sum = feed.result()
    grad_dgu = squares(feed_sum, down_total, dgu.shape[1])
    whole = hidden_width // FEED * FEED
    grad_dgu, grad_rest = grad_dgu[:, :2 * whole].reshape(square_rows, -1, 2, FEED), grad_dgu[:, 2 * whole:]
    grad_rest = grad_rest.reshape(square_rows, 2, hidden_width - whole)
    grad_gate, grad_up = [
        jnp.concatenate([grad_dgu[:, :, n].reshape(square_rows, -1), grad_rest[:, n]], axis=1) for n in range(2)]
    grad_down = feed_sum[:down_total].reshape(width // CHUNK, down_out, CHUNK)[:, :feed_rows]
    grad_down = jnp.swapaxes(grad_down, 0, 1).reshape(feed_rows, width)
    token_a, token_b, small, out_a, out_b, *cross.ends = own.step(
        hold=[token_a, token_b, small, out_a, out_b] + list(cross.ends), after=[grad_gate, grad_up, grad_down])
    small = small_step(small)
    tokens_grad = jnp.stack(group.two_rows(token_a, token_b))
    cross_sum = cross.result()
    grad_cross = [squares(cross_sum, n * step, width) for n in range(3)]
    grad_cross[1] = by_pairs(grad_cross[1], 1)
    small, out_a, out_b = own.step(hold=[small, out_a, out_b], after=[tokens_grad] + grad_cross, direct=True)
    layer_output = jnp.stack(group.two_rows(out_a, out_b))
    while sum_axes:
        small = small_step(small)
    own_sum = own.result()
    grad_own = [squares(own_sum, n * step, width) for n in (0, 2, 1)]

    return (
        layer_output,
        tokens_grad,
        memory_grad,
        by_pairs(grad_own[0], 1),
        grad_own[1],
        grad_cross[2],
        grad_cross[1],
        grad_own[2],
        grad_cross[0],
        grad_gate,
        grad_up,
        grad_down,
        small[0],
        small[1],
        small[2],
        small[3, :dbias.size].reshape(dbias.shape),
    )


def solution(mesh):
    data, whole, grads = P("row", "seq", None), P(), P(("seq", "row"), None)
    in_specs = (data, P("row", "seq"), data, data) + (whole,) * 13
    out_specs = (data,) * 3 + (grads,) * 9 + (whole,) * 4
    return jax.shard_map(on_device, mesh=mesh, in_specs=in_specs, out_specs=out_specs, check_vma=False)
```
